32 devices in a mesh: groups: 2 (over x), cell: 16 (over z, y, core), gene: 1.
Axes of the slice: x: 2, y: 2, z: 4, core: 2. Of those that a mesh axis runs over, the one named last changes fastest.
Arguments:
- expression: bfloat16 [2048, 30720], P(('groups', 'cell'), 'gene'), parts along dimension 0, may hold values from -6 to 6
- start_basis: bfloat16 [61440, 64], P(('groups', 'gene', 'cell')), parts along dimension 0, may hold values from -0.03125 to 0.03125
Outputs:
- basis_out: float32 [61440, 64], P(('groups', 'gene', 'cell')), parts along dimension 0
The draws below stay inside these ranges and needn't reach their ends.
There are 2 independent parts, one for each index of `groups`. The reference program is written for one: setup_inputs(seed, part) draws one part's arguments, and reference() takes and returns one part's arrays. A program takes and returns all parts, laid end to end along the dimension named above; each array names one. Nothing has to cross between parts.
All inputs are finite; a program needn't handle non-finite values.
Results may differ from the reference program's by a relative error of at most 0.006.
Values may be sent and summed in bfloat16 or wider, within the bound.
No kernel may reach another device: no remote copies, remote signals or barrier semaphores. Data moves between devices by JAX's collectives and lax.ppermute only.
A program may use at most 64 MiB of HBM per device.

```python
import math
import jax
import jax.numpy as jnp
from jax import lax

GENES = 30720
RANK = 64
ITERS = 2
CELLS = 1024


def spiked(entries, stream_key, source, target, blocks, factor):
    owner, partner = [(jnp.arange(entries.shape[dim]) // (entries.shape[dim] // blocks)).reshape([-1 if axis == dim else 1 for axis in range(entries.ndim)]) for dim in (source, target)]
    chosen = jax.random.permutation(stream_key, blocks)[partner]
    strong = (owner == chosen) | (owner == (partner + blocks // 2) % blocks)
    return jnp.where(strong, factor * entries, entries)


def levels(key, dims, shards, least, largest):
    def one(position, shards_of):
        heights = jax.random.uniform(jax.random.fold_in(jax.random.fold_in(key, 6), position), (shards_of,), jnp.float32, least / len(shards), largest / len(shards))
        return jnp.repeat(jnp.exp(heights), dims[position] // shards_of).reshape((-1,) + (1,) * (len(dims) - position - 1))

    factor_of = one(*shards[0])
    for cut in shards[1:]:
        factor_of = factor_of * one(*cut)
    return factor_of


def centred(own_key, extent, scale, bound, split=(), kind=jnp.bfloat16):
    drawn = jax.random.normal(own_key, extent, jnp.float32) * scale
    if len(split) > 0:
        drawn = levels(own_key, extent, split, -0.22, 0.18) * drawn
    return jnp.clip(drawn, min=-bound, max=bound).astype(kind)


def bell_draw_with(key, dims, spread, most, cuts, heavy, kind=jnp.bfloat16):
    entries = spread * jax.random.normal(key, dims, jnp.float32)
    if cuts:
        entries = entries * levels(key, dims, cuts, -0.22, 0.18)
    return jnp.clip(spiked(entries, jax.random.fold_in(key, 3), *heavy), -most, most).astype(kind)


def setup_inputs(seed: int = 0, part: int = 0) -> dict:
    key_of = jax.random.split(jax.random.key(seed), 3)
    own_keys = jax.random.split(jax.random.fold_in(key_of[2], part), 3)
    expression = bell_draw_with(own_keys[0], (CELLS, GENES), 1.0, 6.0, ((0, 16),), (0, 1, 16, 2.0))
    start_basis = centred(own_keys[1], (GENES, RANK), GENES ** -0.5, 0.03125, ((0, 16),))
    return dict(expression=expression, start_basis=start_basis)


def reference(expression, start_basis):
    basis = start_basis
    ortho = jnp.zeros((GENES, RANK), jnp.float32)
    for step in range(ITERS):
        image = jnp.dot(expression.astype(jnp.float32), basis.astype(jnp.float32), preferred_element_type=jnp.float32).astype(jnp.bfloat16)
        loading = lax.dot_general(expression.astype(jnp.float32), image.astype(jnp.float32), (((0,), (0,)), ((), ())), preferred_element_type=jnp.float32)
        gram = lax.dot_general(loading.astype(jnp.float32), loading.astype(jnp.float32), (((0,), (0,)), ((), ())), precision=lax.Precision.HIGHEST, preferred_element_type=jnp.float32)
        lower = jnp.linalg.cholesky(gram)
        ortho = jax.scipy.linalg.solve_triangular(lower, loading.T, lower=True).T
        basis = ortho.astype(jnp.bfloat16)
    return ortho * math.sqrt(GENES)
```

```python
import functools
import math

import jax
import jax.numpy as jnp
from jax import lax
from jax.experimental import pallas as pl
from jax.experimental.pallas import tpu as pltpu
from jax.sharding import PartitionSpec as P

GENES = 30720
ITERS = 2
PARTS = 2
GROUP = 8
BIG = pltpu.CompilerParams(vmem_limit_bytes=32 * 2**20)
VMEM = pl.BlockSpec(memory_space=pltpu.VMEM)
HIGHEST = lax.Precision.HIGHEST
f32, bf16 = jnp.float32, jnp.bfloat16


def nn(a, b, precision=None):
    return lax.dot_general(a, b, (((1,), (0,)), ((), ())), precision=precision, preferred_element_type=f32)


def nt(a, b, precision=None):
    return lax.dot_general(a, b, (((1,), (1,)), ((), ())), precision=precision, preferred_element_type=f32)


def struct(shape, dtype):
    return jax.ShapeDtypeStruct(shape, dtype)


def cost(flops, bytes_accessed):
    return pl.CostEstimate(flops=flops, bytes_accessed=bytes_accessed, transcendentals=0)


def pack_kernel(width, ids, matrix, *refs):
    outs, sem = refs[:-1], refs[-1]
    copies = []
    for k, out in enumerate(outs):
        for j in range(2):
            start = pl.multiple_of(ids[2 * k + j] * width, 128)
            copies.append(pltpu.make_async_copy(
                matrix.at[:, pl.ds(start, width)], out.at[:, pl.ds(j * width, width)], sem.at[2 * k + j]))
    for copy in copies:
        copy.start()
    for copy in copies:
        copy.wait()


def pack(matrix, ids, width):
    rows, count = matrix.shape[0], ids.shape[0] // 2
    anywhere = pl.BlockSpec(memory_space=pl.ANY)
    return pl.pallas_call(
        functools.partial(pack_kernel, width),
        in_specs=[pl.BlockSpec(memory_space=pltpu.SMEM), anywhere],
        out_specs=[anywhere] * count,
        out_shape=[struct((rows, 2 * width), matrix.dtype)] * count,
        scratch_shapes=[pltpu.SemaphoreType.DMA((2 * count,))],
        cost_estimate=cost(0, 8 * rows * count * width),
    )(ids, matrix)


def slot_specs(blocks, rows, width):
    specs = []
    for j in blocks:
        specs.append(pl.BlockSpec((rows, width), functools.partial(lambda j, s, ids: (0, ids[j]), j)))
        specs += [pl.BlockSpec((rows, width), functools.partial(lambda j, s, ids: (0, j), j))] * (GROUP - 1)
    return specs


def whole_spec(shape):
    return pl.BlockSpec(shape, lambda s, ids: (0,) * len(shape))


def prefetched(kernel, ids, args, in_specs, outs, estimate):
    return pl.pallas_call(
        kernel,
        grid_spec=pltpu.PrefetchScalarGridSpec(
            num_scalar_prefetch=1, grid=(1,), in_specs=in_specs,
            out_specs=[whole_spec(x.shape) for x in outs],
        ),
        out_shape=outs,
        compiler_params=BIG,
        cost_estimate=estimate,
    )(ids, *args)


def scores_kernel(counts, carried, ids, *refs):
    refs = list(refs)
    slots = [[refs.pop(0) for _ in range(GROUP)] for _ in counts]
    pieces = [[refs.pop(0) for _ in range(count)] for count in counts]
    carry = [refs.pop(0) for _ in range(2)] if carried else None
    for odd in range(2):
        total = carry[odd][...] if carried else 0.0
        for block, parts in zip(slots, pieces):
            basis = jnp.concatenate([ref[...] for ref in parts], axis=0) if len(parts) > 1 else parts[0][...]
            total = total + jnp.concatenate([nt(basis, ref[...]) for ref in block[odd::2]], axis=1)
        refs[odd][...] = total


def scores(slots, ids, blocks, pieces, carry):
    rows, width = slots[0].shape[0], pieces[0][0].shape[1]
    rank = sum(x.shape[0] for x in pieces[0])
    outs = [struct((rank, rows * GROUP // 2), f32)] * 2
    args = list(slots) * len(blocks) + [x for parts in pieces for x in parts] + list(carry or ())
    specs = slot_specs(blocks, rows, width) + [whole_spec(x.shape) for x in args[len(blocks) * GROUP:]]
    estimate = cost(2 * rank * rows * width * GROUP * len(blocks), 2 * rows * width * GROUP * len(blocks))
    kernel = functools.partial(scores_kernel, [len(parts) for parts in pieces], carry is not None)
    return prefetched(kernel, ids, args, specs, outs, estimate)


def image_kernel(normalised, *refs):
    value, mates = refs[0][...], [ref[...] for ref in refs[1:4]]
    size = value.shape[1] // (GROUP // 2)

    def turned(x, mask):
        return jnp.concatenate([x[:, (j ^ mask) * size:((j ^ mask) + 1) * size] for j in range(GROUP // 2)], axis=1)

    value = (value + turned(mates[0], 1)) + (turned(mates[1], 2) + turned(mates[2], 3))
    if normalised:
        value = nn(refs[4][...], value, HIGHEST)
    refs[-1][...] = value.astype(bf16)


def image_of(value, mates, inverse):
    args = [value, *mates] + ([] if inverse is None else [inverse])
    return pl.pallas_call(
        functools.partial(image_kernel, inverse is not None),
        in_specs=[VMEM] * len(args), out_specs=VMEM, out_shape=struct(value.shape, bf16),
        compiler_params=BIG, cost_estimate=cost(12 * value.size * value.shape[0], 16 * value.size),
    )(*args)


def terms_kernel(ids, *refs):
    slots, images, outs = refs[:GROUP], refs[GROUP:GROUP + 2], refs[GROUP + 2:]
    total = 0.0
    for odd in range(2):
        stacked = jnp.concatenate([ref[...] for ref in slots[odd::2]], axis=0)
        total = total + nn(images[odd][...], stacked)
    step = total.shape[0] // len(outs)
    for part, out in enumerate(outs):
        out[...] = total[part * step:(part + 1) * step].astype(out.dtype)


def terms(slots, ids, block, images, width, parts, dtype):
    rows, rank = slots[0].shape[0], images[0].shape[0]
    args = list(slots) + list(images)
    specs = slot_specs([block], rows, width) + [whole_spec(x.shape) for x in images]
    outs = [struct((rank // parts, width), dtype)] * parts
    estimate = cost(2 * rank * rows * width * GROUP, 2 * rows * width * GROUP)
    return prefetched(terms_kernel, ids, args, specs, outs, estimate)


def fold_kernel(count, with_gram, received, own, *refs):
    before, outs = refs[:count], refs[count:]
    value = own[...] + received[...].astype(f32)
    outs[0][...] = value.astype(outs[0].dtype)
    if not with_gram:
        outs[1][...] = value
        return
    if count:
        value = jnp.concatenate([ref[...] for ref in before] + [value], axis=0)
    outs[1][...] = nt(value, value, HIGHEST)


def fold(received, own, before, dtype, gram):
    rank = own.shape[0] * (1 + len(before))
    second = struct((rank, rank), f32) if gram else struct(own.shape, f32)
    return pl.pallas_call(
        functools.partial(fold_kernel, len(before), gram),
        in_specs=[VMEM] * (2 + len(before)), out_specs=[VMEM] * 2,
        out_shape=[struct(own.shape, dtype), second],
        compiler_params=BIG, cost_estimate=cost(12 * rank * own.size, 12 * own.size),
    )(received, own, *before)


def inverse_factor(gram):
    size = gram.shape[0]
    row = lax.broadcasted_iota(jnp.int32, (size, size), 0)
    column = lax.broadcasted_iota(jnp.int32, (size, size), 1)
    both = jnp.concatenate([gram, jnp.where(row == column, 1.0, 0.0).astype(f32)], axis=1)
    blocks = [both[8 * b:8 * b + 8] for b in range(size // 8)]
    inner = lax.broadcasted_iota(jnp.int32, (8, 2 * size), 0)
    done = []
    for j in range(size):
        b, i = divmod(j, 8)
        root = lax.rsqrt(blocks[b][i:i + 1, j:j + 1])
        pivot = blocks[b][i:i + 1] * root
        done.append(pivot)
        for k in range(b, size // 8):
            factor = jnp.broadcast_to(blocks[k][:, j:j + 1] * root, (8, 2 * size))
            if k == b:
                factor = jnp.where(inner > i, factor, 0.0)
            blocks[k] = blocks[k] - factor * pivot
    return jnp.concatenate(done, axis=0)[:, size:]


def factor_kernel(gram, out):
    out[...] = inverse_factor(gram[...])


def factor_call(gram):
    return pl.pallas_call(
        factor_kernel, in_specs=[VMEM], out_specs=VMEM, out_shape=struct(gram.shape, f32),
        cost_estimate=pl.CostEstimate(flops=20_000_000, bytes_accessed=32768, transcendentals=64),
    )(gram)


def output_kernel(scale, gram, loading, out):
    out[...] = nn(inverse_factor(gram[...]), loading[...], HIGHEST) * scale


def output_call(gram, loading):
    return pl.pallas_call(
        functools.partial(output_kernel, math.sqrt(GENES)),
        in_specs=[VMEM, VMEM], out_specs=VMEM, out_shape=struct(loading.shape, f32),
        compiler_params=pltpu.CompilerParams(vmem_limit_bytes=24 * 2**20),
    )(gram, loading)


def mate(value, cells, mask):
    return lax.ppermute(value, "cell", [(i, i ^ mask) for i in range(cells)])


def total_over_cells(value, cells):
    for low in range(0, cells.bit_length() - 1, 2):
        one, two = 1 << low, 2 << low
        value = (value + mate(value, cells, one)) + (mate(value, cells, two) + mate(value, cells, one | two))
    return value


def square_program(cells, expression, start_basis):
    width, rank = start_basis.shape
    index = lax.axis_index("cell").astype(jnp.int32)
    masks = jnp.arange(1, GROUP, dtype=jnp.int32)
    wanted = index ^ masks
    packs = pack(expression, jnp.stack([wanted, wanted ^ GROUP], axis=1).reshape(-1), width)
    ids = jnp.stack([index, index ^ GROUP])
    basis = start_basis.T
    basis_mate = [mate(basis, cells, GROUP)]
    received = {k: mate(packs[k - 1], cells, k) for k in (2, 4, 3, 5, 6, 7, 1)}
    slots = [expression] + [received[k] for k in range(1, GROUP)]
    step = rank // PARTS

    def summed_image(even, odd, inverse):
        even = even + mate(odd, cells, 1)
        image = image_of(even, [mate(even, cells, mask) for mask in (2, 4, 6)], inverse)
        return image, mate(image, cells, 1)

    even, odd = scores(slots, ids, (0, 1), [[basis], basis_mate], None)
    images = summed_image(even, odd, None)

    for iteration in range(1, ITERS):
        sent = terms(slots, ids, 1, images, width, PARTS, bf16)
        arrived = [mate(x, cells, GROUP) for x in sent]
        own = terms(slots, ids, 0, images, width, PARTS, f32)
        rounded, exact = [], []
        for part in range(PARTS - 1):
            rows, kept = fold(arrived[part], own[part], [], bf16, False)
            rounded.append(rows)
            exact.append(kept)
        rows, gram = fold(arrived[-1], own[-1], exact, bf16, True)
        rounded.append(rows)
        others = [mate(x, cells, GROUP) for x in rounded]
        inverse = factor_call(total_over_cells(gram, cells))
        carry = scores(slots, ids, (0,), [rounded], None)
        even, odd = scores(slots, ids, (1,), [others], carry)
        images = summed_image(even, odd, inverse)

    (sent,) = terms(slots, ids, 1, images, width, 1, bf16)
    arrived = mate(sent, cells, GROUP)
    (own,) = terms(slots, ids, 0, images, width, 1, f32)
    loading, gram = fold(arrived, own, [], f32, True)
    return output_call(total_over_cells(gram, cells), loading).T


def plain_program(expression, start_basis):
    basis = start_basis
    for _ in range(ITERS):
        whole = lax.all_gather(basis, "cell", axis=0, tiled=True)
        partial = jnp.dot(expression, whole, preferred_element_type=f32)
        image = lax.psum(partial, "gene").astype(bf16)
        partial = lax.dot_general(expression, image, (((0,), (0,)), ((), ())), preferred_element_type=f32)
        loading = lax.psum_scatter(partial, "cell", scatter_dimension=0, tiled=True)
        gram = lax.dot_general(loading, loading, (((0,), (0,)), ((), ())), precision=HIGHEST, preferred_element_type=f32)
        lower = jnp.linalg.cholesky(lax.psum(gram, ("cell", "gene")))
        ortho = jax.scipy.linalg.solve_triangular(lower, loading.T, lower=True).T
        basis = ortho.astype(bf16)
    return ortho * math.sqrt(GENES)


def solution(mesh):
    cells, genes = mesh.shape["cell"], mesh.shape["gene"]

    def on_device(expression, start_basis):
        width, rank = start_basis.shape
        fits = genes == 1 and cells == 2 * GROUP and width % 128 == 0 and rank == 64
        if fits and expression.shape[0] % 16 == 0:
            return square_program(cells, expression, start_basis)
        return plain_program(expression, start_basis)

    return jax.shard_map(
        on_device,
        mesh=mesh,
        in_specs=(P(("groups", "cell"), "gene"), P(("groups", "gene", "cell"), None)),
        out_specs=P(("groups", "gene", "cell"), None),
        check_vma=False,
    )
```

```python
import functools
import math

import jax
import jax.numpy as jnp
from jax import lax
from jax.experimental import pallas as pl
from jax.experimental.pallas import tpu as pltpu
from jax.sharding import PartitionSpec as P

GENES = 30720
ITERS = 2
PARTS = 2
GROUP = 8
BIG = pltpu.CompilerParams(vmem_limit_bytes=16 * 2**20)
SMALL = pltpu.CompilerParams(vmem_limit_bytes=4 * 2**20)
VMEM = pl.BlockSpec(memory_space=pltpu.VMEM)
HIGHEST = lax.Precision.HIGHEST
f32, bf16 = jnp.float32, jnp.bfloat16


def nn(a, b, precision=None):
    return lax.dot_general(a, b, (((1,), (0,)), ((), ())), precision=precision, preferred_element_type=f32)


def nt(a, b, precision=None):
    return lax.dot_general(a, b, (((1,), (1,)), ((), ())), precision=precision, preferred_element_type=f32)


def struct(shape, dtype):
    return jax.ShapeDtypeStruct(shape, dtype)


def cost(flops, bytes_accessed):
    return pl.CostEstimate(flops=flops, bytes_accessed=bytes_accessed, transcendentals=0)


def pack_kernel(ids, first, second, out):
    width = first.shape[1]
    out[:, :width] = first[...]
    out[:, width:] = second[...]


def pack(matrix, ids, width):
    rows = matrix.shape[0]
    return pl.pallas_call(
        pack_kernel,
        grid_spec=pltpu.PrefetchScalarGridSpec(
            num_scalar_prefetch=1, grid=(1,),
            in_specs=[pl.BlockSpec((rows, width), lambda s, ids: (0, ids[0])),
                      pl.BlockSpec((rows, width), lambda s, ids: (0, ids[1]))],
            out_specs=pl.BlockSpec((rows, 2 * width), lambda s, ids: (0, 0)),
        ),
        out_shape=struct((rows, 2 * width), matrix.dtype),
        compiler_params=SMALL,
        cost_estimate=cost(0, 8 * rows * width),
    )(ids, matrix, matrix)


def call(kernel, args, outs, estimate):
    return pl.pallas_call(
        kernel, in_specs=[VMEM] * len(args), out_specs=[VMEM] * len(outs), out_shape=outs,
        compiler_params=BIG, cost_estimate=estimate,
    )(*args)


def stacked(slots, block, width):
    return jnp.concatenate([ref[:, block * width:(block + 1) * width] for ref in slots], axis=0)


def scores_kernel(count, own, other, *refs):
    width = own.shape[1]
    slots, before, out = refs[:count], refs[count:-1], refs[-1]
    total = nt(own[...], stacked(slots, 0, width)) + nt(other[...], stacked(slots, 1, width))
    out[...] = jnp.concatenate([ref[...] for ref in before] + [total], axis=0) if before else total


def scores(slots, own, other, before):
    rank, width = own.shape
    cells = slots[0].shape[0] * len(slots)
    outs = [struct((rank + sum(x.shape[0] for x in before), cells), f32)]
    return call(functools.partial(scores_kernel, len(slots)), [own, other, *slots, *before], outs,
                cost(4 * rank * cells * width, 4 * cells * width))[0]


def image_kernel(normalised, *refs):
    value, mates = refs[0][...], [ref[...] for ref in refs[1:4]]
    size = value.shape[1] // (GROUP // 2)

    def turned(x, mask):
        return jnp.concatenate([x[:, (j ^ mask) * size:((j ^ mask) + 1) * size] for j in range(GROUP // 2)], axis=1)

    value = (value + turned(mates[0], 1)) + (turned(mates[1], 2) + turned(mates[2], 3))
    if normalised:
        value = nn(refs[4][...], value, HIGHEST)
    refs[-1][...] = value.astype(bf16)


def image_of(value, mates, inverse):
    args = [value, *mates] + ([] if inverse is None else [inverse])
    return pl.pallas_call(
        functools.partial(image_kernel, inverse is not None),
        in_specs=[VMEM] * len(args), out_specs=VMEM, out_shape=struct(value.shape, bf16),
        compiler_params=BIG, cost_estimate=cost(12 * value.size * value.shape[0], 16 * value.size),
    )(*args)


def terms_kernel(block, *refs):
    slots, images, outs = refs[:GROUP], refs[GROUP:GROUP + 2], refs[GROUP + 2:]
    width = outs[0].shape[1]
    total = nn(images[0][...], stacked(slots[0::2], block, width))
    total = total + nn(images[1][...], stacked(slots[1::2], block, width))
    step = total.shape[0] // len(outs)
    for part, out in enumerate(outs):
        out[...] = total[part * step:(part + 1) * step].astype(out.dtype)


def terms(slots, block, images, parts, dtype):
    rank, width = images[0].shape[0], slots[0].shape[1] // 2
    outs = [struct((rank // parts, width), dtype)] * parts
    cells = slots[0].shape[0] * GROUP
    return call(functools.partial(terms_kernel, block), [*slots, *images], outs,
                cost(2 * rank * cells * width, 2 * cells * width))


def fold_kernel(count, with_gram, received, own, *refs):
    before, outs = refs[:count], refs[count:]
    value = own[...] + received[...].astype(f32)
    outs[0][...] = value.astype(outs[0].dtype)
    if not with_gram:
        outs[1][...] = value
        return
    if count:
        value = jnp.concatenate([ref[...] for ref in before] + [value], axis=0)
    outs[1][...] = nt(value, value, HIGHEST)


def fold(received, own, before, dtype, gram):
    rank = own.shape[0] * (1 + len(before))
    second = struct((rank, rank), f32) if gram else struct(own.shape, f32)
    return pl.pallas_call(
        functools.partial(fold_kernel, len(before), gram),
        in_specs=[VMEM] * (2 + len(before)), out_specs=[VMEM] * 2,
        out_shape=[struct(own.shape, dtype), second],
        compiler_params=BIG, cost_estimate=cost(12 * rank * own.size, 12 * own.size),
    )(received, own, *before)


def inverse_factor(gram):
    size = gram.shape[0]
    row = lax.broadcasted_iota(jnp.int32, (size, size), 0)
    column = lax.broadcasted_iota(jnp.int32, (size, size), 1)
    both = jnp.concatenate([gram, jnp.where(row == column, 1.0, 0.0).astype(f32)], axis=1)
    blocks = [both[8 * b:8 * b + 8] for b in range(size // 8)]
    inner = lax.broadcasted_iota(jnp.int32, (8, 2 * size), 0)
    done = []
    for j in range(size):
        b, i = divmod(j, 8)
        root = lax.rsqrt(blocks[b][i:i + 1, j:j + 1])
        pivot = blocks[b][i:i + 1] * root
        done.append(pivot)
        for k in range(b, size // 8):
            factor = jnp.broadcast_to(blocks[k][:, j:j + 1] * root, (8, 2 * size))
            if k == b:
                factor = jnp.where(inner > i, factor, 0.0)
            blocks[k] = blocks[k] - factor * pivot
    return jnp.concatenate(done, axis=0)[:, size:]


def factor_kernel(gram, out):
    out[...] = inverse_factor(gram[...])


def factor_call(gram):
    return pl.pallas_call(
        factor_kernel, in_specs=[VMEM], out_specs=VMEM, out_shape=struct(gram.shape, f32),
        cost_estimate=pl.CostEstimate(flops=20_000_000, bytes_accessed=32768, transcendentals=64),
    )(gram)


def output_kernel(scale, gram, loading, out):
    out[...] = nn(inverse_factor(gram[...]), loading[...], HIGHEST) * scale


def output_call(gram, loading):
    return pl.pallas_call(
        functools.partial(output_kernel, math.sqrt(GENES)),
        in_specs=[VMEM, VMEM], out_specs=VMEM, out_shape=struct(loading.shape, f32),
        compiler_params=pltpu.CompilerParams(vmem_limit_bytes=16 * 2**20),
    )(gram, loading)


def mate(value, cells, mask):
    return lax.ppermute(value, "cell", [(i, i ^ mask) for i in range(cells)])


def total_over_cells(value, cells):
    for low in range(0, cells.bit_length() - 1, 2):
        one, two = 1 << low, 2 << low
        value = (value + mate(value, cells, one)) + (mate(value, cells, two) + mate(value, cells, one | two))
    return value


def square_program(cells, expression, start_basis):
    width, rank = start_basis.shape
    index = lax.axis_index("cell").astype(jnp.int32)
    slots = [None] * GROUP
    for k in (3, 5, 7, 1, 2, 4, 6, 0):
        packed = pack(expression, jnp.stack([index ^ k, index ^ k ^ GROUP]), width)
        slots[k] = mate(packed, cells, k) if k else packed
    step = rank // PARTS

    def summed_image(even, odd, inverse):
        even = even + mate(odd, cells, 1)
        image = image_of(even, [mate(even, cells, mask) for mask in (2, 4, 6)], inverse)
        return image, mate(image, cells, 1)

    basis = start_basis.T
    basis_mate = mate(basis, cells, GROUP)
    odd = scores(slots[1::2], basis, basis_mate, [])
    even = scores(slots[0::2], basis, basis_mate, [])
    images = summed_image(even, odd, None)

    for iteration in range(1, ITERS):
        sent = terms(slots, 1, images, PARTS, bf16)
        own = terms(slots, 0, images, PARTS, f32)
        exact, rounded = [], []
        for part in range(PARTS):
            last = part == PARTS - 1
            rows, kept = fold(mate(sent[part], cells, GROUP), own[part], exact if last else [], bf16, last)
            rounded.append(rows)
            exact.append(kept)
        inverse = factor_call(total_over_cells(exact.pop(), cells))
        odd, even = [], []
        for rows in rounded:
            other = mate(rows, cells, GROUP)
            if len(odd) == PARTS - 1:
                other, inverse = lax.optimization_barrier((other, inverse))
            odd.append(scores(slots[1::2], rows, other, odd))
            even.append(scores(slots[0::2], rows, other, even))
        images = summed_image(even[-1], odd[-1], inverse)

    (sent,) = terms(slots, 1, images, 1, bf16)
    (own,) = terms(slots, 0, images, 1, f32)
    loading, gram = fold(mate(sent, cells, GROUP), own, [], f32, True)
    return output_call(total_over_cells(gram, cells), loading).T


def plain_program(expression, start_basis):
    basis = start_basis
    for _ in range(ITERS):
        whole = lax.all_gather(basis, "cell", axis=0, tiled=True)
        partial = jnp.dot(expression, whole, preferred_element_type=f32)
        image = lax.psum(partial, "gene").astype(bf16)
        partial = lax.dot_general(expression, image, (((0,), (0,)), ((), ())), preferred_element_type=f32)
        loading = lax.psum_scatter(partial, "cell", scatter_dimension=0, tiled=True)
        gram = lax.dot_general(loading, loading, (((0,), (0,)), ((), ())), precision=HIGHEST, preferred_element_type=f32)
        lower = jnp.linalg.cholesky(lax.psum(gram, ("cell", "gene")))
        ortho = jax.scipy.linalg.solve_triangular(lower, loading.T, lower=True).T
        basis = ortho.astype(bf16)
    return ortho * math.sqrt(GENES)


def solution(mesh):
    cells, genes = mesh.shape["cell"], mesh.shape["gene"]

    def on_device(expression, start_basis):
        width, rank = start_basis.shape
        fits = genes == 1 and cells == 2 * GROUP and width % 128 == 0 and rank == 64
        if fits and expression.shape[0] % 16 == 0:
            return square_program(cells, expression, start_basis)
        return plain_program(expression, start_basis)

    return jax.shard_map(
        on_device,
        mesh=mesh,
        in_specs=(P(("groups", "cell"), "gene"), P(("groups", "gene", "cell"), None)),
        out_specs=P(("groups", "gene", "cell"), None),
        check_vma=False,
    )
```

```python
import functools
import math

import jax
import jax.numpy as jnp
from jax import lax
from jax.experimental import pallas as pl
from jax.experimental.pallas import tpu as pltpu
from jax.sharding import PartitionSpec as P

GENES = 30720
ITERS = 2
GROUP = 8
BIG = pltpu.CompilerParams(vmem_limit_bytes=16 * 2**20)
VMEM = pl.BlockSpec(memory_space=pltpu.VMEM)
HIGHEST = lax.Precision.HIGHEST
f32, bf16 = jnp.float32, jnp.bfloat16


def nn(a, b, precision=None):
    return lax.dot_general(a, b, (((1,), (0,)), ((), ())), precision=precision, preferred_element_type=f32)


def nt(a, b, precision=None):
    return lax.dot_general(a, b, (((1,), (1,)), ((), ())), precision=precision, preferred_element_type=f32)


def struct(shape, dtype):
    return jax.ShapeDtypeStruct(shape, dtype)


def cost(flops, bytes_accessed):
    return pl.CostEstimate(flops=flops, bytes_accessed=bytes_accessed, transcendentals=0)


def pack_kernel(ids, matrix, *refs):
    outs, sem = refs[:-1], refs[-1]
    width = outs[0].shape[1] // 2
    copies = []
    for k, out in enumerate(outs):
        for j in range(2):
            start = pl.multiple_of(ids[2 * k + j] * width, 128)
            copies.append(pltpu.make_async_copy(
                matrix.at[:, pl.ds(start, width)], out.at[:, pl.ds(j * width, width)], sem.at[2 * k + j]))
    for copy in copies:
        copy.start()
    for copy in copies:
        copy.wait()


def pack(matrix, ids, width):
    rows, count = matrix.shape[0], ids.shape[0] // 2
    return pl.pallas_call(
        pack_kernel,
        in_specs=[pl.BlockSpec(memory_space=pltpu.SMEM), pl.BlockSpec(memory_space=pltpu.HBM)],
        out_specs=[VMEM] * count,
        out_shape=[struct((rows, 2 * width), matrix.dtype)] * count,
        scratch_shapes=[pltpu.SemaphoreType.DMA((2 * count,))],
        compiler_params=BIG,
        cost_estimate=cost(0, 8 * rows * count * width),
    )(ids, matrix)


def call(kernel, args, outs, estimate):
    return pl.pallas_call(
        kernel, in_specs=[VMEM] * len(args), out_specs=[VMEM] * len(outs), out_shape=outs,
        compiler_params=BIG, cost_estimate=estimate,
    )(*args)


def scores_kernel(block, width, basis, *refs):
    slots, before, outs = refs[:GROUP], refs[GROUP:-2], refs[-2:]
    rows = slots[0].shape[0]
    for odd in range(2):
        for pair in range(GROUP // 4):
            picked = [slots[4 * pair + odd], slots[4 * pair + 2 + odd]]
            big = jnp.concatenate([ref[:, block * width:(block + 1) * width] for ref in picked], axis=0)
            value = nt(big, basis[...]).T
            lanes = slice(2 * pair * rows, 2 * (pair + 1) * rows)
            outs[odd][:, lanes] = value + before[odd][:, lanes] if before else value


def scores(slots, block, basis, before):
    rank, width = basis.shape
    cells = slots[0].shape[0] * GROUP
    return call(functools.partial(scores_kernel, block, width), [basis, *slots, *before],
                [struct((rank, cells // 2), f32)] * 2, cost(2 * rank * cells * width, 2 * cells * width))


def image_kernel(normalised, *refs):
    value, mates = refs[0][...], [ref[...] for ref in refs[1:4]]
    size = value.shape[1] // (GROUP // 2)

    def turned(x, mask):
        return jnp.concatenate([x[:, (j ^ mask) * size:((j ^ mask) + 1) * size] for j in range(GROUP // 2)], axis=1)

    value = (value + turned(mates[0], 1)) + (turned(mates[1], 2) + turned(mates[2], 3))
    if normalised:
        value = nn(refs[4][...], value, HIGHEST)
    refs[-1][...] = value.astype(bf16)


def image_of(value, mates, inverse):
    args = [value, *mates] + ([] if inverse is None else [inverse])
    return pl.pallas_call(
        functools.partial(image_kernel, inverse is not None),
        in_specs=[VMEM] * len(args), out_specs=VMEM, out_shape=struct(value.shape, bf16),
        compiler_params=BIG, cost_estimate=cost(12 * value.size * value.shape[0], 16 * value.size),
    )(*args)


def terms_kernel(block, *refs):
    slots, images, out = refs[:GROUP], refs[GROUP:GROUP + 2], refs[-1]
    width = out.shape[1]
    chunk = width // 3 if width % 384 == 0 else width
    for start in range(0, width, chunk):
        total = 0.0
        for odd in range(2):
            lanes = slice(block * width + start, block * width + start + chunk)
            big = jnp.concatenate([ref[:, lanes] for ref in slots[odd::2]], axis=0)
            total = total + nn(images[odd][...], big)
        out[:, start:start + chunk] = total.astype(out.dtype)


def terms(slots, block, images, dtype):
    rank, width = images[0].shape[0], slots[0].shape[1] // 2
    cells = slots[0].shape[0] * GROUP
    return call(functools.partial(terms_kernel, block), [*slots, *images], [struct((rank, width), dtype)],
                cost(2 * rank * cells * width, 2 * cells * width))[0]


def fold_kernel(received, own, loading, gram):
    value = own[...] + received[...].astype(f32)
    loading[...] = value.astype(loading.dtype)
    gram[...] = nt(value, value, HIGHEST)


def fold(received, own, dtype):
    rank = own.shape[0]
    return call(fold_kernel, [received, own], [struct(own.shape, dtype), struct((rank, rank), f32)],
                cost(12 * rank * own.size, 12 * own.size))


def inverse_factor(gram):
    size = gram.shape[0]
    row = lax.broadcasted_iota(jnp.int32, (size, size), 0)
    column = lax.broadcasted_iota(jnp.int32, (size, size), 1)
    both = jnp.concatenate([gram, jnp.where(row == column, 1.0, 0.0).astype(f32)], axis=1)
    panels = size // 8
    shape = (8, 2 * size)
    blocks = [both[8 * b:8 * b + 8] for b in range(panels)]
    inner = lax.broadcasted_iota(jnp.int32, shape, 0)
    done = []
    for b in range(panels):
        columns = [
            {k: jnp.broadcast_to(blocks[k][:, 8 * b + t:8 * b + t + 1], shape) for k in range(b, panels)}
            for t in range(8)
        ]
        for t in range(8):
            root = lax.rsqrt(jnp.broadcast_to(columns[t][b][t:t + 1], shape))
            scaled = {k: x * root for k, x in columns[t].items()}
            for s in range(t + 1, 8):
                along = jnp.broadcast_to(scaled[b][s:s + 1], shape)
                for k in range(b, panels):
                    columns[s][k] = columns[s][k] - scaled[k] * along
            pivot = jnp.broadcast_to(blocks[b][t:t + 1], shape) * root
            done.append(pivot[:1])
            for k in range(b, panels):
                factor = jnp.where(inner > t, scaled[k], 0.0) if k == b else scaled[k]
                blocks[k] = blocks[k] - factor * pivot
    return jnp.concatenate(done, axis=0)[:, size:]


def factor_kernel(gram, out):
    out[...] = inverse_factor(gram[...])


def factor_call(gram):
    return pl.pallas_call(
        factor_kernel, in_specs=[VMEM], out_specs=VMEM, out_shape=struct(gram.shape, f32),
        cost_estimate=pl.CostEstimate(flops=100_000, bytes_accessed=32768, transcendentals=64),
    )(gram)


def output_kernel(scale, gram, loading, out):
    out[...] = nn(inverse_factor(gram[...]), loading[...], HIGHEST) * scale


def output_call(gram, loading):
    return pl.pallas_call(
        functools.partial(output_kernel, math.sqrt(GENES)),
        in_specs=[VMEM, VMEM], out_specs=VMEM, out_shape=struct(loading.shape, f32),
        compiler_params=pltpu.CompilerParams(vmem_limit_bytes=16 * 2**20),
    )(gram, loading)


def mate(value, cells, mask):
    return lax.ppermute(value, "cell", [(i, i ^ mask) for i in range(cells)])


def total_over_cells(value, cells):
    for low in range(0, cells.bit_length() - 1, 2):
        one, two = 1 << low, 2 << low
        value = (value + mate(value, cells, one)) + (mate(value, cells, two) + mate(value, cells, one | two))
    return value


def square_program(cells, expression, start_basis):
    width = start_basis.shape[0]
    index = lax.axis_index("cell").astype(jnp.int32)
    members = index ^ jnp.arange(GROUP, dtype=jnp.int32)
    slots = pack(expression, jnp.stack([members, members ^ GROUP], axis=1).reshape(-1), width)
    slots = [mate(x, cells, k) if k else x for k, x in enumerate(slots)]

    def image_from(basis, other, inverse):
        even, odd = scores(slots, 1, other, scores(slots, 0, basis, []))
        even = even + mate(odd, cells, 1)
        image = image_of(even, [mate(even, cells, mask) for mask in (2, 4, 6)], inverse)
        return image, mate(image, cells, 1)

    def loading_from(images, dtype):
        received = mate(terms(slots, 1, images, bf16), cells, GROUP)
        rows, gram = fold(received, terms(slots, 0, images, f32), dtype)
        return rows, total_over_cells(gram, cells)

    basis = start_basis.T
    images = image_from(basis, mate(basis, cells, GROUP), None)
    for _ in range(1, ITERS):
        rows, gram = loading_from(images, bf16)
        other, gram = lax.optimization_barrier((mate(rows, cells, GROUP), gram))
        images = image_from(rows, other, factor_call(gram))
    loading, gram = loading_from(images, f32)
    return output_call(gram, loading).T


def plain_program(expression, start_basis):
    basis = start_basis
    for _ in range(ITERS):
        whole = lax.all_gather(basis, "cell", axis=0, tiled=True)
        partial = jnp.dot(expression, whole, preferred_element_type=f32)
        image = lax.psum(partial, "gene").astype(bf16)
        partial = lax.dot_general(expression, image, (((0,), (0,)), ((), ())), preferred_element_type=f32)
        loading = lax.psum_scatter(partial, "cell", scatter_dimension=0, tiled=True)
        gram = lax.dot_general(loading, loading, (((0,), (0,)), ((), ())), precision=HIGHEST, preferred_element_type=f32)
        lower = jnp.linalg.cholesky(lax.psum(gram, ("cell", "gene")))
        ortho = jax.scipy.linalg.solve_triangular(lower, loading.T, lower=True).T
        basis = ortho.astype(bf16)
    return ortho * math.sqrt(GENES)


def solution(mesh):
    cells, genes = mesh.shape["cell"], mesh.shape["gene"]

    def on_device(expression, start_basis):
        width, rank = start_basis.shape
        fits = genes == 1 and cells == 2 * GROUP and width % 128 == 0 and rank == 64
        if fits and expression.shape[0] % 16 == 0:
            return square_program(cells, expression, start_basis)
        return plain_program(expression, start_basis)

    return jax.shard_map(
        on_device,
        mesh=mesh,
        in_specs=(P(("groups", "cell"), "gene"), P(("groups", "gene", "cell"), None)),
        out_specs=P(("groups", "gene", "cell"), None),
        check_vma=False,
    )
```

```python
import functools
import math

import jax
import jax.numpy as jnp
from jax import lax
from jax.experimental import pallas as pl
from jax.experimental.pallas import tpu as pltpu
from jax.sharding import PartitionSpec as P

GENES = 30720
ITERS = 2
GROUP = 8
BIG = pltpu.CompilerParams(vmem_limit_bytes=16 * 2**20)
VMEM = pl.BlockSpec(memory_space=pltpu.VMEM)
HIGHEST = lax.Precision.HIGHEST
f32, bf16 = jnp.float32, jnp.bfloat16


def nn(a, b, precision=None):
    return lax.dot_general(a, b, (((1,), (0,)), ((), ())), precision=precision, preferred_element_type=f32)


def nt(a, b, precision=None):
    return lax.dot_general(a, b, (((1,), (1,)), ((), ())), precision=precision, preferred_element_type=f32)


def struct(shape, dtype):
    return jax.ShapeDtypeStruct(shape, dtype)


def cost(flops, bytes_accessed):
    return pl.CostEstimate(flops=flops, bytes_accessed=bytes_accessed, transcendentals=0)


def pack_kernel(ids, matrix, *refs):
    outs, sem = refs[:-1], refs[-1]
    width = outs[0].shape[1] // 2
    copies = []
    for k, out in enumerate(outs):
        for j in range(2):
            start = pl.multiple_of(ids[2 * k + j] * width, 128)
            copies.append(pltpu.make_async_copy(
                matrix.at[:, pl.ds(start, width)], out.at[:, pl.ds(j * width, width)], sem.at[2 * k + j]))
    for copy in copies:
        copy.start()
    for copy in copies:
        copy.wait()


def pack(matrix, ids, width):
    rows, count = matrix.shape[0], ids.shape[0] // 2
    return pl.pallas_call(
        pack_kernel,
        in_specs=[pl.BlockSpec(memory_space=pltpu.SMEM), pl.BlockSpec(memory_space=pltpu.HBM)],
        out_specs=[VMEM] * count,
        out_shape=[struct((rows, 2 * width), matrix.dtype)] * count,
        scratch_shapes=[pltpu.SemaphoreType.DMA((2 * count,))],
        compiler_params=pltpu.CompilerParams(vmem_limit_bytes=56 * 2**20),
        cost_estimate=cost(0, 8 * rows * count * width),
    )(ids, matrix)


def call(kernel, args, outs, estimate):
    return pl.pallas_call(
        kernel, in_specs=[VMEM] * len(args), out_specs=[VMEM] * len(outs), out_shape=outs,
        compiler_params=BIG, cost_estimate=estimate,
    )(*args)


def scores_kernel(block, width, basis, *refs):
    slots, before, outs = refs[:GROUP], refs[GROUP:-2], refs[-2:]
    rows = slots[0].shape[0]
    for odd in range(2):
        for pair in range(GROUP // 4):
            picked = [slots[4 * pair + odd], slots[4 * pair + 2 + odd]]
            big = jnp.concatenate([ref[:, block * width:(block + 1) * width] for ref in picked], axis=0)
            value = nt(big, basis[...]).T
            lanes = slice(2 * pair * rows, 2 * (pair + 1) * rows)
            outs[odd][:, lanes] = value + before[odd][:, lanes] if before else value


def scores(slots, block, basis, before):
    rank, width = basis.shape
    cells = slots[0].shape[0] * GROUP
    return call(functools.partial(scores_kernel, block, width), [basis, *slots, *before],
                [struct((rank, cells // 2), f32)] * 2, cost(2 * rank * cells * width, 2 * cells * width))


def image_kernel(normalised, own, values, *refs):
    size = values.shape[2] // 4

    def turned(x, mask):
        return jnp.concatenate([x[:, (j ^ mask) * size:((j ^ mask) + 1) * size] for j in range(4)], axis=1)

    terms = [turned(values[r], r) for r in range(4)]
    value = (terms[0] + terms[1]) + (terms[2] + terms[3])
    for bit in range(2):
        value = jnp.where((own[0] >> bit) & 1 == 1, turned(value, 1 << bit), value)
    if normalised:
        value = nn(refs[0][...], value, HIGHEST)
    refs[-1][...] = value.astype(bf16)


def image_of(own, values, inverse):
    args = [own, values] + ([] if inverse is None else [inverse])
    return pl.pallas_call(
        functools.partial(image_kernel, inverse is not None),
        in_specs=[pl.BlockSpec(memory_space=pltpu.SMEM)] + [VMEM] * (len(args) - 1), out_specs=VMEM,
        out_shape=struct(values.shape[1:], bf16),
        compiler_params=BIG, cost_estimate=cost(12 * values.size, 4 * values.size),
    )(*args)


def terms_kernel(block, *refs):
    slots, images, out = refs[:GROUP], refs[GROUP:GROUP + 2], refs[-1]
    width = out.shape[1]
    chunk = width // 3 if width % 384 == 0 else width
    for start in range(0, width, chunk):
        total = 0.0
        for odd in range(2):
            lanes = slice(block * width + start, block * width + start + chunk)
            big = jnp.concatenate([ref[:, lanes] for ref in slots[odd::2]], axis=0)
            total = total + nn(images[odd][...], big)
        out[:, start:start + chunk] = total.astype(out.dtype)


def terms(slots, block, images, dtype):
    rank, width = images[0].shape[0], slots[0].shape[1] // 2
    cells = slots[0].shape[0] * GROUP
    return call(functools.partial(terms_kernel, block), [*slots, *images], [struct((rank, width), dtype)],
                cost(2 * rank * cells * width, 2 * cells * width))[0]


def fold_kernel(received, own, loading, gram):
    value = own[...] + received[...].astype(f32)
    loading[...] = value.astype(loading.dtype)
    gram[...] = nt(value, value, HIGHEST)


def fold(received, own, dtype):
    rank = own.shape[0]
    return call(fold_kernel, [received, own], [struct(own.shape, dtype), struct((rank, rank), f32)],
                cost(12 * rank * own.size, 12 * own.size))


def inverse_factor(gram):
    size = gram.shape[0]
    row = lax.broadcasted_iota(jnp.int32, (size, size), 0)
    column = lax.broadcasted_iota(jnp.int32, (size, size), 1)
    both = jnp.concatenate([gram, jnp.where(row == column, 1.0, 0.0).astype(f32)], axis=1)
    panels = size // 8
    shape = (8, 2 * size)
    blocks = [both[8 * b:8 * b + 8] for b in range(panels)]
    inner = lax.broadcasted_iota(jnp.int32, shape, 0)
    done = []
    for b in range(panels):
        columns = [
            {k: jnp.broadcast_to(blocks[k][:, 8 * b + t:8 * b + t + 1], shape) for k in range(b, panels)}
            for t in range(8)
        ]
        for t in range(8):
            root = lax.rsqrt(jnp.broadcast_to(columns[t][b][t:t + 1], shape))
            scaled = {k: x * root for k, x in columns[t].items()}
            for s in range(t + 1, 8):
                along = jnp.broadcast_to(scaled[b][s:s + 1], shape)
                for k in range(b, panels):
                    columns[s][k] = columns[s][k] - scaled[k] * along
            pivot = jnp.broadcast_to(blocks[b][t:t + 1], shape) * root
            done.append(pivot[:1])
            for k in range(b, panels):
                factor = jnp.where(inner > t, scaled[k], 0.0) if k == b else scaled[k]
                blocks[k] = blocks[k] - factor * pivot
    return jnp.concatenate(done, axis=0)[:, size:]


def factor_kernel(gram, out):
    out[...] = inverse_factor(gram[...])


def factor_call(gram):
    return pl.pallas_call(
        factor_kernel, in_specs=[VMEM], out_specs=VMEM, out_shape=struct(gram.shape, f32),
        cost_estimate=pl.CostEstimate(flops=100_000, bytes_accessed=32768, transcendentals=64),
    )(gram)


def output_kernel(scale, gram, loading, out):
    out[...] = nn(inverse_factor(gram[...]), loading[...], HIGHEST) * scale


def output_call(gram, loading):
    return pl.pallas_call(
        functools.partial(output_kernel, math.sqrt(GENES)),
        in_specs=[VMEM, VMEM], out_specs=VMEM, out_shape=struct(loading.shape, f32),
        compiler_params=pltpu.CompilerParams(vmem_limit_bytes=16 * 2**20),
    )(gram, loading)


def mate(value, cells, mask):
    return lax.ppermute(value, "cell", [(i, i ^ mask) for i in range(cells)])


def from_four(value, cells, low):
    four = [base + low * j for base in range(cells) if not base & (3 * low) for j in range(4)]
    groups = [four[i:i + 4] for i in range(0, cells, 4)]
    return lax.all_to_all(jnp.broadcast_to(value, (4,) + value.shape), "cell", 0, 0, axis_index_groups=groups)


def total_over_cells(value, cells):
    for low in (4, 1):
        x = from_four(value, cells, low)
        value = (x[0] + x[1]) + (x[2] + x[3])
    return value


def square_program(cells, expression, start_basis):
    width = start_basis.shape[0]
    index = lax.axis_index("cell").astype(jnp.int32)
    members = index ^ jnp.arange(GROUP, dtype=jnp.int32)
    packs = pack(expression, jnp.stack([members, members ^ GROUP], axis=1).reshape(-1), width)
    slots = list(packs)
    for k in (1, 6, 2, 4, 7, 3, 5):
        slots[k] = mate(packs[k], cells, k)

    place = ((index >> 1) & 3).reshape(1)

    def image_from(basis, other, inverse):
        even, odd = scores(slots, 1, other, scores(slots, 0, basis, []))
        even = even + mate(odd, cells, 1)
        image = image_of(place, from_four(even, cells, 2), inverse)
        return image, mate(image, cells, 1)

    def loading_from(images, dtype):
        received = mate(terms(slots, 1, images, bf16), cells, GROUP)
        rows, gram = fold(received, terms(slots, 0, images, f32), dtype)
        return rows, total_over_cells(gram, cells)

    basis = start_basis.T
    images = image_from(basis, mate(basis, cells, GROUP), None)
    for _ in range(1, ITERS):
        rows, gram = loading_from(images, bf16)
        other, gram = lax.optimization_barrier((mate(rows, cells, GROUP), gram))
        images = image_from(rows, other, factor_call(gram))
    loading, gram = loading_from(images, f32)
    return output_call(gram, loading).T


def plain_program(expression, start_basis):
    basis = start_basis
    for _ in range(ITERS):
        whole = lax.all_gather(basis, "cell", axis=0, tiled=True)
        partial = jnp.dot(expression, whole, preferred_element_type=f32)
        image = lax.psum(partial, "gene").astype(bf16)
        partial = lax.dot_general(expression, image, (((0,), (0,)), ((), ())), preferred_element_type=f32)
        loading = lax.psum_scatter(partial, "cell", scatter_dimension=0, tiled=True)
        gram = lax.dot_general(loading, loading, (((0,), (0,)), ((), ())), precision=HIGHEST, preferred_element_type=f32)
        lower = jnp.linalg.cholesky(lax.psum(gram, ("cell", "gene")))
        ortho = jax.scipy.linalg.solve_triangular(lower, loading.T, lower=True).T
        basis = ortho.astype(bf16)
    return ortho * math.sqrt(GENES)


def solution(mesh):
    cells, genes = mesh.shape["cell"], mesh.shape["gene"]

    def on_device(expression, start_basis):
        width, rank = start_basis.shape
        fits = genes == 1 and cells == 2 * GROUP and width % 128 == 0 and rank == 64
        if fits and expression.shape[0] % 16 == 0:
            return square_program(cells, expression, start_basis)
        return plain_program(expression, start_basis)

    return jax.shard_map(
        on_device,
        mesh=mesh,
        in_specs=(P(("groups", "cell"), "gene"), P(("groups", "gene", "cell"), None)),
        out_specs=P(("groups", "gene", "cell"), None),
        check_vma=False,
    )
```

```python
import functools
import math

import jax
import jax.numpy as jnp
from jax import lax
from jax.experimental import pallas as pl
from jax.experimental.pallas import tpu as pltpu
from jax.sharding import PartitionSpec as P

GENES = 30720
ITERS = 2
GROUP = 8
BIG = pltpu.CompilerParams(vmem_limit_bytes=16 * 2**20)
VMEM = pl.BlockSpec(memory_space=pltpu.VMEM)
HIGHEST = lax.Precision.HIGHEST
f32, bf16 = jnp.float32, jnp.bfloat16


def nn(a, b, precision=None):
    return lax.dot_general(a, b, (((1,), (0,)), ((), ())), precision=precision, preferred_element_type=f32)


def nt(a, b, precision=None):
    return lax.dot_general(a, b, (((1,), (1,)), ((), ())), precision=precision, preferred_element_type=f32)


def three(x):
    high = x.astype(bf16)
    rest = x - high.astype(f32)
    middle = rest.astype(bf16)
    return high, middle, (rest - middle.astype(f32)).astype(bf16)


def exact_nn(a, b):
    a1, a2, a3 = three(a)
    b1, b2, b3 = three(b)
    return nn(jnp.concatenate([a3, a2, a1, a2, a1, a1], axis=1), jnp.concatenate([b1, b2, b3, b1, b2, b1], axis=0))


def exact_gram(a):
    size = a.shape[0]
    parts = jnp.concatenate(three(a), axis=0)
    every = nt(parts, parts)

    def part(i, j):
        return every[i * size:(i + 1) * size, j * size:(j + 1) * size]

    small = (part(0, 2) + part(2, 0)) + part(1, 1)
    return part(0, 0) + ((part(0, 1) + part(1, 0)) + small)


def struct(shape, dtype):
    return jax.ShapeDtypeStruct(shape, dtype)


def cost(flops, bytes_accessed):
    return pl.CostEstimate(flops=flops, bytes_accessed=bytes_accessed, transcendentals=0)


def pack_kernel(ids, matrix, *refs):
    outs, sem = refs[:-1], refs[-1]
    width = outs[0].shape[1] // 2
    copies = []
    for k, out in enumerate(outs):
        for j in range(2):
            start = pl.multiple_of(ids[2 * k + j] * width, 128)
            copies.append(pltpu.make_async_copy(
                matrix.at[:, pl.ds(start, width)], out.at[:, pl.ds(j * width, width)], sem.at[2 * k + j]))
    for copy in copies:
        copy.start()
    for copy in copies:
        copy.wait()


def pack(matrix, ids, width, direct):
    rows, count = matrix.shape[0], ids.shape[0] // 2
    return pl.pallas_call(
        pack_kernel,
        in_specs=[pl.BlockSpec(memory_space=pltpu.SMEM), pl.BlockSpec(memory_space=pltpu.HBM)],
        out_specs=[VMEM] * count,
        out_shape=[struct((rows, 2 * width), matrix.dtype)] * count,
        scratch_shapes=[pltpu.SemaphoreType.DMA((2 * count,))],
        compiler_params=pltpu.CompilerParams(vmem_limit_bytes=(60 if direct else 16) * 2**20),
        cost_estimate=cost(0, 8 * rows * count * width),
    )(ids, matrix)


def call(kernel, args, outs, estimate):
    return pl.pallas_call(
        kernel, in_specs=[VMEM] * len(args), out_specs=[VMEM] * len(outs), out_shape=outs,
        compiler_params=BIG, cost_estimate=estimate,
    )(*args)


def scores_kernel(pairs, blocks, counts, picked, joined, with_gram, width, *refs):
    refs = list(refs)
    bases = [[refs.pop(0) for _ in range(count)] for count in counts]
    slots = {k: refs.pop(0) for k in picked}
    gram = refs.pop(0)[...] if with_gram else None
    before, outs = refs[:-2], refs[-2:]
    rank = gram.shape[0] if with_gram else 0
    for odd in range(2):
        left = 0
        if joined:
            left = before[odd].shape[1]
            outs[odd][:, :left] = before[odd][...]
        for pair in pairs:
            value = 0.0
            for block, parts in zip(blocks, bases):
                start = block * width
                for part in parts:
                    stop = min(start + part.shape[1], (block + 1) * width)
                    big = [slots[4 * pair + odd][:, start:stop], slots[4 * pair + 2 + odd][:, start:stop]]
                    value = value + nt(jnp.concatenate(big, axis=0), part[:, :stop - start])
                    start = stop
            value = value.T
            lanes = slice(left, left + value.shape[1])
            left += value.shape[1]
            outs[odd][:, lanes] = value + before[odd][:, lanes] if before and not joined else value
        if with_gram:
            tail = bases[-1][-1]
            first = tail.shape[1] - 3 * rank
            theirs = [tail[:, first + i * rank:first + (i + 1) * rank].astype(f32) for i in range(3)]
            outs[odd][:, left:] = gram + ((theirs[0] + theirs[1]) + theirs[2])


def scores(slots, pairs, blocks, bases, before=(), joined=False, gram=None):
    rank = bases[0][0].shape[0]
    width = slots[pairs[0] * 4].shape[1] // 2
    picked = [4 * pair + k for pair in pairs for k in range(4)]
    rows = slots[picked[0]].shape[0]
    cells = 2 * rows * len(pairs) + (before[0].shape[1] if joined else 0) + (0 if gram is None else rank)
    counts = [len(parts) for parts in bases]
    args = [x for parts in bases for x in parts] + [slots[k] for k in picked]
    args += ([] if gram is None else [gram]) + list(before)
    work = rows * len(picked) * width * len(blocks)
    kernel = functools.partial(scores_kernel, pairs, blocks, counts, picked, joined, gram is not None, width)
    return call(kernel, args, [struct((rank, cells), f32)] * 2, cost(2 * rank * work, 2 * work))


def image_kernel(normalised, *refs):
    values, out = [ref[...] for ref in refs[:-1]], refs[-1]
    cells = out.shape[1]
    size = cells // (GROUP // 2)

    def turned(x, mask):
        return jnp.concatenate([x[:, (j ^ mask) * size:((j ^ mask) + 1) * size] for j in range(GROUP // 2)], axis=1)

    value = (values[0][:, :cells] + turned(values[1], 1)) + (turned(values[2], 2) + turned(values[3], 3))
    if normalised:
        gram = [x[:, cells:] for x in values]
        value = exact_nn(inverse_factor((gram[0] + gram[1]) + (gram[2] + gram[3])), value)
    out[...] = value.astype(bf16)


def image_of(value, mates, rows, normalised):
    rank, cells = value.shape[0], rows * GROUP // 2
    return call(functools.partial(image_kernel, normalised), [value, *mates], [struct((rank, cells), bf16)],
                cost(12 * value.size * rank, 16 * value.size))[0]


def terms_kernel(block, width, *refs):
    slots, images, outs = refs[:GROUP], refs[GROUP:GROUP + 2], refs[GROUP + 2:]
    start = block * width
    for out in outs:
        step = out.shape[1] // 2 if out.shape[1] % 256 == 0 else out.shape[1]
        for left in range(0, out.shape[1], step):
            total = 0.0
            for odd in range(2):
                big = jnp.concatenate([ref[:, start:start + step] for ref in slots[odd::2]], axis=0)
                total = total + nn(images[odd][...], big)
            out[:, left:left + step] = total.astype(out.dtype)
            start += step


def terms(slots, block, images, cuts, dtype):
    rank, width = images[0].shape[0], slots[0].shape[1] // 2
    cells = slots[0].shape[0] * GROUP
    return call(functools.partial(terms_kernel, block, width), [*slots, *images], [struct((rank, w), dtype) for w in cuts],
                cost(2 * rank * cells * width, 2 * cells * width))


def fold_kernel(final, received, own, *refs):
    before, outs = refs[:-2], refs[-2:]
    width = own.shape[1]
    value = own[...] + received[...].astype(f32)
    outs[0][:, :width] = value.astype(outs[0].dtype)
    gram = exact_gram(value)
    for ref in before:
        gram = gram + ref[...]
    outs[1][...] = gram
    if final:
        for i, part in enumerate(three(gram)):
            outs[0][:, width + i * part.shape[1]:width + (i + 1) * part.shape[1]] = part


def fold(received, own, before, dtype, final):
    rank, width = own.shape
    return call(functools.partial(fold_kernel, final), [received, own, *before],
                [struct((rank, width + (3 * rank if final else 0)), dtype), struct((rank, rank), f32)],
                cost(12 * rank * own.size, 12 * own.size))


def inverse_factor(gram):
    size = gram.shape[0]
    row = lax.broadcasted_iota(jnp.int32, (size, size), 0)
    column = lax.broadcasted_iota(jnp.int32, (size, size), 1)
    both = jnp.concatenate([gram, jnp.where(row == column, 1.0, 0.0).astype(f32)], axis=1)
    panels = size // 8
    shape = (8, 2 * size)
    blocks = [both[8 * b:8 * b + 8] for b in range(panels)]
    inner = lax.broadcasted_iota(jnp.int32, shape, 0)
    done = []
    for b in range(panels):
        columns = [
            {k: jnp.broadcast_to(blocks[k][:, 8 * b + t:8 * b + t + 1], shape) for k in range(b, panels)}
            for t in range(8)
        ]
        for t in range(8):
            root = lax.rsqrt(jnp.broadcast_to(columns[t][b][t:t + 1], shape))
            scaled = {k: x * root for k, x in columns[t].items()}
            for s in range(t + 1, 8):
                along = jnp.broadcast_to(scaled[b][s:s + 1], shape)
                for k in range(b, panels):
                    columns[s][k] = columns[s][k] - scaled[k] * along
            pivot = jnp.broadcast_to(blocks[b][t:t + 1], shape) * root
            done.append(pivot[:1])
            for k in range(b, panels):
                factor = jnp.where(inner > t, scaled[k], 0.0) if k == b else scaled[k]
                blocks[k] = blocks[k] - factor * pivot
    return jnp.concatenate(done, axis=0)[:, size:]


def output_kernel(scale, gram, loading, out):
    out[...] = exact_nn(inverse_factor(gram[...]), loading[...]) * scale


def output_call(gram, loading):
    return pl.pallas_call(
        functools.partial(output_kernel, math.sqrt(GENES)),
        in_specs=[VMEM, VMEM], out_specs=VMEM, out_shape=struct(loading.shape, f32),
        compiler_params=pltpu.CompilerParams(vmem_limit_bytes=16 * 2**20),
    )(gram, loading)


def mate(value, cells, mask):
    return lax.ppermute(value, "cell", [(i, i ^ mask) for i in range(cells)])


def total_over_cells(value, cells):
    for one, two in ((GROUP, 1), (2, 4)):
        value = (value + mate(value, cells, one)) + (mate(value, cells, one | two) + mate(value, cells, two))
    return value


def square_program(cells, expression, start_basis):
    width, rows = start_basis.shape[0], expression.shape[0]
    index = lax.axis_index("cell").astype(jnp.int32)
    slots = [None] * GROUP
    for masks, direct in (((2, 4), True), ((1, 6, 3, 5, 7, 0), False)):
        members = index ^ jnp.array(masks, jnp.int32)
        ids = jnp.stack([members, members ^ GROUP], axis=1).reshape(-1)
        for k, packed in zip(masks, pack(expression, ids, width, direct)):
            slots[k] = mate(packed, cells, k) if k else packed

    def image_from(totals, normalised):
        even, odd = totals
        even = even + mate(odd, cells, 1)
        image = image_of(even, [mate(even, cells, mask) for mask in (2, 4, 6)], rows, normalised)
        return image, mate(image, cells, 1)

    def terms_and_received(images, cuts):
        sent = terms(slots, 1, images, cuts, bf16)
        own = terms(slots, 0, images, cuts, f32)
        return zip([mate(x, cells, GROUP) for x in sent], own)

    half = -(-6 * width // 1280) * 128
    basis = start_basis.T
    bases = [[basis], [mate(basis, cells, GROUP)]]
    images = image_from(scores(slots, (1,), (0, 1), bases, scores(slots, (0,), (0, 1), bases), True), False)
    for _ in range(1, ITERS):
        parts, copies, gram = [], [], []
        for received, own in terms_and_received(images, (half, width - half)):
            part, total = fold(received, own, gram, bf16, bool(parts))
            gram = [total]
            parts.append(part)
            copies.append(mate(part, cells, GROUP))
        early = scores(slots, (0, 1), (0,), [parts])
        images = image_from(scores(slots, (0, 1), (1,), [copies], early, gram=gram[0]), True)
    ((received, own),) = terms_and_received(images, (width,))
    loading, gram = fold(received, own, [], f32, False)
    return output_call(total_over_cells(gram, cells), loading).T


def plain_program(expression, start_basis):
    basis = start_basis
    for _ in range(ITERS):
        whole = lax.all_gather(basis, "cell", axis=0, tiled=True)
        partial = jnp.dot(expression, whole, preferred_element_type=f32)
        image = lax.psum(partial, "gene").astype(bf16)
        partial = lax.dot_general(expression, image, (((0,), (0,)), ((), ())), preferred_element_type=f32)
        loading = lax.psum_scatter(partial, "cell", scatter_dimension=0, tiled=True)
        gram = lax.dot_general(loading, loading, (((0,), (0,)), ((), ())), precision=HIGHEST, preferred_element_type=f32)
        lower = jnp.linalg.cholesky(lax.psum(gram, ("cell", "gene")))
        ortho = jax.scipy.linalg.solve_triangular(lower, loading.T, lower=True).T
        basis = ortho.astype(bf16)
    return ortho * math.sqrt(GENES)


def solution(mesh):
    cells, genes = mesh.shape["cell"], mesh.shape["gene"]

    def on_device(expression, start_basis):
        width, rank = start_basis.shape
        fits = genes == 1 and cells == 2 * GROUP and width % 128 == 0 and rank == 64
        if fits and expression.shape[0] % 16 == 0:
            return square_program(cells, expression, start_basis)
        return plain_program(expression, start_basis)

    return jax.shard_map(
        on_device,
        mesh=mesh,
        in_specs=(P(("groups", "cell"), "gene"), P(("groups", "gene", "cell"), None)),
        out_specs=P(("groups", "gene", "cell"), None),
        check_vma=False,
    )
```

```python
import functools
import math

import jax
import jax.numpy as jnp
from jax import lax
from jax.experimental import pallas as pl
from jax.experimental.pallas import tpu as pltpu
from jax.sharding import PartitionSpec as P

GENES = 30720
ITERS = 2
GROUP = 8
BIG = pltpu.CompilerParams(vmem_limit_bytes=16 * 2**20)
VMEM = pl.BlockSpec(memory_space=pltpu.VMEM)
HIGHEST = lax.Precision.HIGHEST
f32, bf16 = jnp.float32, jnp.bfloat16


def nn(a, b, precision=None):
    return lax.dot_general(a, b, (((1,), (0,)), ((), ())), precision=precision, preferred_element_type=f32)


def nt(a, b, precision=None):
    return lax.dot_general(a, b, (((1,), (1,)), ((), ())), precision=precision, preferred_element_type=f32)


def three(x):
    high = x.astype(bf16)
    rest = x - high.astype(f32)
    middle = rest.astype(bf16)
    return high, middle, (rest - middle.astype(f32)).astype(bf16)


def exact_nn(a, b):
    a1, a2, a3 = three(a)
    b1, b2, b3 = three(b)
    return nn(jnp.concatenate([a3, a2, a1, a2, a1, a1], axis=1), jnp.concatenate([b1, b2, b3, b1, b2, b1], axis=0))


def exact_gram(a):
    size = a.shape[0]
    parts = jnp.concatenate(three(a), axis=0)
    every = nt(parts, parts)

    def part(i, j):
        return every[i * size:(i + 1) * size, j * size:(j + 1) * size]

    small = (part(0, 2) + part(2, 0)) + part(1, 1)
    return part(0, 0) + ((part(0, 1) + part(1, 0)) + small)


def struct(shape, dtype):
    return jax.ShapeDtypeStruct(shape, dtype)


def cost(flops, bytes_accessed):
    return pl.CostEstimate(flops=flops, bytes_accessed=bytes_accessed, transcendentals=0)


def pack_kernel(ids, matrix, *refs):
    outs, sem = refs[:-1], refs[-1]
    width = outs[0].shape[1] // 2
    copies = []
    for k, out in enumerate(outs):
        for j in range(2):
            start = pl.multiple_of(ids[2 * k + j] * width, 128)
            copies.append(pltpu.make_async_copy(
                matrix.at[:, pl.ds(start, width)], out.at[:, pl.ds(j * width, width)], sem.at[2 * k + j]))
    for copy in copies:
        copy.start()
    for copy in copies:
        copy.wait()


def pack(matrix, ids, width):
    rows, count = matrix.shape[0], ids.shape[0] // 2
    return pl.pallas_call(
        pack_kernel,
        in_specs=[pl.BlockSpec(memory_space=pltpu.SMEM), pl.BlockSpec(memory_space=pltpu.HBM)],
        out_specs=[VMEM] * count,
        out_shape=[struct((rows, 2 * width), matrix.dtype)] * count,
        scratch_shapes=[pltpu.SemaphoreType.DMA((2 * count,))],
        compiler_params=BIG,
        cost_estimate=cost(0, 8 * rows * count * width),
    )(ids, matrix)


def call(kernel, args, outs, estimate):
    return pl.pallas_call(
        kernel, in_specs=[VMEM] * len(args), out_specs=[VMEM] * len(outs), out_shape=outs,
        compiler_params=BIG, cost_estimate=estimate,
    )(*args)


def scores_kernel(work, counts, picked, with_gram, width, *refs):
    refs = list(refs)
    bases = {block: [refs.pop(0) for _ in range(count)] for block, count in counts}
    slots = {k: refs.pop(0) for k in picked}
    gram = refs.pop(0)[...] if with_gram else None
    before, outs = refs[:-2], refs[-2:]
    rank = gram.shape[0] if with_gram else 0
    for odd in range(2):
        left = 0
        for pair, blocks in work:
            value = 0.0
            for block in blocks:
                start = block * width
                for part in bases[block]:
                    stop = min(start + part.shape[1], (block + 1) * width)
                    big = [slots[4 * pair + odd][:, start:stop], slots[4 * pair + 2 + odd][:, start:stop]]
                    value = value + nt(jnp.concatenate(big, axis=0), part[:, :stop - start])
                    start = stop
            value = value.T
            lanes = slice(left, left + value.shape[1])
            left = lanes.stop
            known = before and lanes.stop <= before[odd].shape[1]
            outs[odd][:, lanes] = value + before[odd][:, lanes] if known else value
        if with_gram:
            tail = bases[counts[-1][0]][-1]
            first = tail.shape[1] - 3 * rank
            theirs = [tail[:, first + i * rank:first + (i + 1) * rank].astype(f32) for i in range(3)]
            outs[odd][:, left:] = gram + ((theirs[0] + theirs[1]) + theirs[2])


def scores(slots, work, bases, before=(), gram=None):
    rank = next(iter(bases.values()))[0].shape[0]
    picked = [4 * pair + k for pair, _ in work for k in range(4)]
    rows, width = slots[picked[0]].shape[0], slots[picked[0]].shape[1] // 2
    cells = 2 * rows * len(work) + (0 if gram is None else rank)
    counts = [(block, len(parts)) for block, parts in bases.items()]
    args = [x for parts in bases.values() for x in parts] + [slots[k] for k in picked]
    args += ([] if gram is None else [gram]) + list(before)
    size = 4 * rows * width * sum(len(blocks) for _, blocks in work)
    kernel = functools.partial(scores_kernel, work, counts, picked, gram is not None, width)
    return call(kernel, args, [struct((rank, cells), f32)] * 2, cost(2 * rank * size, 2 * size))


def image_kernel(normalised, *refs):
    values, out = [ref[...] for ref in refs[:-1]], refs[-1]
    cells = out.shape[1]
    size = cells // (GROUP // 2)

    def turned(x, mask):
        return jnp.concatenate([x[:, (j ^ mask) * size:((j ^ mask) + 1) * size] for j in range(GROUP // 2)], axis=1)

    value = (values[0][:, :cells] + turned(values[3], 3)) + (turned(values[1], 1) + turned(values[2], 2))
    if normalised:
        gram = [x[:, cells:] for x in values]
        value = exact_nn(inverse_factor((gram[0] + gram[3]) + (gram[1] + gram[2])), value)
    out[...] = value.astype(bf16)


def image_of(value, mates, rows, normalised):
    rank, cells = value.shape[0], rows * GROUP // 2
    return call(functools.partial(image_kernel, normalised), [value, *mates], [struct((rank, cells), bf16)],
                cost(12 * value.size * rank, 16 * value.size))[0]


def terms_kernel(block, width, *refs):
    slots, images, outs = refs[:GROUP], refs[GROUP:GROUP + 2], refs[GROUP + 2:]
    start = block * width
    for out in outs:
        step = out.shape[1] // 2 if out.shape[1] % 256 == 0 else out.shape[1]
        for left in range(0, out.shape[1], step):
            total = 0.0
            for odd in range(2):
                big = jnp.concatenate([ref[:, start:start + step] for ref in slots[odd::2]], axis=0)
                total = total + nn(images[odd][...], big)
            out[:, left:left + step] = total.astype(out.dtype)
            start += step


def terms(slots, block, images, cuts, dtype):
    rank, width = images[0].shape[0], slots[0].shape[1] // 2
    cells = slots[0].shape[0] * GROUP
    return call(functools.partial(terms_kernel, block, width), [*slots, *images], [struct((rank, w), dtype) for w in cuts],
                cost(2 * rank * cells * width, 2 * cells * width))


def fold_kernel(final, received, own, *refs):
    before, outs = refs[:-2], refs[-2:]
    width = own.shape[1]
    value = own[...] + received[...].astype(f32)
    outs[0][:, :width] = value.astype(outs[0].dtype)
    gram = exact_gram(value)
    for ref in before:
        gram = gram + ref[...]
    outs[1][...] = gram
    if final:
        for i, part in enumerate(three(gram)):
            outs[0][:, width + i * part.shape[1]:width + (i + 1) * part.shape[1]] = part


def fold(received, own, before, dtype, final):
    rank, width = own.shape
    return call(functools.partial(fold_kernel, final), [received, own, *before],
                [struct((rank, width + (3 * rank if final else 0)), dtype), struct((rank, rank), f32)],
                cost(12 * rank * own.size, 12 * own.size))


def inverse_factor(gram):
    size = gram.shape[0]
    row = lax.broadcasted_iota(jnp.int32, (size, size), 0)
    column = lax.broadcasted_iota(jnp.int32, (size, size), 1)
    both = jnp.concatenate([gram, jnp.where(row == column, 1.0, 0.0).astype(f32)], axis=1)
    panels = size // 8
    shape = (8, 2 * size)
    blocks = [both[8 * b:8 * b + 8] for b in range(panels)]
    inner = lax.broadcasted_iota(jnp.int32, shape, 0)
    done = []
    for b in range(panels):
        columns = [
            {k: jnp.broadcast_to(blocks[k][:, 8 * b + t:8 * b + t + 1], shape) for k in range(b, panels)}
            for t in range(8)
        ]
        for t in range(8):
            root = lax.rsqrt(jnp.broadcast_to(columns[t][b][t:t + 1], shape))
            scaled = {k: x * root for k, x in columns[t].items()}
            for s in range(t + 1, 8):
                along = jnp.broadcast_to(scaled[b][s:s + 1], shape)
                for k in range(b, panels):
                    columns[s][k] = columns[s][k] - scaled[k] * along
            pivot = jnp.broadcast_to(blocks[b][t:t + 1], shape) * root
            done.append(pivot[:1])
            for k in range(b, panels):
                factor = jnp.where(inner > t, scaled[k], 0.0) if k == b else scaled[k]
                blocks[k] = blocks[k] - factor * pivot
    return jnp.concatenate(done, axis=0)[:, size:]


def output_kernel(scale, gram, loading, out):
    out[...] = exact_nn(inverse_factor(gram[...]), loading[...]) * scale


def output_call(gram, loading):
    return pl.pallas_call(
        functools.partial(output_kernel, math.sqrt(GENES)),
        in_specs=[VMEM, VMEM], out_specs=VMEM, out_shape=struct(loading.shape, f32),
        compiler_params=pltpu.CompilerParams(vmem_limit_bytes=16 * 2**20),
    )(gram, loading)


def mate(value, cells, mask, other=None):
    masks = (mask, mask if other is None else other)
    return lax.ppermute(value, "cell", [(i, i ^ masks[i % 2]) for i in range(cells)])


def legs(value, cells):
    return [mate(value, cells, 2, 4), mate(value, cells, 4, 2), mate(value, cells, 6)]


def total_over_cells(value, cells):
    value = (value + mate(value, cells, GROUP | 1)) + (mate(value, cells, GROUP) + mate(value, cells, 1))
    one, two, both = legs(value, cells)
    return (value + both) + (one + two)


def square_program(cells, expression, start_basis):
    width, rows = start_basis.shape[0], expression.shape[0]
    index = lax.axis_index("cell").astype(jnp.int32)
    masks = ((0, 0), (1, 1), (2, 4), (3, 5), (4, 2), (5, 3), (6, 6), (7, 7))
    members = index ^ jnp.where(index % 2 == 0, *jnp.array(masks, jnp.int32).T)
    packs = pack(expression, jnp.stack([members, members ^ GROUP], axis=1).reshape(-1), width)
    slots = [mate(x, cells, *pair) if k else x for k, (x, pair) in enumerate(zip(packs, masks))]

    def image_from(totals, normalised):
        even, odd = totals
        even = even + mate(odd, cells, 1)
        image = image_of(even, legs(even, cells), rows, normalised)
        return image, mate(image, cells, 1)

    def terms_and_received(images, cuts):
        sent = terms(slots, 1, images, cuts, bf16)
        own = terms(slots, 0, images, cuts, f32)
        return zip([mate(x, cells, GROUP) for x in sent], own)

    first = -(-6 * width // 1280) * 128
    basis = start_basis.T
    bases = {0: [basis], 1: [mate(basis, cells, GROUP)]}
    early = scores(slots, [(0, (0,))], {0: [basis]})
    images = image_from(scores(slots, [(0, (1,)), (1, (0, 1))], bases, early), False)
    for _ in range(1, ITERS):
        parts, copies, gram = [], [], []
        for received, own in terms_and_received(images, (first, width - first)):
            part, total = fold(received, own, gram, bf16, bool(parts))
            gram = [total]
            parts.append(part)
            copies.append(mate(part, cells, GROUP))
        early = scores(slots, [(0, (0,)), (1, (0,))], {0: parts})
        images = image_from(scores(slots, [(0, (1,)), (1, (1,))], {1: copies}, early, gram[0]), True)
    ((received, own),) = terms_and_received(images, (width,))
    loading, gram = fold(received, own, [], f32, False)
    return output_call(total_over_cells(gram, cells), loading).T


def plain_program(expression, start_basis):
    basis = start_basis
    for _ in range(ITERS):
        whole = lax.all_gather(basis, "cell", axis=0, tiled=True)
        partial = jnp.dot(expression, whole, preferred_element_type=f32)
        image = lax.psum(partial, "gene").astype(bf16)
        partial = lax.dot_general(expression, image, (((0,), (0,)), ((), ())), preferred_element_type=f32)
        loading = lax.psum_scatter(partial, "cell", scatter_dimension=0, tiled=True)
        gram = lax.dot_general(loading, loading, (((0,), (0,)), ((), ())), precision=HIGHEST, preferred_element_type=f32)
        lower = jnp.linalg.cholesky(lax.psum(gram, ("cell", "gene")))
        ortho = jax.scipy.linalg.solve_triangular(lower, loading.T, lower=True).T
        basis = ortho.astype(bf16)
    return ortho * math.sqrt(GENES)


def solution(mesh):
    cells, genes = mesh.shape["cell"], mesh.shape["gene"]

    def on_device(expression, start_basis):
        width, rank = start_basis.shape
        fits = genes == 1 and cells == 2 * GROUP and width % 128 == 0 and rank == 64
        if fits and expression.shape[0] % 16 == 0:
            return square_program(cells, expression, start_basis)
        return plain_program(expression, start_basis)

    return jax.shard_map(
        on_device,
        mesh=mesh,
        in_specs=(P(("groups", "cell"), "gene"), P(("groups", "gene", "cell"), None)),
        out_specs=P(("groups", "gene", "cell"), None),
        check_vma=False,
    )
```

```python
import functools
import math

import jax
import jax.numpy as jnp
from jax import lax
from jax.experimental import pallas as pl
from jax.experimental.pallas import tpu as pltpu
from jax.sharding import PartitionSpec as P

GENES = 30720
ITERS = 2
GROUP = 8
BIG = pltpu.CompilerParams(vmem_limit_bytes=16 * 2**20)
VMEM = pl.BlockSpec(memory_space=pltpu.VMEM)
HIGHEST = lax.Precision.HIGHEST
f32, bf16 = jnp.float32, jnp.bfloat16


def nn(a, b, precision=None):
    return lax.dot_general(a, b, (((1,), (0,)), ((), ())), precision=precision, preferred_element_type=f32)


def nt(a, b, precision=None):
    return lax.dot_general(a, b, (((1,), (1,)), ((), ())), precision=precision, preferred_element_type=f32)


def three(x):
    high = x.astype(bf16)
    rest = x - high.astype(f32)
    middle = rest.astype(bf16)
    return high, middle, (rest - middle.astype(f32)).astype(bf16)


def exact_nn(a, b):
    a1, a2, a3 = three(a)
    b1, b2, b3 = three(b)
    return nn(jnp.concatenate([a3, a2, a1, a2, a1, a1], axis=1), jnp.concatenate([b1, b2, b3, b1, b2, b1], axis=0))


def exact_gram(a):
    size = a.shape[0]
    parts = jnp.concatenate(three(a), axis=0)
    every = nt(parts, parts)

    def part(i, j):
        return every[i * size:(i + 1) * size, j * size:(j + 1) * size]

    small = (part(0, 2) + part(2, 0)) + part(1, 1)
    return part(0, 0) + ((part(0, 1) + part(1, 0)) + small)


def struct(shape, dtype):
    return jax.ShapeDtypeStruct(shape, dtype)


def cost(flops, bytes_accessed):
    return pl.CostEstimate(flops=flops, bytes_accessed=bytes_accessed, transcendentals=0)


def pack_kernel(masks, matrix, *refs):
    outs, sem = refs[:-1], refs[-1]
    width = outs[0].shape[1] // 2
    index = lax.axis_index("cell")
    copies = []
    for k, (out, pair) in enumerate(zip(outs, masks)):
        member = index ^ jnp.where(index % 2 == 0, *pair)
        for j, block in enumerate((member, member ^ GROUP)):
            start = pl.multiple_of(block * width, 128)
            copies.append(pltpu.make_async_copy(
                matrix.at[:, pl.ds(start, width)], out.at[:, pl.ds(j * width, width)], sem.at[2 * k + j]))
    for copy in copies:
        copy.start()
    for copy in copies:
        copy.wait()


def pack(matrix, masks, width):
    rows, count = matrix.shape[0], len(masks)
    return pl.pallas_call(
        functools.partial(pack_kernel, masks),
        in_specs=[pl.BlockSpec(memory_space=pltpu.HBM)],
        out_specs=[VMEM] * count,
        out_shape=[struct((rows, 2 * width), matrix.dtype)] * count,
        scratch_shapes=[pltpu.SemaphoreType.DMA((2 * count,))],
        compiler_params=BIG,
        cost_estimate=cost(0, 8 * rows * count * width),
    )(matrix)


def call(kernel, args, outs, estimate):
    return pl.pallas_call(
        kernel, in_specs=[VMEM] * len(args), out_specs=[VMEM] * len(outs), out_shape=outs,
        compiler_params=BIG, cost_estimate=estimate,
    )(*args)


def scores_kernel(work, counts, picked, with_gram, width, *refs):
    refs = list(refs)
    bases = {block: [refs.pop(0) for _ in range(count)] for block, count in counts}
    slots = {k: refs.pop(0) for k in picked}
    gram = refs.pop(0)[...] if with_gram else None
    before, outs = refs[:-2], refs[-2:]
    rank = gram.shape[0] if with_gram else 0
    for odd in range(2):
        left = 0
        for pair, blocks in work:
            value = 0.0
            for block in blocks:
                start = block * width
                for part in bases[block]:
                    stop = min(start + part.shape[1], (block + 1) * width)
                    big = [slots[4 * pair + odd][:, start:stop], slots[4 * pair + 2 + odd][:, start:stop]]
                    value = value + nt(jnp.concatenate(big, axis=0), part[:, :stop - start])
                    start = stop
            lanes = slice(left, left + 2 * next(iter(slots.values())).shape[0])
            left = lanes.stop
            if blocks:
                value = value.T
            if before and lanes.stop <= before[odd].shape[1]:
                value = value + before[odd][:, lanes]
            outs[odd][:, lanes] = value
        if with_gram:
            tail = bases[counts[-1][0]][-1]
            first = tail.shape[1] - 3 * rank
            theirs = [tail[:, first + i * rank:first + (i + 1) * rank].astype(f32) for i in range(3)]
            outs[odd][:, left:] = gram + ((theirs[0] + theirs[1]) + theirs[2])


def scores(slots, work, bases, before=(), gram=None):
    rank = next(iter(bases.values()))[0].shape[0]
    picked = [4 * pair + k for pair, blocks in work if blocks for k in range(4)]
    rows, width = slots[picked[0]].shape[0], slots[picked[0]].shape[1] // 2
    cells = 2 * rows * len(work) + (0 if gram is None else rank)
    counts = [(block, len(parts)) for block, parts in bases.items()]
    args = [x for parts in bases.values() for x in parts] + [slots[k] for k in picked]
    args += ([] if gram is None else [gram]) + list(before)
    size = 4 * rows * width * sum(len(blocks) for _, blocks in work)
    kernel = functools.partial(scores_kernel, work, counts, picked, gram is not None, width)
    return call(kernel, args, [struct((rank, cells), f32)] * 2, cost(2 * rank * size, 2 * size))


def image_kernel(normalised, *refs):
    values, out = [ref[...] for ref in refs[:-1]], refs[-1]
    cells = out.shape[1]
    size = cells // (GROUP // 2)

    def turned(x, mask):
        return jnp.concatenate([x[:, (j ^ mask) * size:((j ^ mask) + 1) * size] for j in range(GROUP // 2)], axis=1)

    value = (values[0][:, :cells] + turned(values[3], 3)) + (turned(values[1], 1) + turned(values[2], 2))
    if normalised:
        gram = [x[:, cells:] for x in values]
        value = exact_nn(inverse_factor((gram[0] + gram[3]) + (gram[1] + gram[2])), value)
    out[...] = value.astype(bf16)


def image_of(value, mates, rows, normalised):
    rank, cells = value.shape[0], rows * GROUP // 2
    return call(functools.partial(image_kernel, normalised), [value, *mates], [struct((rank, cells), bf16)],
                cost(12 * value.size * rank, 16 * value.size))[0]


def terms_kernel(block, width, *refs):
    slots, images, outs = refs[:GROUP], refs[GROUP:GROUP + 2], refs[GROUP + 2:]
    start = block * width
    for out in outs:
        step = out.shape[1] // 2 if out.shape[1] % 256 == 0 else out.shape[1]
        for left in range(0, out.shape[1], step):
            total = 0.0
            for odd in range(2):
                big = jnp.concatenate([ref[:, start:start + step] for ref in slots[odd::2]], axis=0)
                total = total + nn(images[odd][...], big)
            out[:, left:left + step] = total.astype(out.dtype)
            start += step


def terms(slots, block, images, cuts, dtype):
    rank, width = images[0].shape[0], slots[0].shape[1] // 2
    cells = slots[0].shape[0] * GROUP
    return call(functools.partial(terms_kernel, block, width), [*slots, *images], [struct((rank, w), dtype) for w in cuts],
                cost(2 * rank * cells * width, 2 * cells * width))


def fold_kernel(final, received, own, *refs):
    before, outs = refs[:-2], refs[-2:]
    width = own.shape[1]
    value = own[...] + received[...].astype(f32)
    outs[0][:, :width] = value.astype(outs[0].dtype)
    gram = exact_gram(value)
    for ref in before:
        gram = gram + ref[...]
    outs[1][...] = gram
    if final:
        for i, part in enumerate(three(gram)):
            outs[0][:, width + i * part.shape[1]:width + (i + 1) * part.shape[1]] = part


def fold(received, own, before, dtype, final):
    rank, width = own.shape
    return call(functools.partial(fold_kernel, final), [received, own, *before],
                [struct((rank, width + (3 * rank if final else 0)), dtype), struct((rank, rank), f32)],
                cost(12 * rank * own.size, 12 * own.size))


def inverse_factor(gram):
    size = gram.shape[0]
    row = lax.broadcasted_iota(jnp.int32, (size, size), 0)
    column = lax.broadcasted_iota(jnp.int32, (size, size), 1)
    both = jnp.concatenate([gram, jnp.where(row == column, 1.0, 0.0).astype(f32)], axis=1)
    panels = size // 8
    shape = (8, 2 * size)
    blocks = [both[8 * b:8 * b + 8] for b in range(panels)]
    inner = lax.broadcasted_iota(jnp.int32, shape, 0)
    done = []
    for b in range(panels):
        columns = [
            {k: jnp.broadcast_to(blocks[k][:, 8 * b + t:8 * b + t + 1], shape) for k in range(b, panels)}
            for t in range(8)
        ]
        for t in range(8):
            root = lax.rsqrt(jnp.broadcast_to(columns[t][b][t:t + 1], shape))
            scaled = {k: x * root for k, x in columns[t].items()}
            for s in range(t + 1, 8):
                along = jnp.broadcast_to(scaled[b][s:s + 1], shape)
                for k in range(b, panels):
                    columns[s][k] = columns[s][k] - scaled[k] * along
            pivot = jnp.broadcast_to(blocks[b][t:t + 1], shape) * root
            done.append(pivot[:1])
            for k in range(b, panels):
                factor = jnp.where(inner > t, scaled[k], 0.0) if k == b else scaled[k]
                blocks[k] = blocks[k] - factor * pivot
    return jnp.concatenate(done, axis=0)[:, size:]


def output_kernel(scale, gram, loading, out):
    out[...] = exact_nn(inverse_factor(gram[...]), loading[...]) * scale


def output_call(gram, loading):
    return pl.pallas_call(
        functools.partial(output_kernel, math.sqrt(GENES)),
        in_specs=[VMEM, VMEM], out_specs=VMEM, out_shape=struct(loading.shape, f32),
        compiler_params=pltpu.CompilerParams(vmem_limit_bytes=16 * 2**20),
    )(gram, loading)


def mate(value, cells, mask, other=None):
    masks = (mask, mask if other is None else other)
    return lax.ppermute(value, "cell", [(i, i ^ masks[i % 2]) for i in range(cells)])


def legs(value, cells):
    return [mate(value, cells, 2, 4), mate(value, cells, 4, 2), mate(value, cells, 6)]


def total_over_cells(value, cells):
    value = value + mate(value, cells, GROUP)
    value = value + mate(value, cells, 1)
    one, two, both = legs(value, cells)
    return (value + both) + (one + two)


def square_program(cells, expression, start_basis):
    width, rows = start_basis.shape[0], expression.shape[0]
    masks = ((0, 0), (1, 1), (2, 4), (3, 5), (4, 2), (5, 3), (6, 6), (7, 7))
    packs = pack(expression, masks, width)
    slots = [mate(x, cells, *pair) if k else x for k, (x, pair) in enumerate(zip(packs, masks))]

    def image_from(totals, normalised):
        even, odd = totals
        even = even + mate(odd, cells, 1)
        image = image_of(even, legs(even, cells), rows, normalised)
        return image, mate(image, cells, 1)

    def terms_and_received(images, cuts):
        sent = terms(slots, 1, images, cuts, bf16)
        own = terms(slots, 0, images, cuts, f32)
        return zip([mate(x, cells, GROUP) for x in sent], own)

    first = -(-6 * width // 1280) * 128
    basis = start_basis.T
    bases = {0: [basis], 1: [mate(basis, cells, GROUP)]}
    early = scores(slots, [(0, (0, 1))], bases)
    images = image_from(scores(slots, [(0, ()), (1, (0, 1))], bases, early), False)
    for _ in range(1, ITERS):
        parts, copies, gram = [], [], []
        for received, own in terms_and_received(images, (first, width - first)):
            part, total = fold(received, own, gram, bf16, bool(parts))
            gram = [total]
            parts.append(part)
            copies.append(mate(part, cells, GROUP))
        early = scores(slots, [(0, (0,)), (1, (0,))], {0: parts})
        images = image_from(scores(slots, [(0, (1,)), (1, (1,))], {1: copies}, early, gram[0]), True)
    ((received, own),) = terms_and_received(images, (width,))
    loading, gram = fold(received, own, [], f32, False)
    return output_call(total_over_cells(gram, cells), loading).T


def plain_program(expression, start_basis):
    basis = start_basis
    for _ in range(ITERS):
        whole = lax.all_gather(basis, "cell", axis=0, tiled=True)
        partial = jnp.dot(expression, whole, preferred_element_type=f32)
        image = lax.psum(partial, "gene").astype(bf16)
        partial = lax.dot_general(expression, image, (((0,), (0,)), ((), ())), preferred_element_type=f32)
        loading = lax.psum_scatter(partial, "cell", scatter_dimension=0, tiled=True)
        gram = lax.dot_general(loading, loading, (((0,), (0,)), ((), ())), precision=HIGHEST, preferred_element_type=f32)
        lower = jnp.linalg.cholesky(lax.psum(gram, ("cell", "gene")))
        ortho = jax.scipy.linalg.solve_triangular(lower, loading.T, lower=True).T
        basis = ortho.astype(bf16)
    return ortho * math.sqrt(GENES)


def solution(mesh):
    cells, genes = mesh.shape["cell"], mesh.shape["gene"]

    def on_device(expression, start_basis):
        width, rank = start_basis.shape
        fits = genes == 1 and cells == 2 * GROUP and width % 128 == 0 and rank == 64
        if fits and expression.shape[0] % 16 == 0:
            return square_program(cells, expression, start_basis)
        return plain_program(expression, start_basis)

    return jax.shard_map(
        on_device,
        mesh=mesh,
        in_specs=(P(("groups", "cell"), "gene"), P(("groups", "gene", "cell"), None)),
        out_specs=P(("groups", "gene", "cell"), None),
        check_vma=False,
    )
```

```python
import functools
import math

import jax
import jax.numpy as jnp
from jax import lax
from jax.experimental import pallas as pl
from jax.experimental.pallas import tpu as pltpu
from jax.sharding import PartitionSpec as P

GENES = 30720
ITERS = 2
GROUP = 8
BIG = pltpu.CompilerParams(vmem_limit_bytes=16 * 2**20)
VMEM = pl.BlockSpec(memory_space=pltpu.VMEM)
HIGHEST = lax.Precision.HIGHEST
f32, bf16 = jnp.float32, jnp.bfloat16


def nn(a, b, precision=None):
    return lax.dot_general(a, b, (((1,), (0,)), ((), ())), precision=precision, preferred_element_type=f32)


def nt(a, b, precision=None):
    return lax.dot_general(a, b, (((1,), (1,)), ((), ())), precision=precision, preferred_element_type=f32)


def three(x):
    high = x.astype(bf16)
    rest = x - high.astype(f32)
    middle = rest.astype(bf16)
    return high, middle, (rest - middle.astype(f32)).astype(bf16)


def exact_nn(a, b):
    a1, a2, a3 = three(a)
    b1, b2, b3 = three(b)
    return nn(jnp.concatenate([a3, a2, a1, a2, a1, a1], axis=1), jnp.concatenate([b1, b2, b3, b1, b2, b1], axis=0))


def exact_gram(a):
    size = a.shape[0]
    parts = jnp.concatenate(three(a), axis=0)
    every = nt(parts, parts)

    def part(i, j):
        return every[i * size:(i + 1) * size, j * size:(j + 1) * size]

    small = (part(0, 2) + part(2, 0)) + part(1, 1)
    return part(0, 0) + ((part(0, 1) + part(1, 0)) + small)


def struct(shape, dtype):
    return jax.ShapeDtypeStruct(shape, dtype)


def cost(flops, bytes_accessed):
    return pl.CostEstimate(flops=flops, bytes_accessed=bytes_accessed, transcendentals=0)


def pack_kernel(masks, matrix, *refs):
    outs, sem = refs[:-1], refs[-1]
    width = outs[0].shape[1] // 2
    index = lax.axis_index("cell")
    copies = []
    for k, (out, pair) in enumerate(zip(outs, masks)):
        member = index ^ jnp.where(index % 2 == 0, *pair)
        for j, block in enumerate((member, member ^ GROUP)):
            start = pl.multiple_of(block * width, 128)
            copies.append(pltpu.make_async_copy(
                matrix.at[:, pl.ds(start, width)], out.at[:, pl.ds(j * width, width)], sem.at[2 * k + j]))
    for copy in copies:
        copy.start()
    for copy in copies:
        copy.wait()


def pack(matrix, masks, width):
    rows, count = matrix.shape[0], len(masks)
    return pl.pallas_call(
        functools.partial(pack_kernel, masks),
        in_specs=[pl.BlockSpec(memory_space=pltpu.HBM)],
        out_specs=[VMEM] * count,
        out_shape=[struct((rows, 2 * width), matrix.dtype)] * count,
        scratch_shapes=[pltpu.SemaphoreType.DMA((2 * count,))],
        compiler_params=BIG,
        cost_estimate=cost(0, 8 * rows * count * width),
    )(matrix)


def call(kernel, args, outs, estimate):
    return pl.pallas_call(
        kernel, in_specs=[VMEM] * len(args), out_specs=[VMEM] * len(outs), out_shape=outs,
        compiler_params=BIG, cost_estimate=estimate,
    )(*args)


def scores_kernel(work, counts, picked, with_gram, width, *refs):
    refs = list(refs)
    bases = {block: [refs.pop(0) for _ in range(count)] for block, count in counts}
    slots = {k: refs.pop(0) for k in picked}
    gram = refs.pop(0)[...] if with_gram else None
    before, outs = refs[:-2], refs[-2:]
    rank = gram.shape[0] if with_gram else 0
    for odd in range(2):
        left = 0
        for pair, blocks in work:
            value = 0.0
            for block in blocks:
                start = block * width
                for part in bases[block]:
                    stop = min(start + part.shape[1], (block + 1) * width)
                    big = [slots[4 * pair + odd][:, start:stop], slots[4 * pair + 2 + odd][:, start:stop]]
                    value = value + nt(jnp.concatenate(big, axis=0), part[:, :stop - start])
                    start = stop
            lanes = slice(left, left + 2 * next(iter(slots.values())).shape[0])
            left = lanes.stop
            if blocks:
                value = value.T
            if before and lanes.stop <= before[odd].shape[1]:
                value = value + before[odd][:, lanes]
            outs[odd][:, lanes] = value
        if with_gram:
            tail = bases[counts[-1][0]][-1]
            first = tail.shape[1] - 3 * rank
            theirs = [tail[:, first + i * rank:first + (i + 1) * rank].astype(f32) for i in range(3)]
            outs[odd][:, left:] = gram + ((theirs[0] + theirs[1]) + theirs[2])


def scores(slots, work, bases, before=(), gram=None):
    rank = next(iter(bases.values()))[0].shape[0]
    picked = [4 * pair + k for pair, blocks in work if blocks for k in range(4)]
    rows, width = slots[picked[0]].shape[0], slots[picked[0]].shape[1] // 2
    cells = 2 * rows * len(work) + (0 if gram is None else rank)
    counts = [(block, len(parts)) for block, parts in bases.items()]
    args = [x for parts in bases.values() for x in parts] + [slots[k] for k in picked]
    args += ([] if gram is None else [gram]) + list(before)
    size = 4 * rows * width * sum(len(blocks) for _, blocks in work)
    kernel = functools.partial(scores_kernel, work, counts, picked, gram is not None, width)
    return call(kernel, args, [struct((rank, cells), f32)] * 2, cost(2 * rank * size, 2 * size))


def image_kernel(normalised, *refs):
    values, out = [ref[...] for ref in refs[:-1]], refs[-1]
    cells = out.shape[1]
    size = cells // (GROUP // 2)

    def turned(x, mask):
        return jnp.concatenate([x[:, (j ^ mask) * size:((j ^ mask) + 1) * size] for j in range(GROUP // 2)], axis=1)

    value = (values[0][:, :cells] + turned(values[3], 3)) + (turned(values[1], 1) + turned(values[2], 2))
    if normalised:
        gram = [x[:, cells:] for x in values]
        value = exact_nn(inverse_factor((gram[0] + gram[3]) + (gram[1] + gram[2])), value)
    out[...] = value.astype(bf16)


def image_of(value, mates, rows, normalised):
    rank, cells = value.shape[0], rows * GROUP // 2
    return call(functools.partial(image_kernel, normalised), [value, *mates], [struct((rank, cells), bf16)],
                cost(12 * value.size * rank, 16 * value.size))[0]


def terms_kernel(block, width, *refs):
    slots, images, outs = refs[:GROUP], refs[GROUP:GROUP + 2], refs[GROUP + 2:]
    start = block * width
    for out in outs:
        step = out.shape[1] // 2 if out.shape[1] % 256 == 0 else out.shape[1]
        for left in range(0, out.shape[1], step):
            total = 0.0
            for odd in range(2):
                big = jnp.concatenate([ref[:, start:start + step] for ref in slots[odd::2]], axis=0)
                total = total + nn(images[odd][...], big)
            out[:, left:left + step] = total.astype(out.dtype)
            start += step


def terms(slots, block, images, cuts, dtype):
    rank, width = images[0].shape[0], slots[0].shape[1] // 2
    cells = slots[0].shape[0] * GROUP
    return call(functools.partial(terms_kernel, block, width), [*slots, *images], [struct((rank, w), dtype) for w in cuts],
                cost(2 * rank * cells * width, 2 * cells * width))


def fold_kernel(final, received, own, *refs):
    before, outs = refs[:-2], refs[-2:]
    width = own.shape[1]
    value = own[...] + received[...].astype(f32)
    outs[0][:, :width] = value.astype(outs[0].dtype)
    gram = exact_gram(value)
    for ref in before:
        gram = gram + ref[...]
    outs[1][...] = gram
    if final:
        for i, part in enumerate(three(gram)):
            outs[0][:, width + i * part.shape[1]:width + (i + 1) * part.shape[1]] = part


def fold(received, own, before, dtype, final):
    rank, width = own.shape
    return call(functools.partial(fold_kernel, final), [received, own, *before],
                [struct((rank, width + (3 * rank if final else 0)), dtype), struct((rank, rank), f32)],
                cost(12 * rank * own.size, 12 * own.size))


def inverse_factor(gram):
    size = gram.shape[0]
    row = lax.broadcasted_iota(jnp.int32, (size, size), 0)
    column = lax.broadcasted_iota(jnp.int32, (size, size), 1)
    both = jnp.concatenate([gram, jnp.where(row == column, 1.0, 0.0).astype(f32)], axis=1)
    panels = size // 8
    shape = (8, 2 * size)
    blocks = [both[8 * b:8 * b + 8] for b in range(panels)]
    inner = lax.broadcasted_iota(jnp.int32, shape, 0)
    done = []
    for b in range(panels):
        columns = [
            {k: jnp.broadcast_to(blocks[k][:, 8 * b + t:8 * b + t + 1], shape) for k in range(b, panels)}
            for t in range(8)
        ]
        for t in range(8):
            root = lax.rsqrt(jnp.broadcast_to(columns[t][b][t:t + 1], shape))
            scaled = {k: x * root for k, x in columns[t].items()}
            for s in range(t + 1, 8):
                along = jnp.broadcast_to(scaled[b][s:s + 1], shape)
                for k in range(b, panels):
                    columns[s][k] = columns[s][k] - scaled[k] * along
            pivot = jnp.broadcast_to(blocks[b][t:t + 1], shape) * root
            done.append(pivot[:1])
            for k in range(b, panels):
                factor = jnp.where(inner > t, scaled[k], 0.0) if k == b else scaled[k]
                blocks[k] = blocks[k] - factor * pivot
    return jnp.concatenate(done, axis=0)[:, size:]


def output_kernel(scale, gram, loading, out):
    total = gram[0]
    for device in range(1, gram.shape[0]):
        total = total + gram[device]
    out[...] = exact_nn(inverse_factor(total), loading[...]) * scale


def output_call(gram, loading):
    return pl.pallas_call(
        functools.partial(output_kernel, math.sqrt(GENES)),
        in_specs=[VMEM, VMEM], out_specs=VMEM, out_shape=struct(loading.shape, f32),
        compiler_params=pltpu.CompilerParams(vmem_limit_bytes=16 * 2**20),
    )(gram, loading)


def mate(value, cells, mask, other=None):
    masks = (mask, mask if other is None else other)
    return lax.ppermute(value, "cell", [(i, i ^ masks[i % 2]) for i in range(cells)])


def legs(value, cells):
    return [mate(value, cells, 2, 4), mate(value, cells, 4, 2), mate(value, cells, 6)]


def square_program(cells, expression, start_basis):
    width, rows = start_basis.shape[0], expression.shape[0]
    masks = ((0, 0), (1, 1), (2, 4), (3, 5), (4, 2), (5, 3), (6, 6), (7, 7))
    packs = pack(expression, masks, width)
    slots = [mate(x, cells, *pair) if k else x for k, (x, pair) in enumerate(zip(packs[:7], masks))]
    leaving, slots[1] = lax.optimization_barrier((start_basis.T, slots[1]))
    basis_mate, *late = lax.optimization_barrier((mate(leaving, cells, GROUP), *packs[7:]))
    slots += [mate(x, cells, *pair) for x, pair in zip(late, masks[7:])]

    def image_from(totals, normalised):
        even, odd = totals
        even = even + mate(odd, cells, 1)
        image = image_of(even, legs(even, cells), rows, normalised)
        return image, mate(image, cells, 1)

    def terms_and_received(images, cuts):
        sent = terms(slots, 1, images, cuts, bf16)
        own = terms(slots, 0, images, cuts, f32)
        return zip([mate(x, cells, GROUP) for x in sent], own)

    first = -(-6 * width // 1280) * 128
    basis = start_basis.T
    bases = {0: [basis], 1: [basis_mate]}
    early = scores(slots, [(0, (0, 1))], bases)
    images = image_from(scores(slots, [(0, ()), (1, (0, 1))], bases, early), False)
    for _ in range(1, ITERS):
        parts, copies, gram = [], [], []
        for received, own in terms_and_received(images, (first, width - first)):
            part, total = fold(received, own, gram, bf16, bool(parts))
            gram = [total]
            parts.append(part)
            copies.append(mate(part, cells, GROUP))
        early = scores(slots, [(0, (0,)), (1, (0,))], {0: parts})
        images = image_from(scores(slots, [(0, (1,)), (1, (1,))], {1: copies}, early, gram[0]), True)
    ((received, own),) = terms_and_received(images, (width,))
    loading, gram = fold(received, own, [], f32, False)
    return output_call(lax.all_gather(gram, "cell"), loading).T


def plain_program(expression, start_basis):
    basis = start_basis
    for _ in range(ITERS):
        whole = lax.all_gather(basis, "cell", axis=0, tiled=True)
        partial = jnp.dot(expression, whole, preferred_element_type=f32)
        image = lax.psum(partial, "gene").astype(bf16)
        partial = lax.dot_general(expression, image, (((0,), (0,)), ((), ())), preferred_element_type=f32)
        loading = lax.psum_scatter(partial, "cell", scatter_dimension=0, tiled=True)
        gram = lax.dot_general(loading, loading, (((0,), (0,)), ((), ())), precision=HIGHEST, preferred_element_type=f32)
        lower = jnp.linalg.cholesky(lax.psum(gram, ("cell", "gene")))
        ortho = jax.scipy.linalg.solve_triangular(lower, loading.T, lower=True).T
        basis = ortho.astype(bf16)
    return ortho * math.sqrt(GENES)


def solution(mesh):
    cells, genes = mesh.shape["cell"], mesh.shape["gene"]

    def on_device(expression, start_basis):
        width, rank = start_basis.shape
        fits = genes == 1 and cells == 2 * GROUP and width % 128 == 0 and rank == 64
        if fits and expression.shape[0] % 16 == 0:
            return square_program(cells, expression, start_basis)
        return plain_program(expression, start_basis)

    return jax.shard_map(
        on_device,
        mesh=mesh,
        in_specs=(P(("groups", "cell"), "gene"), P(("groups", "gene", "cell"), None)),
        out_specs=P(("groups", "gene", "cell"), None),
        check_vma=False,
    )
```

```python
import functools
import math

import jax
import jax.numpy as jnp
from jax import lax
from jax.experimental import pallas as pl
from jax.experimental.pallas import tpu as pltpu
from jax.sharding import PartitionSpec as P

GENES = 30720
ITERS = 2
GROUP = 8
BIG = pltpu.CompilerParams(vmem_limit_bytes=16 * 2**20)
VMEM = pl.BlockSpec(memory_space=pltpu.VMEM)
HIGHEST = lax.Precision.HIGHEST
f32, bf16 = jnp.float32, jnp.bfloat16


def nn(a, b, precision=None):
    return lax.dot_general(a, b, (((1,), (0,)), ((), ())), precision=precision, preferred_element_type=f32)


def nt(a, b, precision=None):
    return lax.dot_general(a, b, (((1,), (1,)), ((), ())), precision=precision, preferred_element_type=f32)


def three(x):
    high = x.astype(bf16)
    rest = x - high.astype(f32)
    middle = rest.astype(bf16)
    return high, middle, (rest - middle.astype(f32)).astype(bf16)


def exact_nn(a, b):
    a1, a2, a3 = three(a)
    b1, b2, b3 = three(b)
    return nn(jnp.concatenate([a3, a2, a1, a2, a1, a1], axis=1), jnp.concatenate([b1, b2, b3, b1, b2, b1], axis=0))


def exact_gram(a):
    size = a.shape[0]
    parts = jnp.concatenate(three(a), axis=0)
    every = nt(parts, parts)

    def part(i, j):
        return every[i * size:(i + 1) * size, j * size:(j + 1) * size]

    small = (part(0, 2) + part(2, 0)) + part(1, 1)
    return part(0, 0) + ((part(0, 1) + part(1, 0)) + small)


def struct(shape, dtype):
    return jax.ShapeDtypeStruct(shape, dtype)


def cost(flops, bytes_accessed):
    return pl.CostEstimate(flops=flops, bytes_accessed=bytes_accessed, transcendentals=0)


def pack_kernel(masks, matrix, *refs):
    outs, sem = refs[:-1], refs[-1]
    width = outs[0].shape[1] // 2
    index = lax.axis_index("cell")
    copies = []
    for k, (out, pair) in enumerate(zip(outs, masks)):
        member = index ^ jnp.where(index % 2 == 0, *pair)
        for j, block in enumerate((member, member ^ GROUP)):
            start = pl.multiple_of(block * width, 128)
            copies.append(pltpu.make_async_copy(
                matrix.at[:, pl.ds(start, width)], out.at[:, pl.ds(j * width, width)], sem.at[2 * k + j]))
    for copy in copies:
        copy.start()
    for copy in copies:
        copy.wait()


def pack(matrix, masks, width):
    rows, count = matrix.shape[0], len(masks)
    return pl.pallas_call(
        functools.partial(pack_kernel, masks),
        in_specs=[pl.BlockSpec(memory_space=pltpu.HBM)],
        out_specs=[VMEM] * count,
        out_shape=[struct((rows, 2 * width), matrix.dtype)] * count,
        scratch_shapes=[pltpu.SemaphoreType.DMA((2 * count,))],
        compiler_params=BIG,
        cost_estimate=cost(0, 8 * rows * count * width),
    )(matrix)


def call(kernel, args, outs, estimate):
    return pl.pallas_call(
        kernel, in_specs=[VMEM] * len(args), out_specs=[VMEM] * len(outs), out_shape=outs,
        compiler_params=BIG, cost_estimate=estimate,
    )(*args)


def scores_kernel(work, counts, picked, with_gram, width, *refs):
    refs = list(refs)
    bases = {block: [refs.pop(0) for _ in range(count)] for block, count in counts}
    slots = {k: refs.pop(0) for k in picked}
    gram = refs.pop(0)[...] if with_gram else None
    before, outs = refs[:-2], refs[-2:]
    rank = gram.shape[0] if with_gram else 0
    for odd in range(2):
        left = 0
        for pair, blocks in work:
            value = 0.0
            for block in blocks:
                start = block * width
                for part in bases[block]:
                    stop = min(start + part.shape[1], (block + 1) * width)
                    big = [slots[4 * pair + odd][:, start:stop], slots[4 * pair + 2 + odd][:, start:stop]]
                    value = value + nt(jnp.concatenate(big, axis=0), part[:, :stop - start])
                    start = stop
            lanes = slice(left, left + 2 * next(iter(slots.values())).shape[0])
            left = lanes.stop
            if blocks:
                value = value.T
            if before and lanes.stop <= before[odd].shape[1]:
                value = value + before[odd][:, lanes]
            outs[odd][:, lanes] = value
        if with_gram:
            tail = bases[counts[-1][0]][-1]
            first = tail.shape[1] - 3 * rank
            theirs = [tail[:, first + i * rank:first + (i + 1) * rank].astype(f32) for i in range(3)]
            outs[odd][:, left:] = gram + ((theirs[0] + theirs[1]) + theirs[2])


def scores(slots, work, bases, before=(), gram=None):
    rank = next(iter(bases.values()))[0].shape[0]
    picked = [4 * pair + k for pair, blocks in work if blocks for k in range(4)]
    rows, width = slots[picked[0]].shape[0], slots[picked[0]].shape[1] // 2
    cells = 2 * rows * len(work) + (0 if gram is None else rank)
    counts = [(block, len(parts)) for block, parts in bases.items()]
    args = [x for parts in bases.values() for x in parts] + [slots[k] for k in picked]
    args += ([] if gram is None else [gram]) + list(before)
    size = 4 * rows * width * sum(len(blocks) for _, blocks in work)
    kernel = functools.partial(scores_kernel, work, counts, picked, gram is not None, width)
    return call(kernel, args, [struct((rank, cells), f32)] * 2, cost(2 * rank * size, 2 * size))


def image_kernel(normalised, *refs):
    values, out = [ref[...] for ref in refs[:-1]], refs[-1]
    cells = out.shape[1]
    size = cells // (GROUP // 2)

    def turned(x, mask):
        return jnp.concatenate([x[:, (j ^ mask) * size:((j ^ mask) + 1) * size] for j in range(GROUP // 2)], axis=1)

    value = (values[0][:, :cells] + turned(values[3], 3)) + (turned(values[1], 1) + turned(values[2], 2))
    if normalised:
        gram = [x[:, cells:] for x in values]
        value = exact_nn(inverse_factor((gram[0] + gram[3]) + (gram[1] + gram[2])), value)
    out[...] = value.astype(bf16)


def image_of(value, mates, rows, normalised):
    rank, cells = value.shape[0], rows * GROUP // 2
    return call(functools.partial(image_kernel, normalised), [value, *mates], [struct((rank, cells), bf16)],
                cost(12 * value.size * rank, 16 * value.size))[0]


def terms_kernel(block, width, *refs):
    slots, images, outs = refs[:GROUP], refs[GROUP:GROUP + 2], refs[GROUP + 2:]
    start = block * width
    for out in outs:
        step = out.shape[1] // 2 if out.shape[1] % 256 == 0 else out.shape[1]
        for left in range(0, out.shape[1], step):
            total = 0.0
            for odd in range(2):
                big = jnp.concatenate([ref[:, start:start + step] for ref in slots[odd::2]], axis=0)
                total = total + nn(images[odd][...], big)
            out[:, left:left + step] = total.astype(out.dtype)
            start += step


def terms(slots, block, images, cuts, dtype):
    rank, width = images[0].shape[0], slots[0].shape[1] // 2
    cells = slots[0].shape[0] * GROUP
    return call(functools.partial(terms_kernel, block, width), [*slots, *images], [struct((rank, w), dtype) for w in cuts],
                cost(2 * rank * cells * width, 2 * cells * width))


def fold_kernel(final, received, own, *refs):
    before, outs = refs[:-2], refs[-2:]
    width = own.shape[1]
    value = own[...] + received[...].astype(f32)
    outs[0][:, :width] = value.astype(outs[0].dtype)
    gram = exact_gram(value)
    for ref in before:
        gram = gram + ref[...]
    outs[1][...] = gram
    if final:
        for i, part in enumerate(three(gram)):
            outs[0][:, width + i * part.shape[1]:width + (i + 1) * part.shape[1]] = part


def fold(received, own, before, dtype, final):
    rank, width = own.shape
    return call(functools.partial(fold_kernel, final), [received, own, *before],
                [struct((rank, width + (3 * rank if final else 0)), dtype), struct((rank, rank), f32)],
                cost(12 * rank * own.size, 12 * own.size))


def inverse_factor(gram):
    size = gram.shape[0]
    row = lax.broadcasted_iota(jnp.int32, (size, size), 0)
    column = lax.broadcasted_iota(jnp.int32, (size, size), 1)
    both = jnp.concatenate([gram, jnp.where(row == column, 1.0, 0.0).astype(f32)], axis=1)
    panels = size // 8
    shape = (8, 2 * size)
    blocks = [both[8 * b:8 * b + 8] for b in range(panels)]
    inner = lax.broadcasted_iota(jnp.int32, shape, 0)
    done = []
    for b in range(panels):
        columns = [
            {k: jnp.broadcast_to(blocks[k][:, 8 * b + t:8 * b + t + 1], shape) for k in range(b, panels)}
            for t in range(8)
        ]
        for t in range(8):
            root = lax.rsqrt(jnp.broadcast_to(columns[t][b][t:t + 1], shape))
            scaled = {k: x * root for k, x in columns[t].items()}
            for s in range(t + 1, 8):
                along = jnp.broadcast_to(scaled[b][s:s + 1], shape)
                for k in range(b, panels):
                    columns[s][k] = columns[s][k] - scaled[k] * along
            pivot = jnp.broadcast_to(blocks[b][t:t + 1], shape) * root
            done.append(pivot[:1])
            for k in range(b, panels):
                factor = jnp.where(inner > t, scaled[k], 0.0) if k == b else scaled[k]
                blocks[k] = blocks[k] - factor * pivot
    return jnp.concatenate(done, axis=0)[:, size:]


def sum_of(stack):
    return (stack[0] + stack[1]) + (stack[2] + stack[3])


def sum_kernel(stack, out):
    out[...] = sum_of(stack)


def sum_call(stack):
    return call(sum_kernel, [stack], [struct(stack.shape[1:], f32)], cost(stack.size, 4 * stack.size))[0]


def output_kernel(scale, gram, loading, out):
    out[...] = exact_nn(inverse_factor(sum_of(gram)), loading[...]) * scale


def output_call(gram, loading):
    return pl.pallas_call(
        functools.partial(output_kernel, math.sqrt(GENES)),
        in_specs=[VMEM, VMEM], out_specs=VMEM, out_shape=struct(loading.shape, f32),
        compiler_params=pltpu.CompilerParams(vmem_limit_bytes=16 * 2**20),
    )(gram, loading)


def mate(value, cells, mask, other=None):
    masks = (mask, mask if other is None else other)
    return lax.ppermute(value, "cell", [(i, i ^ masks[i % 2]) for i in range(cells)])


def legs(value, cells):
    return [mate(value, cells, 2, 4), mate(value, cells, 4, 2), mate(value, cells, 6)]


def gathered(value, cells, low, high):
    groups = [[base, base ^ low, base ^ high, base ^ low ^ high] for base in range(cells) if not base & (low | high)]
    return lax.all_gather(value, "cell", axis_index_groups=groups)


def square_program(cells, expression, start_basis):
    width, rows = start_basis.shape[0], expression.shape[0]
    masks = ((0, 0), (1, 1), (2, 4), (3, 5), (4, 2), (5, 3), (6, 6), (7, 7))
    packs = pack(expression, masks, width)
    slots = [mate(x, cells, *pair) if k else x for k, (x, pair) in enumerate(zip(packs, masks))]

    def image_from(totals, normalised):
        even, odd = totals
        even = even + mate(odd, cells, 1)
        image = image_of(even, legs(even, cells), rows, normalised)
        return image, mate(image, cells, 1)

    def terms_and_received(images, cuts):
        sent = terms(slots, 1, images, cuts, bf16)
        own = terms(slots, 0, images, cuts, f32)
        return zip([mate(x, cells, GROUP) for x in sent], own)

    first = -(-6 * width // 1280) * 128
    basis = start_basis.T
    bases = {0: [basis], 1: [mate(basis, cells, GROUP)]}
    early = scores(slots, [(0, (0, 1))], bases)
    images = image_from(scores(slots, [(0, ()), (1, (0, 1))], bases, early), False)
    for _ in range(1, ITERS):
        parts, copies, gram = [], [], []
        for received, own in terms_and_received(images, (first, width - first)):
            part, total = fold(received, own, gram, bf16, bool(parts))
            gram = [total]
            parts.append(part)
            copies.append(mate(part, cells, GROUP))
        early = scores(slots, [(0, (0,)), (1, (0,))], {0: parts})
        images = image_from(scores(slots, [(0, (1,)), (1, (1,))], {1: copies}, early, gram[0]), True)
    ((received, own),) = terms_and_received(images, (width,))
    loading, gram = fold(received, own, [], f32, False)
    gram = sum_call(gathered(gram, cells, GROUP, 1))
    return output_call(gathered(gram, cells, 2, 4), loading).T


def plain_program(expression, start_basis):
    basis = start_basis
    for _ in range(ITERS):
        whole = lax.all_gather(basis, "cell", axis=0, tiled=True)
        partial = jnp.dot(expression, whole, preferred_element_type=f32)
        image = lax.psum(partial, "gene").astype(bf16)
        partial = lax.dot_general(expression, image, (((0,), (0,)), ((), ())), preferred_element_type=f32)
        loading = lax.psum_scatter(partial, "cell", scatter_dimension=0, tiled=True)
        gram = lax.dot_general(loading, loading, (((0,), (0,)), ((), ())), precision=HIGHEST, preferred_element_type=f32)
        lower = jnp.linalg.cholesky(lax.psum(gram, ("cell", "gene")))
        ortho = jax.scipy.linalg.solve_triangular(lower, loading.T, lower=True).T
        basis = ortho.astype(bf16)
    return ortho * math.sqrt(GENES)


def solution(mesh):
    cells, genes = mesh.shape["cell"], mesh.shape["gene"]

    def on_device(expression, start_basis):
        width, rank = start_basis.shape
        fits = genes == 1 and cells == 2 * GROUP and width % 128 == 0 and rank == 64
        if fits and expression.shape[0] % 16 == 0:
            return square_program(cells, expression, start_basis)
        return plain_program(expression, start_basis)

    return jax.shard_map(
        on_device,
        mesh=mesh,
        in_specs=(P(("groups", "cell"), "gene"), P(("groups", "gene", "cell"), None)),
        out_specs=P(("groups", "gene", "cell"), None),
        check_vma=False,
    )
```

```python
import functools
import math

import jax
import jax.numpy as jnp
from jax import lax
from jax.experimental import pallas as pl
from jax.experimental.pallas import tpu as pltpu
from jax.sharding import PartitionSpec as P

GENES = 30720
ITERS = 2
GROUP = 8
BIG = pltpu.CompilerParams(vmem_limit_bytes=16 * 2**20)
VMEM = pl.BlockSpec(memory_space=pltpu.VMEM)
HIGHEST = lax.Precision.HIGHEST
f32, bf16 = jnp.float32, jnp.bfloat16


def nn(a, b, precision=None):
    return lax.dot_general(a, b, (((1,), (0,)), ((), ())), precision=precision, preferred_element_type=f32)


def nt(a, b, precision=None):
    return lax.dot_general(a, b, (((1,), (1,)), ((), ())), precision=precision, preferred_element_type=f32)


def three(x):
    high = x.astype(bf16)
    rest = x - high.astype(f32)
    middle = rest.astype(bf16)
    return high, middle, (rest - middle.astype(f32)).astype(bf16)


def exact_nn(a, b):
    a1, a2, a3 = three(a)
    b1, b2, b3 = three(b)
    return nn(jnp.concatenate([a3, a2, a1, a2, a1, a1], axis=1), jnp.concatenate([b1, b2, b3, b1, b2, b1], axis=0))


def exact_gram(a):
    size = a.shape[0]
    parts = jnp.concatenate(three(a), axis=0)
    every = nt(parts, parts)

    def part(i, j):
        return every[i * size:(i + 1) * size, j * size:(j + 1) * size]

    small = (part(0, 2) + part(2, 0)) + part(1, 1)
    return part(0, 0) + ((part(0, 1) + part(1, 0)) + small)


def struct(shape, dtype):
    return jax.ShapeDtypeStruct(shape, dtype)


def cost(flops, bytes_accessed):
    return pl.CostEstimate(flops=flops, bytes_accessed=bytes_accessed, transcendentals=0)


def pack_kernel(masks, matrix, *refs):
    outs, sem = refs[:-1], refs[-1]
    width = outs[0].shape[1] // 2
    index = lax.axis_index("cell")
    copies = []
    for k, (out, pair) in enumerate(zip(outs, masks)):
        member = index ^ jnp.where(index % 2 == 0, *pair)
        for j, block in enumerate((member, member ^ GROUP)):
            start = pl.multiple_of(block * width, 128)
            copies.append(pltpu.make_async_copy(
                matrix.at[:, pl.ds(start, width)], out.at[:, pl.ds(j * width, width)], sem.at[2 * k + j]))
    for copy in copies:
        copy.start()
    for copy in copies:
        copy.wait()


def pack(matrix, masks, width):
    rows, count = matrix.shape[0], len(masks)
    return pl.pallas_call(
        functools.partial(pack_kernel, masks),
        in_specs=[pl.BlockSpec(memory_space=pltpu.HBM)],
        out_specs=[VMEM] * count,
        out_shape=[struct((rows, 2 * width), matrix.dtype)] * count,
        scratch_shapes=[pltpu.SemaphoreType.DMA((2 * count,))],
        compiler_params=BIG,
        cost_estimate=cost(0, 8 * rows * count * width),
    )(matrix)


def call(kernel, args, outs, estimate):
    return pl.pallas_call(
        kernel, in_specs=[VMEM] * len(args), out_specs=[VMEM] * len(outs), out_shape=outs,
        compiler_params=BIG, cost_estimate=estimate,
    )(*args)


def scores_kernel(work, counts, picked, with_gram, width, offset, *refs):
    refs = list(refs)
    bases = {block: [refs.pop(0) for _ in range(count)] for block, count in counts}
    slots = {k: refs.pop(0) for k in picked}
    gram = refs.pop(0)[...] if with_gram else None
    before, outs = refs[:-2], refs[-2:]
    for odd in range(2):
        left = 0
        for pair, blocks in work:
            value = 0.0
            for block in blocks:
                start = block * width + offset
                for part in bases[block]:
                    stop = start + part.shape[1]
                    big = [slots[4 * pair + odd][:, start:stop], slots[4 * pair + 2 + odd][:, start:stop]]
                    value = value + nt(jnp.concatenate(big, axis=0), part[...])
                    start = stop
            lanes = slice(left, left + 2 * next(iter(slots.values())).shape[0])
            left = lanes.stop
            if blocks:
                value = value.T
            if before and lanes.stop <= before[odd].shape[1]:
                value = value + before[odd][:, lanes]
            outs[odd][:, lanes] = value
        if with_gram:
            outs[odd][:, left:] = gram


def scores(slots, work, bases, before=(), gram=None, offset=0):
    rank = next(iter(bases.values()))[0].shape[0]
    picked = [4 * pair + k for pair, blocks in work if blocks for k in range(4)]
    rows, width = slots[picked[0]].shape[0], slots[picked[0]].shape[1] // 2
    cells = 2 * rows * len(work) + (0 if gram is None else rank)
    counts = [(block, len(parts)) for block, parts in bases.items()]
    args = [x for parts in bases.values() for x in parts] + [slots[k] for k in picked]
    args += ([] if gram is None else [gram]) + list(before)
    size = 4 * rows * width * sum(len(blocks) for _, blocks in work)
    kernel = functools.partial(scores_kernel, work, counts, picked, gram is not None, width, offset)
    return call(kernel, args, [struct((rank, cells), f32)] * 2, cost(2 * rank * size, 2 * size))


def image_kernel(normalised, *refs):
    values, out = [ref[...] for ref in refs[:-1]], refs[-1]
    cells = out.shape[1]
    size = cells // (GROUP // 2)

    def turned(x, mask):
        return jnp.concatenate([x[:, (j ^ mask) * size:((j ^ mask) + 1) * size] for j in range(GROUP // 2)], axis=1)

    value = (values[0][:, :cells] + turned(values[3], 3)) + (turned(values[1], 1) + turned(values[2], 2))
    if normalised:
        gram = [x[:, cells:] for x in values]
        value = exact_nn(inverse_factor((gram[0] + gram[3]) + (gram[1] + gram[2])), value)
    out[...] = value.astype(bf16)


def image_of(value, mates, rows, normalised):
    rank, cells = value.shape[0], rows * GROUP // 2
    return call(functools.partial(image_kernel, normalised), [value, *mates], [struct((rank, cells), bf16)],
                cost(12 * value.size * rank, 16 * value.size))[0]


def terms_kernel(starts, *refs):
    slots, images, out = refs[:GROUP], refs[GROUP:GROUP + 2], refs[-1]
    width = out.shape[1]
    rank = out.shape[0] // len(starts)
    step = width // 2 if width % 256 == 0 else width
    for part, start in enumerate(starts):
        for left in range(0, width, step):
            total = 0.0
            for odd in range(2):
                big = jnp.concatenate([ref[:, start + left:start + left + step] for ref in slots[odd::2]], axis=0)
                total = total + nn(images[odd][...], big)
            out[part * rank:(part + 1) * rank, left:left + step] = total.astype(out.dtype)


def terms(slots, starts, width, images, dtype):
    rank, cells = images[0].shape[0], slots[0].shape[0] * GROUP
    size = cells * width * len(starts)
    return call(functools.partial(terms_kernel, starts), [*slots, *images],
                [struct((rank * len(starts), width), dtype)], cost(2 * rank * size, 2 * size))[0]


def both_kernel(sent, received, *refs):
    before, rows, gram = refs[:-3], refs[-3:-1], refs[-1]
    rank = rows[0].shape[0]
    grams = []
    for block in range(2):
        mine, theirs = slice(block * rank, (block + 1) * rank), slice((1 - block) * rank, (2 - block) * rank)
        value = sent[mine].astype(f32) + received[theirs].astype(f32)
        rows[block][...] = value.astype(bf16)
        grams.append(exact_gram(value))
    total = grams[0] + grams[1]
    for ref in before:
        total = total + ref[...]
    gram[...] = total


def both(sent, received, before):
    rank, width = sent.shape[0] // 2, sent.shape[1]
    return call(both_kernel, [sent, received, *before], [struct((rank, width), bf16)] * 2 + [struct((rank, rank), f32)],
                cost(24 * rank * rank * width, 24 * rank * width))


def loading_kernel(received, own, loading, gram):
    value = own[...] + received[...].astype(f32)
    loading[...] = value
    gram[...] = exact_gram(value)


def loading_and_gram(received, own):
    rank, width = own.shape
    return call(loading_kernel, [received, own], [struct((rank, width), f32), struct((rank, rank), f32)],
                cost(12 * rank * rank * width, 12 * rank * width))


def inverse_factor(gram):
    size = gram.shape[0]
    row = lax.broadcasted_iota(jnp.int32, (size, size), 0)
    column = lax.broadcasted_iota(jnp.int32, (size, size), 1)
    both = jnp.concatenate([gram, jnp.where(row == column, 1.0, 0.0).astype(f32)], axis=1)
    panels = size // 8
    shape = (8, 2 * size)
    blocks = [both[8 * b:8 * b + 8] for b in range(panels)]
    inner = lax.broadcasted_iota(jnp.int32, shape, 0)
    done = []
    for b in range(panels):
        columns = [
            {k: jnp.broadcast_to(blocks[k][:, 8 * b + t:8 * b + t + 1], shape) for k in range(b, panels)}
            for t in range(8)
        ]
        for t in range(8):
            root = lax.rsqrt(jnp.broadcast_to(columns[t][b][t:t + 1], shape))
            scaled = {k: x * root for k, x in columns[t].items()}
            for s in range(t + 1, 8):
                along = jnp.broadcast_to(scaled[b][s:s + 1], shape)
                for k in range(b, panels):
                    columns[s][k] = columns[s][k] - scaled[k] * along
            pivot = jnp.broadcast_to(blocks[b][t:t + 1], shape) * root
            done.append(pivot[:1])
            for k in range(b, panels):
                factor = jnp.where(inner > t, scaled[k], 0.0) if k == b else scaled[k]
                blocks[k] = blocks[k] - factor * pivot
    return jnp.concatenate(done, axis=0)[:, size:]


def output_kernel(scale, gram, loading, out):
    out[...] = exact_nn(inverse_factor(gram[...]), loading[...]) * scale


def output_call(gram, loading):
    return pl.pallas_call(
        functools.partial(output_kernel, math.sqrt(GENES)),
        in_specs=[VMEM, VMEM], out_specs=VMEM, out_shape=struct(loading.shape, f32),
        compiler_params=pltpu.CompilerParams(vmem_limit_bytes=16 * 2**20),
    )(gram, loading)


def mate(value, cells, mask, other=None):
    masks = (mask, mask if other is None else other)
    return lax.ppermute(value, "cell", [(i, i ^ masks[i % 2]) for i in range(cells)])


def legs(value, cells):
    return [mate(value, cells, 2, 4), mate(value, cells, 4, 2), mate(value, cells, 6)]


def total_over_cells(value, cells):
    value = (value + mate(value, cells, GROUP | 1)) + (mate(value, cells, GROUP) + mate(value, cells, 1))
    one, two, both_ways = legs(value, cells)
    return (value + both_ways) + (one + two)


def square_program(cells, expression, start_basis):
    width, rows = start_basis.shape[0], expression.shape[0]
    masks = ((0, 0), (1, 1), (2, 4), (3, 5), (4, 2), (5, 3), (6, 6), (7, 7))
    packs = pack(expression, masks, width)
    slots = [mate(x, cells, *pair) if k else x for k, (x, pair) in enumerate(zip(packs, masks))]

    def image_from(totals, normalised):
        even, odd = totals
        even = even + mate(odd, cells, 1)
        image = image_of(even, legs(even, cells), rows, normalised)
        return image, mate(image, cells, 1)

    first = -(-6 * width // 1280) * 128
    basis = start_basis.T
    bases = {0: [basis], 1: [mate(basis, cells, GROUP)]}
    early = scores(slots, [(0, (0, 1))], bases)
    images = image_from(scores(slots, [(0, ()), (1, (0, 1))], bases, early), False)
    for _ in range(1, ITERS):
        totals, gram = (), []
        for start, stop in ((0, first), (first, width)):
            sent = terms(slots, (start, width + start), stop - start, images, bf16)
            own, other, total = both(sent, mate(sent, cells, GROUP), gram)
            gram = [total]
            totals = scores(slots, [(0, (0, 1)), (1, (0, 1))], {0: [own], 1: [other]}, totals,
                            total if stop == width else None, start)
        images = image_from(totals, True)
    received = mate(terms(slots, (width,), width, images, bf16), cells, GROUP)
    loading, gram = loading_and_gram(received, terms(slots, (0,), width, images, f32))
    return output_call(total_over_cells(gram, cells), loading).T


def plain_program(expression, start_basis):
    basis = start_basis
    for _ in range(ITERS):
        whole = lax.all_gather(basis, "cell", axis=0, tiled=True)
        partial = jnp.dot(expression, whole, preferred_element_type=f32)
        image = lax.psum(partial, "gene").astype(bf16)
        partial = lax.dot_general(expression, image, (((0,), (0,)), ((), ())), preferred_element_type=f32)
        loading = lax.psum_scatter(partial, "cell", scatter_dimension=0, tiled=True)
        gram = lax.dot_general(loading, loading, (((0,), (0,)), ((), ())), precision=HIGHEST, preferred_element_type=f32)
        lower = jnp.linalg.cholesky(lax.psum(gram, ("cell", "gene")))
        ortho = jax.scipy.linalg.solve_triangular(lower, loading.T, lower=True).T
        basis = ortho.astype(bf16)
    return ortho * math.sqrt(GENES)


def solution(mesh):
    cells, genes = mesh.shape["cell"], mesh.shape["gene"]

    def on_device(expression, start_basis):
        width, rank = start_basis.shape
        fits = genes == 1 and cells == 2 * GROUP and width % 128 == 0 and rank == 64
        if fits and expression.shape[0] % 16 == 0:
            return square_program(cells, expression, start_basis)
        return plain_program(expression, start_basis)

    return jax.shard_map(
        on_device,
        mesh=mesh,
        in_specs=(P(("groups", "cell"), "gene"), P(("groups", "gene", "cell"), None)),
        out_specs=P(("groups", "gene", "cell"), None),
        check_vma=False,
    )
```

```python
import functools
import math

import jax
import jax.numpy as jnp
from jax import lax
from jax.experimental import pallas as pl
from jax.experimental.pallas import tpu as pltpu
from jax.sharding import PartitionSpec as P

GENES = 30720
ITERS = 2
GROUP = 8
BIG = pltpu.CompilerParams(vmem_limit_bytes=16 * 2**20)
VMEM = pl.BlockSpec(memory_space=pltpu.VMEM)
HIGHEST = lax.Precision.HIGHEST
f32, bf16 = jnp.float32, jnp.bfloat16


def nn(a, b, precision=None):
    return lax.dot_general(a, b, (((1,), (0,)), ((), ())), precision=precision, preferred_element_type=f32)


def nt(a, b, precision=None):
    return lax.dot_general(a, b, (((1,), (1,)), ((), ())), precision=precision, preferred_element_type=f32)


def three(x):
    high = x.astype(bf16)
    rest = x - high.astype(f32)
    middle = rest.astype(bf16)
    return high, middle, (rest - middle.astype(f32)).astype(bf16)


def exact_nn(a, b):
    a1, a2, a3 = three(a)
    b1, b2, b3 = three(b)
    return nn(jnp.concatenate([a3, a2, a1, a2, a1, a1], axis=1), jnp.concatenate([b1, b2, b3, b1, b2, b1], axis=0))


def exact_gram(a):
    size = a.shape[0]
    parts = jnp.concatenate(three(a), axis=0)
    every = nt(parts, parts)

    def part(i, j):
        return every[i * size:(i + 1) * size, j * size:(j + 1) * size]

    small = (part(0, 2) + part(2, 0)) + part(1, 1)
    return part(0, 0) + ((part(0, 1) + part(1, 0)) + small)


def struct(shape, dtype):
    return jax.ShapeDtypeStruct(shape, dtype)


def cost(flops, bytes_accessed):
    return pl.CostEstimate(flops=flops, bytes_accessed=bytes_accessed, transcendentals=0)


def pack_kernel(masks, matrix, *refs):
    outs, held, sem = refs[:-2], refs[-2], refs[-1]
    rows, width = matrix.shape[0], outs[0].shape[1] // 2
    step = 16 if rows % 16 == 0 else rows
    index = lax.axis_index("cell")
    copies = [pltpu.make_async_copy(matrix.at[pl.ds(low, step)], held.at[pl.ds(low, step)], sem.at[i])
              for i, low in enumerate(range(0, rows, step))]
    for copy in copies:
        copy.start()
    for i, copy in enumerate(copies):
        copy.wait()
        some = pl.ds(i * step, step)
        for out, pair in zip(outs, masks):
            member = index ^ jnp.where(index % 2 == 0, *pair)
            for j, block in enumerate((member, member ^ GROUP)):
                start = pl.multiple_of(block * width, 128)
                out[some, pl.ds(j * width, width)] = held[some, pl.ds(start, width)]


def pack(matrix, masks, width):
    rows, count = matrix.shape[0], len(masks)
    return pl.pallas_call(
        functools.partial(pack_kernel, masks),
        in_specs=[pl.BlockSpec(memory_space=pltpu.HBM)],
        out_specs=[VMEM] * count,
        out_shape=[struct((rows, 2 * width), matrix.dtype)] * count,
        scratch_shapes=[pltpu.VMEM(matrix.shape, matrix.dtype), pltpu.SemaphoreType.DMA((rows // 16 if rows % 16 == 0 else 1,))],
        compiler_params=pltpu.CompilerParams(vmem_limit_bytes=48 * 2**20),
        cost_estimate=cost(0, 8 * rows * count * width),
    )(matrix)


def call(kernel, args, outs, estimate):
    return pl.pallas_call(
        kernel, in_specs=[VMEM] * len(args), out_specs=[VMEM] * len(outs), out_shape=outs,
        compiler_params=BIG, cost_estimate=estimate,
    )(*args)


def scores_kernel(work, odds, counts, picked, with_gram, width, offset, *refs):
    refs = list(refs)
    bases = {block: [refs.pop(0) for _ in range(count)] for block, count in counts}
    slots = {k: refs.pop(0) for k in picked}
    gram = refs.pop(0)[...] if with_gram else None
    before, outs = refs[:-len(odds)], refs[-len(odds):]
    for i, odd in enumerate(odds):
        left = 0
        for pair, blocks in work:
            value = 0.0
            for block in blocks:
                start = block * width + offset
                for part in bases[block]:
                    stop = start + part.shape[1]
                    big = [slots[4 * pair + odd][:, start:stop], slots[4 * pair + 2 + odd][:, start:stop]]
                    value = value + nt(jnp.concatenate(big, axis=0), part[...])
                    start = stop
            lanes = slice(left, left + 2 * next(iter(slots.values())).shape[0])
            left = lanes.stop
            if blocks:
                value = value.T
            if before and lanes.stop <= before[i].shape[1]:
                value = value + before[i][:, lanes]
            outs[i][:, lanes] = value
        if with_gram:
            outs[i][:, left:] = gram


def scores(slots, work, bases, before=(), gram=None, offset=0, odds=(0, 1)):
    rank = next(iter(bases.values()))[0].shape[0]
    picked = [4 * pair + 2 * k + odd for pair, blocks in work if blocks for k in range(2) for odd in odds]
    rows, width = slots[picked[0]].shape[0], slots[picked[0]].shape[1] // 2
    cells = 2 * rows * len(work) + (0 if gram is None else rank)
    counts = [(block, len(parts)) for block, parts in bases.items()]
    args = [x for parts in bases.values() for x in parts] + [slots[k] for k in picked]
    args += ([] if gram is None else [gram]) + list(before)
    size = 2 * len(odds) * rows * width * sum(len(blocks) for _, blocks in work)
    kernel = functools.partial(scores_kernel, work, odds, counts, picked, gram is not None, width, offset)
    return call(kernel, args, [struct((rank, cells), f32)] * len(odds), cost(2 * rank * size, 2 * size))


def image_kernel(normalised, *refs):
    values, out = [ref[...] for ref in refs[:-1]], refs[-1]
    cells = out.shape[1]
    size = cells // (GROUP // 2)

    def turned(x, mask):
        return jnp.concatenate([x[:, (j ^ mask) * size:((j ^ mask) + 1) * size] for j in range(GROUP // 2)], axis=1)

    value = (values[0][:, :cells] + turned(values[3], 3)) + (turned(values[1], 1) + turned(values[2], 2))
    if normalised:
        gram = [x[:, cells:] for x in values]
        value = exact_nn(inverse_factor((gram[0] + gram[3]) + (gram[1] + gram[2])), value)
    out[...] = value.astype(bf16)


def image_of(value, mates, rows, normalised):
    rank, cells = value.shape[0], rows * GROUP // 2
    return call(functools.partial(image_kernel, normalised), [value, *mates], [struct((rank, cells), bf16)],
                cost(12 * value.size * rank, 16 * value.size))[0]


def terms_kernel(starts, *refs):
    slots, images, out = refs[:GROUP], refs[GROUP:GROUP + 2], refs[-1]
    width = out.shape[1]
    rank = out.shape[0] // len(starts)
    step = width // 2 if width % 256 == 0 else width
    for part, start in enumerate(starts):
        for left in range(0, width, step):
            total = 0.0
            for odd in range(2):
                big = jnp.concatenate([ref[:, start + left:start + left + step] for ref in slots[odd::2]], axis=0)
                total = total + nn(images[odd][...], big)
            out[part * rank:(part + 1) * rank, left:left + step] = total.astype(out.dtype)


def terms(slots, starts, width, images, dtype):
    rank, cells = images[0].shape[0], slots[0].shape[0] * GROUP
    size = cells * width * len(starts)
    return call(functools.partial(terms_kernel, starts), [*slots, *images],
                [struct((rank * len(starts), width), dtype)], cost(2 * rank * size, 2 * size))[0]


def both_kernel(sent, received, *refs):
    before, rows, gram = refs[:-3], refs[-3:-1], refs[-1]
    rank = rows[0].shape[0]
    grams = []
    for block in range(2):
        mine, theirs = slice(block * rank, (block + 1) * rank), slice((1 - block) * rank, (2 - block) * rank)
        value = sent[mine].astype(f32) + received[theirs].astype(f32)
        rows[block][...] = value.astype(bf16)
        grams.append(exact_gram(value))
    total = grams[0] + grams[1]
    for ref in before:
        total = total + ref[...]
    gram[...] = total


def both(sent, received, before):
    rank, width = sent.shape[0] // 2, sent.shape[1]
    return call(both_kernel, [sent, received, *before], [struct((rank, width), bf16)] * 2 + [struct((rank, rank), f32)],
                cost(24 * rank * rank * width, 24 * rank * width))


def loading_kernel(received, own, loading, gram):
    value = own[...] + received[...].astype(f32)
    loading[...] = value
    gram[...] = exact_gram(value)


def loading_and_gram(received, own):
    rank, width = own.shape
    return call(loading_kernel, [received, own], [struct((rank, width), f32), struct((rank, rank), f32)],
                cost(12 * rank * rank * width, 12 * rank * width))


def inverse_factor(gram):
    size = gram.shape[0]
    row = lax.broadcasted_iota(jnp.int32, (size, size), 0)
    column = lax.broadcasted_iota(jnp.int32, (size, size), 1)
    both = jnp.concatenate([gram, jnp.where(row == column, 1.0, 0.0).astype(f32)], axis=1)
    panels = size // 8
    shape = (8, 2 * size)
    blocks = [both[8 * b:8 * b + 8] for b in range(panels)]
    inner = lax.broadcasted_iota(jnp.int32, shape, 0)
    done = []
    for b in range(panels):
        columns = [
            {k: jnp.broadcast_to(blocks[k][:, 8 * b + t:8 * b + t + 1], shape) for k in range(b, panels)}
            for t in range(8)
        ]
        corner = {(s, t): jnp.broadcast_to(columns[t][b][s:s + 1], shape) for t in range(8) for s in range(t, 8)}
        for t in range(8):
            root = lax.rsqrt(corner[t, t])
            along = {s: corner[s, t] * root for s in range(t + 1, 8)}
            for u in range(t + 1, 8):
                for s in range(u, 8):
                    corner[s, u] = corner[s, u] - along[s] * along[u]
            scaled = {k: x * root for k, x in columns[t].items()}
            for s in range(t + 1, 8):
                for k in range(b, panels):
                    columns[s][k] = columns[s][k] - scaled[k] * along[s]
            pivot = jnp.broadcast_to(blocks[b][t:t + 1], shape) * root
            done.append(pivot[:1])
            for k in range(b, panels):
                factor = jnp.where(inner > t, scaled[k], 0.0) if k == b else scaled[k]
                blocks[k] = blocks[k] - factor * pivot
    return jnp.concatenate(done, axis=0)[:, size:]


def output_kernel(scale, gram, loading, out):
    out[...] = exact_nn(inverse_factor(gram[...]), loading[...]) * scale


def output_call(gram, loading):
    return pl.pallas_call(
        functools.partial(output_kernel, math.sqrt(GENES)),
        in_specs=[VMEM, VMEM], out_specs=VMEM, out_shape=struct(loading.shape, f32),
        compiler_params=pltpu.CompilerParams(vmem_limit_bytes=16 * 2**20),
    )(gram, loading)


def mate(value, cells, mask, other=None):
    masks = (mask, mask if other is None else other)
    return lax.ppermute(value, "cell", [(i, i ^ masks[i % 2]) for i in range(cells)])


def legs(value, cells):
    return [mate(value, cells, 2, 4), mate(value, cells, 4, 2), mate(value, cells, 6)]


def total_over_cells(value, cells):
    value = (value + mate(value, cells, GROUP | 1)) + (mate(value, cells, GROUP) + mate(value, cells, 1))
    one, two, both_ways = legs(value, cells)
    return (value + both_ways) + (one + two)


def square_program(cells, expression, start_basis):
    width, rows = start_basis.shape[0], expression.shape[0]
    masks = ((0, 0), (1, 1), (2, 4), (3, 5), (4, 2), (5, 3), (6, 6), (7, 7))
    packs = pack(expression, masks, width)
    slots = [mate(x, cells, *pair) if k else x for k, (x, pair) in enumerate(zip(packs, masks))]

    def image_from(work, bases, before, normalised, *rest):
        (odd,) = scores(slots, work, bases, before[1:], *rest, odds=(1,))
        (even,) = scores(slots, work, bases, before[:1], *rest, odds=(0,))
        even = even + mate(odd, cells, 1)
        image = image_of(even, legs(even, cells), rows, normalised)
        return image, mate(image, cells, 1)

    first = -(-6 * width // 1280) * 128
    basis = start_basis.T
    bases = {0: [basis], 1: [mate(basis, cells, GROUP)]}
    early = scores(slots, [(0, (0, 1))], bases)
    images = image_from([(0, ()), (1, (0, 1))], bases, early, False)
    everything = [(0, (0, 1)), (1, (0, 1))]
    for _ in range(1, ITERS):
        rows_of, total = [], []
        for start, stop in ((0, first), (first, width)):
            sent = terms(slots, (start, width + start), stop - start, images, bf16)
            own, other, gram = both(sent, mate(sent, cells, GROUP), total)
            rows_of.append({0: [own], 1: [other]})
            total = [gram]
        early = scores(slots, everything, rows_of[0])
        images = image_from(everything, rows_of[1], early, True, gram, first)
    received = mate(terms(slots, (width,), width, images, bf16), cells, GROUP)
    loading, gram = loading_and_gram(received, terms(slots, (0,), width, images, f32))
    return output_call(total_over_cells(gram, cells), loading).T


def plain_program(expression, start_basis):
    basis = start_basis
    for _ in range(ITERS):
        whole = lax.all_gather(basis, "cell", axis=0, tiled=True)
        partial = jnp.dot(expression, whole, preferred_element_type=f32)
        image = lax.psum(partial, "gene").astype(bf16)
        partial = lax.dot_general(expression, image, (((0,), (0,)), ((), ())), preferred_element_type=f32)
        loading = lax.psum_scatter(partial, "cell", scatter_dimension=0, tiled=True)
        gram = lax.dot_general(loading, loading, (((0,), (0,)), ((), ())), precision=HIGHEST, preferred_element_type=f32)
        lower = jnp.linalg.cholesky(lax.psum(gram, ("cell", "gene")))
        ortho = jax.scipy.linalg.solve_triangular(lower, loading.T, lower=True).T
        basis = ortho.astype(bf16)
    return ortho * math.sqrt(GENES)


def solution(mesh):
    cells, genes = mesh.shape["cell"], mesh.shape["gene"]

    def on_device(expression, start_basis):
        width, rank = start_basis.shape
        fits = genes == 1 and cells == 2 * GROUP and width % 128 == 0 and rank == 64
        if fits and expression.shape[0] % 16 == 0:
            return square_program(cells, expression, start_basis)
        return plain_program(expression, start_basis)

    return jax.shard_map(
        on_device,
        mesh=mesh,
        in_specs=(P(("groups", "cell"), "gene"), P(("groups", "gene", "cell"), None)),
        out_specs=P(("groups", "gene", "cell"), None),
        check_vma=False,
    )
```

```python
import functools
import math

import jax
import jax.numpy as jnp
from jax import lax
from jax.experimental import pallas as pl
from jax.experimental.pallas import tpu as pltpu
from jax.sharding import PartitionSpec as P

GENES = 30720
ITERS = 2
GROUP = 8
BIG = pltpu.CompilerParams(vmem_limit_bytes=16 * 2**20)
VMEM = pl.BlockSpec(memory_space=pltpu.VMEM)
HIGHEST = lax.Precision.HIGHEST
f32, bf16 = jnp.float32, jnp.bfloat16


def nn(a, b, precision=None):
    return lax.dot_general(a, b, (((1,), (0,)), ((), ())), precision=precision, preferred_element_type=f32)


def nt(a, b, precision=None):
    return lax.dot_general(a, b, (((1,), (1,)), ((), ())), precision=precision, preferred_element_type=f32)


def three(x):
    high = x.astype(bf16)
    rest = x - high.astype(f32)
    middle = rest.astype(bf16)
    return high, middle, (rest - middle.astype(f32)).astype(bf16)


def exact_nn(a, b):
    size = a.shape[0]
    parts = three(a)
    total = 0.0
    for count, part in zip((1, 2, 3), reversed(three(b))):
        product = nn(jnp.concatenate(parts[:count], axis=0), part)
        for i in reversed(range(count)):
            total = total + product[i * size:(i + 1) * size]
    return total


def exact_gram(a):
    size = a.shape[0]
    parts = jnp.concatenate(three(a), axis=0)
    every = nt(parts, parts)

    def part(i, j):
        return every[i * size:(i + 1) * size, j * size:(j + 1) * size]

    small = (part(0, 2) + part(2, 0)) + part(1, 1)
    return part(0, 0) + ((part(0, 1) + part(1, 0)) + small)


def struct(shape, dtype):
    return jax.ShapeDtypeStruct(shape, dtype)


def cost(flops, bytes_accessed):
    return pl.CostEstimate(flops=flops, bytes_accessed=bytes_accessed, transcendentals=0)


def pack_kernel(masks, matrix, *refs):
    outs, held, sem = refs[:-2], refs[-2], refs[-1]
    rows, width = matrix.shape[0], outs[0].shape[1] // 2
    step = 16 if rows % 16 == 0 else rows
    index = lax.axis_index("cell")
    copies = [pltpu.make_async_copy(matrix.at[pl.ds(low, step)], held.at[pl.ds(low, step)], sem.at[i])
              for i, low in enumerate(range(0, rows, step))]
    for copy in copies:
        copy.start()
    for i, copy in enumerate(copies):
        copy.wait()
        some = pl.ds(i * step, step)
        for out, pair in zip(outs, masks):
            member = index ^ jnp.where(index % 2 == 0, *pair)
            for j, block in enumerate((member, member ^ GROUP)):
                start = pl.multiple_of(block * width, 128)
                out[some, pl.ds(j * width, width)] = held[some, pl.ds(start, width)]


def pack(matrix, masks, width):
    rows, count = matrix.shape[0], len(masks)
    return pl.pallas_call(
        functools.partial(pack_kernel, masks),
        in_specs=[pl.BlockSpec(memory_space=pltpu.HBM)],
        out_specs=[VMEM] * count,
        out_shape=[struct((rows, 2 * width), matrix.dtype)] * count,
        scratch_shapes=[pltpu.VMEM(matrix.shape, matrix.dtype), pltpu.SemaphoreType.DMA((rows // 16 if rows % 16 == 0 else 1,))],
        compiler_params=pltpu.CompilerParams(vmem_limit_bytes=48 * 2**20),
        cost_estimate=cost(0, 8 * rows * count * width),
    )(matrix)


def call(kernel, args, outs, estimate):
    return pl.pallas_call(
        kernel, in_specs=[VMEM] * len(args), out_specs=[VMEM] * len(outs), out_shape=outs,
        compiler_params=BIG, cost_estimate=estimate,
    )(*args)


def scores_kernel(work, odds, counts, picked, with_gram, width, offset, *refs):
    refs = list(refs)
    bases = {block: [refs.pop(0) for _ in range(count)] for block, count in counts}
    slots = {k: refs.pop(0) for k in picked}
    gram = refs.pop(0)[...] if with_gram else None
    before, outs = refs[:-len(odds)], refs[-len(odds):]
    for i, odd in enumerate(odds):
        left, values = 0, []
        for pair, blocks in work:
            value = 0.0
            for block in blocks:
                start = block * width + offset
                for part in bases[block]:
                    stop = start + part.shape[1]
                    big = [slots[4 * pair + odd][:, start:stop], slots[4 * pair + 2 + odd][:, start:stop]]
                    value = value + nt(jnp.concatenate(big, axis=0), part[...])
                    start = stop
            lanes = slice(left, left + 2 * next(iter(slots.values())).shape[0])
            left = lanes.stop
            if blocks:
                value = value.T
            if before and lanes.stop <= before[i].shape[1]:
                value = value + before[i][:, lanes]
            values.append(value)
        if with_gram:
            rank = gram.shape[0]
            rows = rank * rank // left
            for j in range(rank // rows):
                outs[i][rank:, j * rank:(j + 1) * rank] = gram[j * rows:(j + 1) * rows]
            outs[i][:rank] = jnp.concatenate(values, axis=1)
        else:
            outs[i][...] = jnp.concatenate(values, axis=1) if len(values) > 1 else values[0]


def scores(slots, work, bases, before=(), gram=None, offset=0, odds=(0, 1)):
    rank = next(iter(bases.values()))[0].shape[0]
    picked = [4 * pair + 2 * k + odd for pair, blocks in work if blocks for k in range(2) for odd in odds]
    rows, width = slots[picked[0]].shape[0], slots[picked[0]].shape[1] // 2
    cells = 2 * rows * len(work)
    height = rank + (0 if gram is None else rank * rank // cells)
    counts = [(block, len(parts)) for block, parts in bases.items()]
    args = [x for parts in bases.values() for x in parts] + [slots[k] for k in picked]
    args += ([] if gram is None else [gram]) + list(before)
    size = 2 * len(odds) * rows * width * sum(len(blocks) for _, blocks in work)
    kernel = functools.partial(scores_kernel, work, odds, counts, picked, gram is not None, width, offset)
    return call(kernel, args, [struct((height, cells), f32)] * len(odds), cost(2 * rank * size, 2 * size))


def image_kernel(normalised, *refs):
    values, out = [ref[...] for ref in refs[:-1]], refs[-1]
    cells = out.shape[1]
    size = cells // (GROUP // 2)

    def turned(x, mask):
        return jnp.concatenate([x[:, (j ^ mask) * size:((j ^ mask) + 1) * size] for j in range(GROUP // 2)], axis=1)

    rank = out.shape[0]
    top = [x[:rank] for x in values]
    value = (top[0] + turned(top[3], 3)) + (turned(top[1], 1) + turned(top[2], 2))
    if normalised:
        below = [x[rank:] for x in values]
        below = (below[0] + below[3]) + (below[1] + below[2])
        gram = jnp.concatenate([below[:, j * rank:(j + 1) * rank] for j in range(cells // rank)], axis=0)
        value = exact_nn(inverse_factor(gram), value)
    out[...] = value.astype(bf16)


def image_of(value, mates, rank, normalised):
    cells = value.shape[1]
    return call(functools.partial(image_kernel, normalised), [value, *mates], [struct((rank, cells), bf16)],
                cost(12 * value.size * rank, 16 * value.size))[0]


def terms_kernel(starts, *refs):
    slots, images, out = refs[:GROUP], refs[GROUP:GROUP + 2], refs[-1]
    width = out.shape[1]
    rank = out.shape[0] // len(starts)
    step = width // 2 if width % 256 == 0 else width
    for part, start in enumerate(starts):
        for left in range(0, width, step):
            total = 0.0
            for odd in range(2):
                big = jnp.concatenate([ref[:, start + left:start + left + step] for ref in slots[odd::2]], axis=0)
                total = total + nn(images[odd][...], big)
            out[part * rank:(part + 1) * rank, left:left + step] = total.astype(out.dtype)


def terms(slots, starts, width, images, dtype):
    rank, cells = images[0].shape[0], slots[0].shape[0] * GROUP
    size = cells * width * len(starts)
    return call(functools.partial(terms_kernel, starts), [*slots, *images],
                [struct((rank * len(starts), width), dtype)], cost(2 * rank * size, 2 * size))[0]


def both_kernel(sent, received, *refs):
    before, rows, gram = refs[:-3], refs[-3:-1], refs[-1]
    rank = rows[0].shape[0]
    grams = []
    for block in range(2):
        mine, theirs = slice(block * rank, (block + 1) * rank), slice((1 - block) * rank, (2 - block) * rank)
        value = sent[mine].astype(f32) + received[theirs].astype(f32)
        rows[block][...] = value.astype(bf16)
        grams.append(exact_gram(value))
    total = grams[0] + grams[1]
    for ref in before:
        total = total + ref[...]
    gram[...] = total


def both(sent, received, before):
    rank, width = sent.shape[0] // 2, sent.shape[1]
    return call(both_kernel, [sent, received, *before], [struct((rank, width), bf16)] * 2 + [struct((rank, rank), f32)],
                cost(24 * rank * rank * width, 24 * rank * width))


def loading_kernel(received, own, *refs):
    before, loading, gram = refs[:-2], refs[-2], refs[-1]
    value = own[...] + received[...].astype(f32)
    loading[...] = value
    total = exact_gram(value)
    for ref in before:
        total = total + ref[...]
    gram[...] = total


def loading_and_gram(received, own, before):
    rank, width = own.shape
    return call(loading_kernel, [received, own, *before], [struct((rank, width), f32), struct((rank, rank), f32)],
                cost(12 * rank * rank * width, 12 * rank * width))


def inverse_factor(gram):
    size = gram.shape[0]
    row = lax.broadcasted_iota(jnp.int32, (size, size), 0)
    column = lax.broadcasted_iota(jnp.int32, (size, size), 1)
    both = jnp.concatenate([gram, jnp.where(row == column, 1.0, 0.0).astype(f32)], axis=1)
    panels = size // 8
    shape = (8, 2 * size)
    blocks = [both[8 * b:8 * b + 8] for b in range(panels)]
    inner = lax.broadcasted_iota(jnp.int32, shape, 0)
    done = []
    for b in range(panels):
        columns = [
            {k: jnp.broadcast_to(blocks[k][:, 8 * b + t:8 * b + t + 1], shape) for k in range(b, panels)}
            for t in range(8)
        ]
        for t in range(8):
            root = lax.rsqrt(jnp.broadcast_to(columns[t][b][t:t + 1], shape))
            scaled = {k: x * root for k, x in columns[t].items()}
            for s in range(t + 1, 8):
                along = jnp.broadcast_to(scaled[b][s:s + 1], shape)
                for k in range(b, panels):
                    columns[s][k] = columns[s][k] - scaled[k] * along
            pivot = jnp.broadcast_to(blocks[b][t:t + 1], shape) * root
            done.append(pivot[:1])
            for k in range(b, panels):
                factor = jnp.where(inner > t, scaled[k], 0.0) if k == b else scaled[k]
                blocks[k] = blocks[k] - factor * pivot
    return jnp.concatenate(done, axis=0)[:, size:]


def output_kernel(scale, gram, *refs):
    parts, out = refs[:-1], refs[-1]
    inverse = inverse_factor(gram[...]) * scale
    start = 0
    for part in parts:
        out[:, start:start + part.shape[1]] = exact_nn(inverse, part[...])
        start += part.shape[1]


def output_call(gram, parts):
    rank, width = gram.shape[0], sum(x.shape[1] for x in parts)
    return call(functools.partial(output_kernel, math.sqrt(GENES)), [gram, *parts], [struct((rank, width), f32)],
                cost(12 * rank * rank * width, 8 * rank * width))[0]


def mate(value, cells, mask, other=None):
    masks = (mask, mask if other is None else other)
    return lax.ppermute(value, "cell", [(i, i ^ masks[i % 2]) for i in range(cells)])


def legs(value, cells):
    return [mate(value, cells, 2, 4), mate(value, cells, 4, 2), mate(value, cells, 6)]


def total_over_cells(value, cells):
    value = (value + mate(value, cells, GROUP | 1)) + (mate(value, cells, GROUP) + mate(value, cells, 1))
    one, two, both_ways = legs(value, cells)
    return (value + both_ways) + (one + two)


def cuts(width, *percents):
    edges = [0]
    for percent in percents:
        edges.append(edges[-1] + -(-percent * width // 12800) * 128)
    edges = [edge for edge in edges if edge < width] + [width]
    return list(zip(edges, edges[1:]))


def square_program(cells, expression, start_basis):
    width, rank = start_basis.shape
    masks = ((0, 0), (1, 1), (2, 4), (3, 5), (4, 2), (5, 3), (6, 6), (7, 7))
    packs = pack(expression, masks, width)
    slots = [mate(x, cells, *pair) if k else x for k, (x, pair) in enumerate(zip(packs, masks))]

    def image_from(work, bases, before, normalised, *rest):
        (odd,) = scores(slots, work, bases, before[1:], *rest, odds=(1,))
        (even,) = scores(slots, work, bases, before[:1], *rest, odds=(0,))
        even = even + mate(odd, cells, 1)
        image = image_of(even, legs(even, cells), rank, normalised)
        return image, mate(image, cells, 1)

    basis = start_basis.T
    bases = {0: [basis], 1: [mate(basis, cells, GROUP)]}
    early = scores(slots, [(0, (0, 1))], bases)
    images = image_from([(0, ()), (1, (0, 1))], bases, early, False)
    everything = [(0, (0, 1)), (1, (0, 1))]
    for _ in range(1, ITERS):
        total, before = [], ()
        arrived = []
        for start, stop in cuts(width, 45, 33):
            sent = terms(slots, (start, width + start), stop - start, images, bf16)
            arrived.append((start, stop, sent, mate(sent, cells, GROUP)))
        for start, stop, sent, received in arrived:
            if before:
                received, *before = lax.optimization_barrier((received, *before))
            own, other, gram = both(sent, received, total)
            total, rows = [gram], {0: [own], 1: [other]}
            if stop < width:
                before = scores(slots, everything, rows, before, offset=start)
        images = image_from(everything, rows, before, True, gram, start)
    parts, total = [], []
    for start, stop in cuts(width, 60):
        received = mate(terms(slots, (width + start,), stop - start, images, bf16), cells, GROUP)
        rows, gram = loading_and_gram(received, terms(slots, (start,), stop - start, images, f32), total)
        parts.append(rows)
        total = [gram]
    return output_call(total_over_cells(gram, cells), parts).T


def plain_program(expression, start_basis):
    basis = start_basis
    for _ in range(ITERS):
        whole = lax.all_gather(basis, "cell", axis=0, tiled=True)
        partial = jnp.dot(expression, whole, preferred_element_type=f32)
        image = lax.psum(partial, "gene").astype(bf16)
        partial = lax.dot_general(expression, image, (((0,), (0,)), ((), ())), preferred_element_type=f32)
        loading = lax.psum_scatter(partial, "cell", scatter_dimension=0, tiled=True)
        gram = lax.dot_general(loading, loading, (((0,), (0,)), ((), ())), precision=HIGHEST, preferred_element_type=f32)
        lower = jnp.linalg.cholesky(lax.psum(gram, ("cell", "gene")))
        ortho = jax.scipy.linalg.solve_triangular(lower, loading.T, lower=True).T
        basis = ortho.astype(bf16)
    return ortho * math.sqrt(GENES)


def solution(mesh):
    cells, genes = mesh.shape["cell"], mesh.shape["gene"]

    def on_device(expression, start_basis):
        width, rank = start_basis.shape
        fits = genes == 1 and cells == 2 * GROUP and width % 128 == 0 and rank == 64
        if fits and expression.shape[0] % 16 == 0:
            return square_program(cells, expression, start_basis)
        return plain_program(expression, start_basis)

    return jax.shard_map(
        on_device,
        mesh=mesh,
        in_specs=(P(("groups", "cell"), "gene"), P(("groups", "gene", "cell"), None)),
        out_specs=P(("groups", "gene", "cell"), None),
        check_vma=False,
    )
```

```python
import functools
import math

import jax
import jax.numpy as jnp
from jax import lax
from jax.experimental import pallas as pl
from jax.experimental.pallas import tpu as pltpu
from jax.sharding import PartitionSpec as P

GENES = 30720
ITERS = 2
GROUP = 8
BIG = pltpu.CompilerParams(vmem_limit_bytes=16 * 2**20)
VMEM = pl.BlockSpec(memory_space=pltpu.VMEM)
HIGHEST = lax.Precision.HIGHEST
f32, bf16 = jnp.float32, jnp.bfloat16


def nn(a, b, precision=None):
    return lax.dot_general(a, b, (((1,), (0,)), ((), ())), precision=precision, preferred_element_type=f32)


def nt(a, b, precision=None):
    return lax.dot_general(a, b, (((1,), (1,)), ((), ())), precision=precision, preferred_element_type=f32)


def three(x):
    high = x.astype(bf16)
    rest = x - high.astype(f32)
    middle = rest.astype(bf16)
    return high, middle, (rest - middle.astype(f32)).astype(bf16)


def exact_nn(a, b):
    a1, a2, a3 = three(a)
    b1, b2, b3 = three(b)
    return nn(jnp.concatenate([a3, a2, a1, a2, a1, a1], axis=1), jnp.concatenate([b1, b2, b3, b1, b2, b1], axis=0))


def exact_gram(a):
    size = a.shape[0]
    parts = jnp.concatenate(three(a), axis=0)
    every = nt(parts, parts)

    def part(i, j):
        return every[i * size:(i + 1) * size, j * size:(j + 1) * size]

    small = (part(0, 2) + part(2, 0)) + part(1, 1)
    return part(0, 0) + ((part(0, 1) + part(1, 0)) + small)


def struct(shape, dtype):
    return jax.ShapeDtypeStruct(shape, dtype)


def cost(flops, bytes_accessed):
    return pl.CostEstimate(flops=flops, bytes_accessed=bytes_accessed, transcendentals=0)


def pack_kernel(masks, matrix, *refs):
    outs, held, sem = refs[:-2], refs[-2], refs[-1]
    rows, width = matrix.shape[0], outs[0].shape[1] // 2
    step = 16 if rows % 16 == 0 else rows
    index = lax.axis_index("cell")
    copies = [pltpu.make_async_copy(matrix.at[pl.ds(low, step)], held.at[pl.ds(low, step)], sem.at[i])
              for i, low in enumerate(range(0, rows, step))]
    for copy in copies:
        copy.start()
    for i, copy in enumerate(copies):
        copy.wait()
        some = pl.ds(i * step, step)
        for out, pair in zip(outs, masks):
            member = index ^ jnp.where(index % 2 == 0, *pair)
            for j, block in enumerate((member, member ^ GROUP)):
                start = pl.multiple_of(block * width, 128)
                out[some, pl.ds(j * width, width)] = held[some, pl.ds(start, width)]


def pack(matrix, masks, width):
    rows, count = matrix.shape[0], len(masks)
    return pl.pallas_call(
        functools.partial(pack_kernel, masks),
        in_specs=[pl.BlockSpec(memory_space=pltpu.HBM)],
        out_specs=[VMEM] * count,
        out_shape=[struct((rows, 2 * width), matrix.dtype)] * count,
        scratch_shapes=[pltpu.VMEM(matrix.shape, matrix.dtype), pltpu.SemaphoreType.DMA((rows // 16 if rows % 16 == 0 else 1,))],
        compiler_params=pltpu.CompilerParams(vmem_limit_bytes=48 * 2**20),
        cost_estimate=cost(0, 8 * rows * count * width),
    )(matrix)


def call(kernel, args, outs, estimate):
    return pl.pallas_call(
        kernel, in_specs=[VMEM] * len(args), out_specs=[VMEM] * len(outs), out_shape=outs,
        compiler_params=BIG, cost_estimate=estimate,
    )(*args)


def scores_kernel(work, odds, counts, picked, with_gram, width, offset, *refs):
    refs = list(refs)
    bases = {block: [refs.pop(0) for _ in range(count)] for block, count in counts}
    slots = {k: refs.pop(0) for k in picked}
    gram = refs.pop(0)[...] if with_gram else None
    before, outs = refs[:-len(odds)], refs[-len(odds):]
    for i, odd in enumerate(odds):
        left, values = 0, []
        for pair, blocks in work:
            value = 0.0
            for block in blocks:
                start = block * width + offset
                for part in bases[block]:
                    stop = start + part.shape[1]
                    big = [slots[4 * pair + odd][:, start:stop], slots[4 * pair + 2 + odd][:, start:stop]]
                    value = value + nt(jnp.concatenate(big, axis=0), part[...])
                    start = stop
            lanes = slice(left, left + 2 * next(iter(slots.values())).shape[0])
            left = lanes.stop
            if blocks:
                value = value.T
            if before and lanes.stop <= before[i].shape[1]:
                value = value + before[i][:, lanes]
            values.append(value)
        if with_gram:
            rank = gram.shape[0]
            rows = rank * rank // left
            for j in range(rank // rows):
                outs[i][rank:, j * rank:(j + 1) * rank] = gram[j * rows:(j + 1) * rows]
            outs[i][:rank] = jnp.concatenate(values, axis=1)
        else:
            outs[i][...] = jnp.concatenate(values, axis=1) if len(values) > 1 else values[0]


def scores(slots, work, bases, before=(), gram=None, offset=0, odds=(0, 1)):
    rank = next(iter(bases.values()))[0].shape[0]
    picked = [4 * pair + 2 * k + odd for pair, blocks in work if blocks for k in range(2) for odd in odds]
    rows, width = slots[picked[0]].shape[0], slots[picked[0]].shape[1] // 2
    cells = 2 * rows * len(work)
    height = rank + (0 if gram is None else rank * rank // cells)
    counts = [(block, len(parts)) for block, parts in bases.items()]
    args = [x for parts in bases.values() for x in parts] + [slots[k] for k in picked]
    args += ([] if gram is None else [gram]) + list(before)
    size = 2 * len(odds) * rows * width * sum(len(blocks) for _, blocks in work)
    kernel = functools.partial(scores_kernel, work, odds, counts, picked, gram is not None, width, offset)
    return call(kernel, args, [struct((height, cells), f32)] * len(odds), cost(2 * rank * size, 2 * size))


def image_kernel(normalised, *refs):
    values, out = [ref[...] for ref in refs[:-1]], refs[-1]
    cells = out.shape[1]
    size = cells // (GROUP // 2)

    def turned(x, mask):
        return jnp.concatenate([x[:, (j ^ mask) * size:((j ^ mask) + 1) * size] for j in range(GROUP // 2)], axis=1)

    rank = out.shape[0]
    top = [x[:rank] for x in values]
    value = (top[0] + turned(top[1], 1)) + (turned(top[2], 2) + turned(top[3], 3))
    if normalised:
        below = [x[rank:] for x in values]
        below = (below[0] + below[1]) + (below[2] + below[3])
        gram = jnp.concatenate([below[:, j * rank:(j + 1) * rank] for j in range(cells // rank)], axis=0)
        value = exact_nn(inverse_factor(gram), value)
    out[...] = value.astype(bf16)


def image_of(value, mates, rank, normalised):
    cells = value.shape[1]
    return call(functools.partial(image_kernel, normalised), [value, *mates], [struct((rank, cells), bf16)],
                cost(12 * value.size * rank, 16 * value.size))[0]


def terms_kernel(starts, *refs):
    slots, images, out = refs[:GROUP], refs[GROUP:GROUP + 2], refs[-1]
    width = out.shape[1]
    rank = out.shape[0] // len(starts)
    step = width // 2 if width % 256 == 0 else width
    for part, start in enumerate(starts):
        for left in range(0, width, step):
            total = 0.0
            for odd in range(2):
                big = jnp.concatenate([ref[:, start + left:start + left + step] for ref in slots[odd::2]], axis=0)
                total = total + nn(images[odd][...], big)
            out[part * rank:(part + 1) * rank, left:left + step] = total.astype(out.dtype)


def terms(slots, starts, width, images, dtype):
    rank, cells = images[0].shape[0], slots[0].shape[0] * GROUP
    size = cells * width * len(starts)
    return call(functools.partial(terms_kernel, starts), [*slots, *images],
                [struct((rank * len(starts), width), dtype)], cost(2 * rank * size, 2 * size))[0]


def both_kernel(sent, received, *refs):
    before, rows, gram = refs[:-3], refs[-3:-1], refs[-1]
    rank = rows[0].shape[0]
    grams = []
    for block in range(2):
        mine, theirs = slice(block * rank, (block + 1) * rank), slice((1 - block) * rank, (2 - block) * rank)
        value = sent[mine].astype(f32) + received[theirs].astype(f32)
        rows[block][...] = value.astype(bf16)
        grams.append(exact_gram(value))
    total = grams[0] + grams[1]
    for ref in before:
        total = total + ref[...]
    gram[...] = total


def both(sent, received, before):
    rank, width = sent.shape[0] // 2, sent.shape[1]
    return call(both_kernel, [sent, received, *before], [struct((rank, width), bf16)] * 2 + [struct((rank, rank), f32)],
                cost(24 * rank * rank * width, 24 * rank * width))


def loading_kernel(received, own, *refs):
    before, loading, gram = refs[:-2], refs[-2], refs[-1]
    value = own[...] + received[...].astype(f32)
    loading[...] = value
    total = exact_gram(value)
    for ref in before:
        total = total + ref[...]
    gram[...] = total


def loading_and_gram(received, own, before):
    rank, width = own.shape
    return call(loading_kernel, [received, own, *before], [struct((rank, width), f32), struct((rank, rank), f32)],
                cost(12 * rank * rank * width, 12 * rank * width))


def inverse_factor(gram):
    size = gram.shape[0]
    row = lax.broadcasted_iota(jnp.int32, (size, size), 0)
    column = lax.broadcasted_iota(jnp.int32, (size, size), 1)
    both = jnp.concatenate([gram, jnp.where(row == column, 1.0, 0.0).astype(f32)], axis=1)
    panels = size // 8
    shape = (8, 2 * size)
    blocks = [both[8 * b:8 * b + 8] for b in range(panels)]
    inner = lax.broadcasted_iota(jnp.int32, shape, 0)
    done = []
    for b in range(panels):
        columns = [
            {k: jnp.broadcast_to(blocks[k][:, 8 * b + t:8 * b + t + 1], shape) for k in range(b, panels)}
            for t in range(8)
        ]
        for t in range(8):
            root = lax.rsqrt(jnp.broadcast_to(columns[t][b][t:t + 1], shape))
            scaled = {k: x * root for k, x in columns[t].items()}
            for s in range(t + 1, 8):
                along = jnp.broadcast_to(scaled[b][s:s + 1], shape)
                for k in range(b, panels):
                    columns[s][k] = columns[s][k] - scaled[k] * along
            pivot = jnp.broadcast_to(blocks[b][t:t + 1], shape) * root
            done.append(pivot[:1])
            for k in range(b, panels):
                factor = jnp.where(inner > t, scaled[k], 0.0) if k == b else scaled[k]
                blocks[k] = blocks[k] - factor * pivot
    return jnp.concatenate(done, axis=0)[:, size:]


def output_kernel(scale, gram, *refs):
    parts, out = refs[:-1], refs[-1]
    inverse = inverse_factor(gram[...]) * scale
    start = 0
    for part in parts:
        out[:, start:start + part.shape[1]] = exact_nn(inverse, part[...])
        start += part.shape[1]


def output_call(gram, parts):
    rank, width = gram.shape[0], sum(x.shape[1] for x in parts)
    return call(functools.partial(output_kernel, math.sqrt(GENES)), [gram, *parts], [struct((rank, width), f32)],
                cost(12 * rank * rank * width, 8 * rank * width))[0]


def mate(value, cells, mask, other=None):
    masks = (mask, mask if other is None else other)
    return lax.ppermute(value, "cell", [(i, i ^ masks[i % 2]) for i in range(cells)])


def legs(value, cells):
    return [mate(value, cells, 6), mate(value, cells, 2, 4), mate(value, cells, 4, 2)]


def total_over_cells(value, cells):
    value = (value + mate(value, cells, GROUP | 1)) + (mate(value, cells, GROUP) + mate(value, cells, 1))
    across, one, two = legs(value, cells)
    return (value + across) + (one + two)


def cuts(width, *percents):
    edges = [0]
    for percent in percents:
        edges.append(edges[-1] + -(-percent * width // 12800) * 128)
    edges = [edge for edge in edges if edge < width] + [width]
    return list(zip(edges, edges[1:]))


def square_program(cells, expression, start_basis):
    width, rank = start_basis.shape
    masks = ((0, 0), (1, 1), (6, 6), (7, 7), (2, 4), (3, 5), (4, 2), (5, 3))
    packs = pack(expression, masks, width)
    slots = [mate(x, cells, *pair) if k else x for k, (x, pair) in enumerate(zip(packs, masks))]

    def image_from(work, bases, before, normalised, *rest):
        (odd,) = scores(slots, work, bases, before[1:], *rest, odds=(1,))
        (even,) = scores(slots, work, bases, before[:1], *rest, odds=(0,))
        even = even + mate(odd, cells, 1)
        image = image_of(even, legs(even, cells), rank, normalised)
        return image, mate(image, cells, 1)

    basis = start_basis.T
    bases = {0: [basis], 1: [mate(basis, cells, GROUP)]}
    early = scores(slots, [(0, (0, 1))], bases)
    images = image_from([(0, ()), (1, (0, 1))], bases, early, False)
    everything = [(0, (0, 1)), (1, (0, 1))]
    for _ in range(1, ITERS):
        total, before = [], ()
        arrived = []
        for start, stop in cuts(width, 45, 33):
            sent = terms(slots, (start, width + start), stop - start, images, bf16)
            arrived.append((start, stop, sent, mate(sent, cells, GROUP)))
        for start, stop, sent, received in arrived:
            if before:
                received, *before = lax.optimization_barrier((received, *before))
            own, other, gram = both(sent, received, total)
            total, rows = [gram], {0: [own], 1: [other]}
            if stop < width:
                before = scores(slots, everything, rows, before, offset=start)
        images = image_from(everything, rows, before, True, gram, start)
    parts, total = [], []
    for start, stop in cuts(width, 60):
        received = mate(terms(slots, (width + start,), stop - start, images, bf16), cells, GROUP)
        rows, gram = loading_and_gram(received, terms(slots, (start,), stop - start, images, f32), total)
        parts.append(rows)
        total = [gram]
    return output_call(total_over_cells(gram, cells), parts).T


def plain_program(expression, start_basis):
    basis = start_basis
    for _ in range(ITERS):
        whole = lax.all_gather(basis, "cell", axis=0, tiled=True)
        partial = jnp.dot(expression, whole, preferred_element_type=f32)
        image = lax.psum(partial, "gene").astype(bf16)
        partial = lax.dot_general(expression, image, (((0,), (0,)), ((), ())), preferred_element_type=f32)
        loading = lax.psum_scatter(partial, "cell", scatter_dimension=0, tiled=True)
        gram = lax.dot_general(loading, loading, (((0,), (0,)), ((), ())), precision=HIGHEST, preferred_element_type=f32)
        lower = jnp.linalg.cholesky(lax.psum(gram, ("cell", "gene")))
        ortho = jax.scipy.linalg.solve_triangular(lower, loading.T, lower=True).T
        basis = ortho.astype(bf16)
    return ortho * math.sqrt(GENES)


def solution(mesh):
    cells, genes = mesh.shape["cell"], mesh.shape["gene"]

    def on_device(expression, start_basis):
        width, rank = start_basis.shape
        fits = genes == 1 and cells == 2 * GROUP and width % 128 == 0 and rank == 64
        if fits and expression.shape[0] % 16 == 0:
            return square_program(cells, expression, start_basis)
        return plain_program(expression, start_basis)

    return jax.shard_map(
        on_device,
        mesh=mesh,
        in_specs=(P(("groups", "cell"), "gene"), P(("groups", "gene", "cell"), None)),
        out_specs=P(("groups", "gene", "cell"), None),
        check_vma=False,
    )
```

```python
import functools
import math

import jax
import jax.numpy as jnp
from jax import lax
from jax.experimental import pallas as pl
from jax.experimental.pallas import tpu as pltpu
from jax.sharding import PartitionSpec as P

GENES = 30720
ITERS = 2
GROUP = 8
BIG = pltpu.CompilerParams(vmem_limit_bytes=16 * 2**20)
VMEM = pl.BlockSpec(memory_space=pltpu.VMEM)
HIGHEST = lax.Precision.HIGHEST
f32, bf16 = jnp.float32, jnp.bfloat16


def nn(a, b, precision=None):
    return lax.dot_general(a, b, (((1,), (0,)), ((), ())), precision=precision, preferred_element_type=f32)


def nt(a, b, precision=None):
    return lax.dot_general(a, b, (((1,), (1,)), ((), ())), precision=precision, preferred_element_type=f32)


def three(x):
    high = x.astype(bf16)
    rest = x - high.astype(f32)
    middle = rest.astype(bf16)
    return high, middle, (rest - middle.astype(f32)).astype(bf16)


def exact_nn(a, b):
    a1, a2, a3 = three(a)
    b1, b2, b3 = three(b)
    return nn(jnp.concatenate([a3, a2, a1, a2, a1, a1], axis=1), jnp.concatenate([b1, b2, b3, b1, b2, b1], axis=0))


def exact_nt(a, b):
    a1, a2, a3 = three(a)
    b1, b2, b3 = three(b)
    return nt(jnp.concatenate([a3, a2, a1, a2, a1, a1], axis=1), jnp.concatenate([b1, b2, b3, b1, b2, b1], axis=1))


def exact_by_bf16(a, b):
    return nn(jnp.concatenate(three(a), axis=1), jnp.concatenate([b] * 3, axis=0))


def first_half():
    return lax.axis_index("cell") & GROUP == 0


def exact_gram(a):
    size = a.shape[0]
    parts = jnp.concatenate(three(a), axis=0)
    every = nt(parts, parts)

    def part(i, j):
        return every[i * size:(i + 1) * size, j * size:(j + 1) * size]

    small = (part(0, 2) + part(2, 0)) + part(1, 1)
    return part(0, 0) + ((part(0, 1) + part(1, 0)) + small)


def struct(shape, dtype):
    return jax.ShapeDtypeStruct(shape, dtype)


def cost(flops, bytes_accessed):
    return pl.CostEstimate(flops=flops, bytes_accessed=bytes_accessed, transcendentals=0)


def pack_kernel(masks, matrix, *refs):
    outs, held, sem = refs[:-2], refs[-2], refs[-1]
    rows, width = matrix.shape[0], outs[0].shape[1] // 2
    step = 16 if rows % 16 == 0 else rows
    index = lax.axis_index("cell")
    copies = [pltpu.make_async_copy(matrix.at[pl.ds(low, step)], held.at[pl.ds(low, step)], sem.at[i])
              for i, low in enumerate(range(0, rows, step))]
    for copy in copies:
        copy.start()
    for i, copy in enumerate(copies):
        copy.wait()
        some = pl.ds(i * step, step)
        for out, pair in zip(outs, masks):
            member = index ^ jnp.where(index % 2 == 0, *pair)
            for j, block in enumerate((member, member ^ GROUP)):
                start = pl.multiple_of(block * width, 128)
                out[some, pl.ds(j * width, width)] = held[some, pl.ds(start, width)]


def pack(matrix, masks, width):
    rows, count = matrix.shape[0], len(masks)
    return pl.pallas_call(
        functools.partial(pack_kernel, masks),
        in_specs=[pl.BlockSpec(memory_space=pltpu.HBM)],
        out_specs=[VMEM] * count,
        out_shape=[struct((rows, 2 * width), matrix.dtype)] * count,
        scratch_shapes=[pltpu.VMEM(matrix.shape, matrix.dtype), pltpu.SemaphoreType.DMA((rows // 16 if rows % 16 == 0 else 1,))],
        compiler_params=pltpu.CompilerParams(vmem_limit_bytes=48 * 2**20),
        cost_estimate=cost(0, 8 * rows * count * width),
    )(matrix)


def call(kernel, args, outs, estimate):
    return pl.pallas_call(
        kernel, in_specs=[VMEM] * len(args), out_specs=[VMEM] * len(outs), out_shape=outs,
        compiler_params=BIG, cost_estimate=estimate,
    )(*args)


def scores_kernel(work, odds, counts, picked, with_gram, width, offset, *refs):
    refs = list(refs)
    bases = {block: [refs.pop(0) for _ in range(count)] for block, count in counts}
    slots = {k: refs.pop(0) for k in picked}
    gram = refs.pop(0)[...] if with_gram else None
    before, outs = refs[:-len(odds)], refs[-len(odds):]
    for i, odd in enumerate(odds):
        left, values = 0, []
        for pair, blocks in work:
            value = 0.0
            for block in blocks:
                start = block * width + offset
                for part in bases[block]:
                    stop = start + part.shape[1]
                    big = [slots[4 * pair + odd][:, start:stop], slots[4 * pair + 2 + odd][:, start:stop]]
                    value = value + nt(jnp.concatenate(big, axis=0), part[...])
                    start = stop
            lanes = slice(left, left + 2 * next(iter(slots.values())).shape[0])
            left = lanes.stop
            if blocks:
                value = value.T
            if before and lanes.stop <= before[i].shape[1]:
                value = value + before[i][:, lanes]
            values.append(value)
        if with_gram:
            rank = gram.shape[0]
            rows = rank * rank // left
            for j in range(rank // rows):
                outs[i][rank:, j * rank:(j + 1) * rank] = gram[j * rows:(j + 1) * rows]
            outs[i][:rank] = jnp.concatenate(values, axis=1)
        else:
            outs[i][...] = jnp.concatenate(values, axis=1) if len(values) > 1 else values[0]


def scores(slots, work, bases, before=(), gram=None, offset=0, odds=(0, 1)):
    rank = next(iter(bases.values()))[0].shape[0]
    picked = [4 * pair + 2 * k + odd for pair, blocks in work if blocks for k in range(2) for odd in odds]
    rows, width = slots[picked[0]].shape[0], slots[picked[0]].shape[1] // 2
    cells = 2 * rows * len(work)
    height = rank + (0 if gram is None else rank * rank // cells)
    counts = [(block, len(parts)) for block, parts in bases.items()]
    args = [x for parts in bases.values() for x in parts] + [slots[k] for k in picked]
    args += ([] if gram is None else [gram]) + list(before)
    size = 2 * len(odds) * rows * width * sum(len(blocks) for _, blocks in work)
    kernel = functools.partial(scores_kernel, work, odds, counts, picked, gram is not None, width, offset)
    return call(kernel, args, [struct((height, cells), f32)] * len(odds), cost(2 * rank * size, 2 * size))


def image_kernel(normalised, *refs):
    values, out = [ref[...] for ref in refs[:-1]], refs[-1]
    cells = out.shape[1]
    size = cells // (GROUP // 2)

    def turned(x, mask):
        return jnp.concatenate([x[:, (j ^ mask) * size:((j ^ mask) + 1) * size] for j in range(GROUP // 2)], axis=1)

    rank = out.shape[0]
    top = [x[:rank] for x in values]
    value = (top[0] + turned(top[1], 1)) + (turned(top[2], 2) + turned(top[3], 3))
    if normalised:
        below = [x[rank:] for x in values]
        below = (below[0] + below[1]) + (below[2] + below[3])
        gram = jnp.concatenate([below[:, j * rank:(j + 1) * rank] for j in range(cells // rank)], axis=0)
        value = exact_nn(factors(gram)[1], value)
    out[...] = value.astype(bf16)


def image_of(value, mates, rank, normalised):
    cells = value.shape[1]
    return call(functools.partial(image_kernel, normalised), [value, *mates], [struct((rank, cells), bf16)],
                cost(12 * value.size * rank, 16 * value.size))[0]


def whiten_kernel(even, odd, even_out, odd_out, factor):
    rank = even.shape[0]
    size = even.shape[1] // (GROUP // 2)
    chips = []
    for j in range(GROUP // 2):
        one, two = (ref[:, j * size:(j + 1) * size] for ref in (even, odd))
        chips.append(nt(one, one) + nt(two, two))
    gram = (chips[0] + chips[1]) + (chips[2] + chips[3])
    diagonal = lax.broadcasted_iota(jnp.int32, gram.shape, 0) == lax.broadcasted_iota(jnp.int32, gram.shape, 1)
    shift = jnp.sum(jnp.where(diagonal, gram, 0.0), keepdims=True) * (1e-5 / rank) + 1e-12
    upper, inverse = factors(gram + jnp.where(diagonal, shift, 0.0))
    for source, out in ((even, even_out), (odd, odd_out)):
        value = exact_by_bf16(inverse, source[...])
        high = value.astype(bf16)
        out[:rank] = high
        out[rank:] = (value - high.astype(f32)).astype(bf16)
    factor[...] = jnp.where(first_half(), inverse, upper)


def whiten(even, odd):
    rank = even.shape[0]
    return call(whiten_kernel, [even, odd], [struct((2 * rank, even.shape[1]), bf16)] * 2 + [struct((rank, rank), f32)],
                cost(12 * even.size * rank, 8 * even.size))


def change_kernel(mine, theirs, out):
    first = first_half()
    inverse = jnp.where(first, mine[...], theirs[...])
    upper = jnp.where(first, theirs[...], mine[...])
    out[...] = exact_nt(inverse, upper)


def change_of(mine, theirs):
    return call(change_kernel, [mine, theirs], [struct(mine.shape, f32)], cost(12 * mine.size, 12 * mine.size))[0]


def terms_kernel(starts, *refs):
    slots, images, out = refs[:GROUP], refs[GROUP:GROUP + 2], refs[-1]
    width = out.shape[1]
    rank = out.shape[0] // len(starts)
    step = width // 2 if width % 256 == 0 else width
    for part, start in enumerate(starts):
        for left in range(0, width, step):
            total = 0.0
            for odd in range(2):
                big = jnp.concatenate([ref[:, start + left:start + left + step] for ref in slots[odd::2]], axis=0)
                total = total + nn(images[odd][...], big)
            out[part * rank:(part + 1) * rank, left:left + step] = (total[:rank] + total[rank:]).astype(out.dtype)


def terms(slots, starts, width, images, dtype):
    rank, cells = images[0].shape[0] // 2, slots[0].shape[0] * GROUP
    size = cells * width * len(starts)
    return call(functools.partial(terms_kernel, starts), [*slots, *images],
                [struct((rank * len(starts), width), dtype)], cost(4 * rank * size, 2 * size))[0]


def both_kernel(sent, received, change, *refs):
    before, rows, gram = refs[:-3], refs[-3:-1], refs[-1]
    rank = rows[0].shape[0]
    first = first_half()
    grams = []
    for block in range(2):
        mine, theirs = slice(block * rank, (block + 1) * rank), slice((1 - block) * rank, (2 - block) * rank)
        one, two = sent[mine].astype(f32), received[theirs].astype(f32)
        value = jnp.where(first, one, two) + exact_by_bf16(change[...], jnp.where(first, two, one).astype(bf16))
        rows[block][...] = value.astype(bf16)
        grams.append(exact_gram(value))
    total = grams[0] + grams[1]
    for ref in before:
        total = total + ref[...]
    gram[...] = total


def both(sent, received, change, before):
    rank, width = sent.shape[0] // 2, sent.shape[1]
    return call(both_kernel, [sent, received, change, *before], [struct((rank, width), bf16)] * 2 + [struct((rank, rank), f32)],
                cost(24 * rank * rank * width, 24 * rank * width))


def loading_kernel(received, own, change, *refs):
    before, loading, gram = refs[:-2], refs[-2], refs[-1]
    first = first_half()
    one, two = own[...], received[...].astype(f32)
    value = jnp.where(first, one, two) + exact_nn(change[...], jnp.where(first, two, one))
    loading[...] = value
    total = exact_gram(value)
    for ref in before:
        total = total + ref[...]
    gram[...] = total


def loading_and_gram(received, own, change, before):
    rank, width = own.shape
    return call(loading_kernel, [received, own, change, *before], [struct((rank, width), f32), struct((rank, rank), f32)],
                cost(12 * rank * rank * width, 12 * rank * width))


def factors(gram):
    size = gram.shape[0]
    row = lax.broadcasted_iota(jnp.int32, (size, size), 0)
    column = lax.broadcasted_iota(jnp.int32, (size, size), 1)
    both = jnp.concatenate([gram, jnp.where(row == column, 1.0, 0.0).astype(f32)], axis=1)
    panels = size // 8
    shape = (8, 2 * size)
    blocks = [both[8 * b:8 * b + 8] for b in range(panels)]
    inner = lax.broadcasted_iota(jnp.int32, shape, 0)
    done = []
    for b in range(panels):
        columns = [
            {k: jnp.broadcast_to(blocks[k][:, 8 * b + t:8 * b + t + 1], shape) for k in range(b, panels)}
            for t in range(8)
        ]
        for t in range(8):
            root = lax.rsqrt(jnp.broadcast_to(columns[t][b][t:t + 1], shape))
            scaled = {k: x * root for k, x in columns[t].items()}
            for s in range(t + 1, 8):
                along = jnp.broadcast_to(scaled[b][s:s + 1], shape)
                for k in range(b, panels):
                    columns[s][k] = columns[s][k] - scaled[k] * along
            pivot = jnp.broadcast_to(blocks[b][t:t + 1], shape) * root
            done.append(pivot[:1])
            for k in range(b, panels):
                factor = jnp.where(inner > t, scaled[k], 0.0) if k == b else scaled[k]
                blocks[k] = blocks[k] - factor * pivot
    rows = jnp.concatenate(done, axis=0)
    return jnp.where(row <= column, rows[:, :size], 0.0), rows[:, size:]


def output_kernel(scale, gram, *refs):
    parts, out = refs[:-1], refs[-1]
    inverse = factors(gram[...])[1] * scale
    start = 0
    for part in parts:
        out[:, start:start + part.shape[1]] = exact_nn(inverse, part[...])
        start += part.shape[1]


def output_call(gram, parts):
    rank, width = gram.shape[0], sum(x.shape[1] for x in parts)
    return call(functools.partial(output_kernel, math.sqrt(GENES)), [gram, *parts], [struct((rank, width), f32)],
                cost(12 * rank * rank * width, 8 * rank * width))[0]


def mate(value, cells, mask, other=None):
    masks = (mask, mask if other is None else other)
    return lax.ppermute(value, "cell", [(i, i ^ masks[i % 2]) for i in range(cells)])


def legs(value, cells):
    return [mate(value, cells, 6), mate(value, cells, 2, 4), mate(value, cells, 4, 2)]


def total_over_cells(value, cells):
    value = (value + mate(value, cells, GROUP | 1)) + (mate(value, cells, GROUP) + mate(value, cells, 1))
    across, one, two = legs(value, cells)
    return (value + across) + (one + two)


def cuts(width, *percents):
    edges = [0]
    for percent in percents:
        edges.append(edges[-1] + -(-percent * width // 12800) * 128)
    edges = [edge for edge in edges if edge < width] + [width]
    return list(zip(edges, edges[1:]))


def square_program(cells, expression, start_basis):
    width, rank = start_basis.shape
    masks = ((0, 0), (1, 1), (6, 6), (7, 7), (2, 4), (3, 5), (4, 2), (5, 3))
    packs = pack(expression, masks, width)
    slots = [mate(x, cells, *pair) if k else x for k, (x, pair) in enumerate(zip(packs, masks))]

    def image_from(work, bases, before, normalised, *rest):
        (odd,) = scores(slots, work, bases, before[1:], *rest, odds=(1,))
        (even,) = scores(slots, work, bases, before[:1], *rest, odds=(0,))
        even = even + mate(odd, cells, 1)
        image = image_of(even, legs(even, cells), rank, normalised)
        *images, factor = whiten(image, mate(image, cells, 1))
        return images, change_of(factor, mate(factor, cells, GROUP))

    basis = start_basis.T
    bases = {0: [basis], 1: [mate(basis, cells, GROUP)]}
    early = scores(slots, [(0, (0, 1))], bases)
    images, change = image_from([(0, ()), (1, (0, 1))], bases, early, False)
    everything = [(0, (0, 1)), (1, (0, 1))]
    for _ in range(1, ITERS):
        total, before = [], ()
        arrived = []
        for start, stop in cuts(width, 45, 33):
            sent = terms(slots, (start, width + start), stop - start, images, bf16)
            arrived.append((start, stop, sent, mate(sent, cells, GROUP)))
        for start, stop, sent, received in arrived:
            if before:
                received, *before = lax.optimization_barrier((received, *before))
            own, other, gram = both(sent, received, change, total)
            total, rows = [gram], {0: [own], 1: [other]}
            if stop < width:
                before = scores(slots, everything, rows, before, offset=start)
        images, change = image_from(everything, rows, before, True, gram, start)
    parts, total = [], []
    for start, stop in cuts(width, 60):
        received = mate(terms(slots, (width + start,), stop - start, images, bf16), cells, GROUP)
        rows, gram = loading_and_gram(received, terms(slots, (start,), stop - start, images, f32), change, total)
        parts.append(rows)
        total = [gram]
    return output_call(total_over_cells(gram, cells), parts).T


def plain_program(expression, start_basis):
    basis = start_basis
    for _ in range(ITERS):
        whole = lax.all_gather(basis, "cell", axis=0, tiled=True)
        partial = jnp.dot(expression, whole, preferred_element_type=f32)
        image = lax.psum(partial, "gene").astype(bf16)
        partial = lax.dot_general(expression, image, (((0,), (0,)), ((), ())), preferred_element_type=f32)
        loading = lax.psum_scatter(partial, "cell", scatter_dimension=0, tiled=True)
        gram = lax.dot_general(loading, loading, (((0,), (0,)), ((), ())), precision=HIGHEST, preferred_element_type=f32)
        lower = jnp.linalg.cholesky(lax.psum(gram, ("cell", "gene")))
        ortho = jax.scipy.linalg.solve_triangular(lower, loading.T, lower=True).T
        basis = ortho.astype(bf16)
    return ortho * math.sqrt(GENES)


def solution(mesh):
    cells, genes = mesh.shape["cell"], mesh.shape["gene"]

    def on_device(expression, start_basis):
        width, rank = start_basis.shape
        fits = genes == 1 and cells == 2 * GROUP and width % 128 == 0 and rank == 64
        if fits and expression.shape[0] % 16 == 0:
            return square_program(cells, expression, start_basis)
        return plain_program(expression, start_basis)

    return jax.shard_map(
        on_device,
        mesh=mesh,
        in_specs=(P(("groups", "cell"), "gene"), P(("groups", "gene", "cell"), None)),
        out_specs=P(("groups", "gene", "cell"), None),
        check_vma=False,
    )
```

```python
import functools
import math

import jax
import jax.numpy as jnp
from jax import lax
from jax.experimental import pallas as pl
from jax.experimental.pallas import tpu as pltpu
from jax.sharding import PartitionSpec as P

GENES = 30720
ITERS = 2
GROUP = 8
BIG = pltpu.CompilerParams(vmem_limit_bytes=16 * 2**20)
VMEM = pl.BlockSpec(memory_space=pltpu.VMEM)
HIGHEST = lax.Precision.HIGHEST
f32, bf16 = jnp.float32, jnp.bfloat16


def nn(a, b, precision=None):
    return lax.dot_general(a, b, (((1,), (0,)), ((), ())), precision=precision, preferred_element_type=f32)


def nt(a, b, precision=None):
    return lax.dot_general(a, b, (((1,), (1,)), ((), ())), precision=precision, preferred_element_type=f32)


def three(x):
    high = x.astype(bf16)
    rest = x - high.astype(f32)
    middle = rest.astype(bf16)
    return high, middle, (rest - middle.astype(f32)).astype(bf16)


def exact_nn(a, b):
    a1, a2, a3 = three(a)
    b1, b2, b3 = three(b)
    return nn(jnp.concatenate([a3, a2, a1, a2, a1, a1], axis=1), jnp.concatenate([b1, b2, b3, b1, b2, b1], axis=0))


def exact_nt(a, b):
    a1, a2, a3 = three(a)
    b1, b2, b3 = three(b)
    return nt(jnp.concatenate([a3, a2, a1, a2, a1, a1], axis=1), jnp.concatenate([b1, b2, b3, b1, b2, b1], axis=1))


def exact_by_bf16(a, b):
    return nn(jnp.concatenate(three(a), axis=1), jnp.concatenate([b] * 3, axis=0))


def first_half():
    return lax.axis_index("cell") & GROUP == 0


def exact_gram(a):
    size = a.shape[0]
    parts = jnp.concatenate(three(a), axis=0)
    every = nt(parts, parts)

    def part(i, j):
        return every[i * size:(i + 1) * size, j * size:(j + 1) * size]

    small = (part(0, 2) + part(2, 0)) + part(1, 1)
    return part(0, 0) + ((part(0, 1) + part(1, 0)) + small)


def struct(shape, dtype):
    return jax.ShapeDtypeStruct(shape, dtype)


def cost(flops, bytes_accessed):
    return pl.CostEstimate(flops=flops, bytes_accessed=bytes_accessed, transcendentals=0)


def pack_kernel(masks, matrix, *refs):
    outs, held, sem = refs[:-2], refs[-2], refs[-1]
    rows, width = matrix.shape[0], outs[0].shape[1] // 2
    step = 16 if rows % 16 == 0 else rows
    index = lax.axis_index("cell")
    copies = [pltpu.make_async_copy(matrix.at[pl.ds(low, step)], held.at[pl.ds(low, step)], sem.at[i])
              for i, low in enumerate(range(0, rows, step))]
    for copy in copies:
        copy.start()
    for i, copy in enumerate(copies):
        copy.wait()
        some = pl.ds(i * step, step)
        for out, pair in zip(outs, masks):
            member = index ^ jnp.where(index % 2 == 0, *pair)
            for j, block in enumerate((member, member ^ GROUP)):
                start = pl.multiple_of(block * width, 128)
                out[some, pl.ds(j * width, width)] = held[some, pl.ds(start, width)]


def pack(matrix, masks, width):
    rows, count = matrix.shape[0], len(masks)
    return pl.pallas_call(
        functools.partial(pack_kernel, masks),
        in_specs=[pl.BlockSpec(memory_space=pltpu.HBM)],
        out_specs=[VMEM] * count,
        out_shape=[struct((rows, 2 * width), matrix.dtype)] * count,
        scratch_shapes=[pltpu.VMEM(matrix.shape, matrix.dtype), pltpu.SemaphoreType.DMA((rows // 16 if rows % 16 == 0 else 1,))],
        compiler_params=pltpu.CompilerParams(vmem_limit_bytes=48 * 2**20),
        cost_estimate=cost(0, 8 * rows * count * width),
    )(matrix)


def call(kernel, args, outs, estimate):
    return pl.pallas_call(
        kernel, in_specs=[VMEM] * len(args), out_specs=[VMEM] * len(outs), out_shape=outs,
        compiler_params=BIG, cost_estimate=estimate,
    )(*args)


def scores_kernel(work, odds, counts, picked, with_gram, width, offset, *refs):
    refs = list(refs)
    bases = {block: [refs.pop(0) for _ in range(count)] for block, count in counts}
    slots = {k: refs.pop(0) for k in picked}
    gram = refs.pop(0)[...] if with_gram else None
    before, outs = refs[:-len(odds)], refs[-len(odds):]
    for i, odd in enumerate(odds):
        left, values = 0, []
        for pair, blocks in work:
            value = 0.0
            for block in blocks:
                start = block * width + offset
                for part in bases[block]:
                    stop = start + part.shape[1]
                    big = [slots[4 * pair + odd][:, start:stop], slots[4 * pair + 2 + odd][:, start:stop]]
                    value = value + nt(jnp.concatenate(big, axis=0), part[...])
                    start = stop
            lanes = slice(left, left + 2 * next(iter(slots.values())).shape[0])
            left = lanes.stop
            if blocks:
                value = value.T
            if before and lanes.stop <= before[i].shape[1]:
                value = value + before[i][:, lanes]
            values.append(value)
        if with_gram:
            rank = gram.shape[0]
            rows = rank * rank // left
            for j in range(rank // rows):
                outs[i][rank:, j * rank:(j + 1) * rank] = gram[j * rows:(j + 1) * rows]
            outs[i][:rank] = jnp.concatenate(values, axis=1)
        else:
            outs[i][...] = jnp.concatenate(values, axis=1) if len(values) > 1 else values[0]


def scores(slots, work, bases, before=(), gram=None, offset=0, odds=(0, 1)):
    rank = next(iter(bases.values()))[0].shape[0]
    picked = [4 * pair + 2 * k + odd for pair, blocks in work if blocks for k in range(2) for odd in odds]
    rows, width = slots[picked[0]].shape[0], slots[picked[0]].shape[1] // 2
    cells = 2 * rows * len(work)
    height = rank + (0 if gram is None else rank * rank // cells)
    counts = [(block, len(parts)) for block, parts in bases.items()]
    args = [x for parts in bases.values() for x in parts] + [slots[k] for k in picked]
    args += ([] if gram is None else [gram]) + list(before)
    size = 2 * len(odds) * rows * width * sum(len(blocks) for _, blocks in work)
    kernel = functools.partial(scores_kernel, work, odds, counts, picked, gram is not None, width, offset)
    return call(kernel, args, [struct((height, cells), f32)] * len(odds), cost(2 * rank * size, 2 * size))


def image_kernel(normalised, *refs):
    values, out = [ref[...] for ref in refs[:-1]], refs[-1]
    cells = out.shape[1]
    size = cells // (GROUP // 2)

    def turned(x, mask):
        return jnp.concatenate([x[:, (j ^ mask) * size:((j ^ mask) + 1) * size] for j in range(GROUP // 2)], axis=1)

    rank = out.shape[0]
    top = [x[:rank] for x in values]
    value = (top[0] + turned(top[1], 1)) + (turned(top[2], 2) + turned(top[3], 3))
    if normalised:
        below = [x[rank:] for x in values]
        below = (below[0] + below[1]) + (below[2] + below[3])
        gram = jnp.concatenate([below[:, j * rank:(j + 1) * rank] for j in range(cells // rank)], axis=0)
        value = exact_nn(factors(gram)[1], value)
    out[...] = value.astype(bf16)


def image_of(value, mates, rank, normalised):
    cells = value.shape[1]
    return call(functools.partial(image_kernel, normalised), [value, *mates], [struct((rank, cells), bf16)],
                cost(12 * value.size * rank, 16 * value.size))[0]


def whiten_kernel(even, odd, even_out, odd_out, factor):
    rank = even.shape[0]
    size = even.shape[1] // (GROUP // 2)
    chips = []
    for j in range(GROUP // 2):
        one, two = (ref[:, j * size:(j + 1) * size] for ref in (even, odd))
        chips.append(nt(one, one) + nt(two, two))
    gram = (chips[0] + chips[1]) + (chips[2] + chips[3])
    diagonal = lax.broadcasted_iota(jnp.int32, gram.shape, 0) == lax.broadcasted_iota(jnp.int32, gram.shape, 1)
    shift = jnp.sum(jnp.where(diagonal, gram, 0.0), keepdims=True) * (1e-5 / rank) + 1e-12
    upper, inverse = factors(gram + jnp.where(diagonal, shift, 0.0))
    for source, out in ((even, even_out), (odd, odd_out)):
        value = exact_by_bf16(inverse, source[...])
        high = value.astype(bf16)
        out[:rank] = high
        out[rank:] = (value - high.astype(f32)).astype(bf16)
    factor[...] = jnp.where(first_half(), inverse, upper)


def whiten(even, odd):
    rank = even.shape[0]
    return call(whiten_kernel, [even, odd], [struct((2 * rank, even.shape[1]), bf16)] * 2 + [struct((rank, rank), f32)],
                cost(12 * even.size * rank, 8 * even.size))


def change_kernel(mine, message, out):
    rank = out.shape[0]
    rows, lanes = message.shape[0], message.shape[1]
    if rows == rank:
        places = [(0, lanes - 3 * rank), (0, lanes - 2 * rank), (0, lanes - rank)]
    else:
        places = [(0, lanes - 2 * rank), (0, lanes - rank), (rank, lanes - 2 * rank)]
    high, middle, low = (message[top:top + rank, left:left + rank].astype(f32) for top, left in places)
    theirs = (high + middle) + low
    first = first_half()
    inverse = jnp.where(first, mine[...], theirs)
    upper = jnp.where(first, theirs, mine[...])
    out[...] = exact_nt(inverse, upper)


def change_of(mine, message):
    return call(change_kernel, [mine, message], [struct(mine.shape, f32)], cost(12 * mine.size, 12 * mine.size))[0]


def terms_kernel(starts, width, with_factor, *refs):
    slots, images, out = refs[:GROUP], refs[GROUP:GROUP + 2], refs[-1]
    rank = out.shape[0] // len(starts)
    step = width // 2 if width % 256 == 0 else width
    for part, start in enumerate(starts):
        for left in range(0, width, step):
            total = 0.0
            for odd in range(2):
                big = jnp.concatenate([ref[:, start + left:start + left + step] for ref in slots[odd::2]], axis=0)
                total = total + nn(images[odd][...], big)
            out[part * rank:(part + 1) * rank, left:left + step] = (total[:rank] + total[rank:]).astype(out.dtype)
    if with_factor:
        tail = list(three(refs[GROUP + 2][...]))
        if len(starts) == 2:
            tail.append(jnp.zeros_like(tail[0]))
        across = len(tail) // len(starts)
        for part in range(len(starts)):
            out[part * rank:(part + 1) * rank, width:] = jnp.concatenate(tail[part * across:(part + 1) * across], axis=1)


def terms(slots, starts, width, images, dtype, factor=None):
    rank, cells = images[0].shape[0] // 2, slots[0].shape[0] * GROUP
    size = cells * width * len(starts)
    tail = 0 if factor is None else (3 if len(starts) == 1 else 2) * rank
    args = [*slots, *images] + ([] if factor is None else [factor])
    return call(functools.partial(terms_kernel, starts, width, factor is not None), args,
                [struct((rank * len(starts), width + tail), dtype)], cost(4 * rank * size, 2 * size))[0]


def both_kernel(sent, received, change, *refs):
    before, rows, gram = refs[:-3], refs[-3:-1], refs[-1]
    rank, width = rows[0].shape
    first = first_half()
    grams = []
    for block in range(2):
        mine, theirs = slice(block * rank, (block + 1) * rank), slice((1 - block) * rank, (2 - block) * rank)
        one, two = sent[mine, :width].astype(f32), received[theirs, :width].astype(f32)
        value = jnp.where(first, one, two) + exact_by_bf16(change[...], jnp.where(first, two, one).astype(bf16))
        rows[block][...] = value.astype(bf16)
        grams.append(exact_gram(value))
    total = grams[0] + grams[1]
    for ref in before:
        total = total + ref[...]
    gram[...] = total


def both(sent, received, width, change, before):
    rank = sent.shape[0] // 2
    return call(both_kernel, [sent, received, change, *before], [struct((rank, width), bf16)] * 2 + [struct((rank, rank), f32)],
                cost(24 * rank * rank * width, 24 * rank * width))


def loading_kernel(received, own, change, *refs):
    before, loading, gram = refs[:-2], refs[-2], refs[-1]
    first = first_half()
    one, two = own[...], received[:, :own.shape[1]].astype(f32)
    value = jnp.where(first, one, two) + exact_nn(change[...], jnp.where(first, two, one))
    loading[...] = value
    total = exact_gram(value)
    for ref in before:
        total = total + ref[...]
    gram[...] = total


def loading_and_gram(received, own, change, before):
    rank, width = own.shape
    return call(loading_kernel, [received, own, change, *before], [struct((rank, width), f32), struct((rank, rank), f32)],
                cost(12 * rank * rank * width, 12 * rank * width))


def factors(gram):
    size = gram.shape[0]
    row = lax.broadcasted_iota(jnp.int32, (size, size), 0)
    column = lax.broadcasted_iota(jnp.int32, (size, size), 1)
    both = jnp.concatenate([gram, jnp.where(row == column, 1.0, 0.0).astype(f32)], axis=1)
    panels = size // 8
    shape = (8, 2 * size)
    blocks = [both[8 * b:8 * b + 8] for b in range(panels)]
    inner = lax.broadcasted_iota(jnp.int32, shape, 0)
    done = []
    for b in range(panels):
        columns = [
            {k: jnp.broadcast_to(blocks[k][:, 8 * b + t:8 * b + t + 1], shape) for k in range(b, panels)}
            for t in range(8)
        ]
        for t in range(8):
            root = lax.rsqrt(jnp.broadcast_to(columns[t][b][t:t + 1], shape))
            scaled = {k: x * root for k, x in columns[t].items()}
            for s in range(t + 1, 8):
                along = jnp.broadcast_to(scaled[b][s:s + 1], shape)
                for k in range(b, panels):
                    columns[s][k] = columns[s][k] - scaled[k] * along
            pivot = jnp.broadcast_to(blocks[b][t:t + 1], shape) * root
            done.append(pivot[:1])
            for k in range(b, panels):
                factor = jnp.where(inner > t, scaled[k], 0.0) if k == b else scaled[k]
                blocks[k] = blocks[k] - factor * pivot
    rows = jnp.concatenate(done, axis=0)
    return jnp.where(row <= column, rows[:, :size], 0.0), rows[:, size:]


def output_kernel(scale, gram, *refs):
    parts, out = refs[:-1], refs[-1]
    inverse = factors(gram[...])[1] * scale
    start = 0
    for part in parts:
        out[:, start:start + part.shape[1]] = exact_nn(inverse, part[...])
        start += part.shape[1]


def output_call(gram, parts):
    rank, width = gram.shape[0], sum(x.shape[1] for x in parts)
    return call(functools.partial(output_kernel, math.sqrt(GENES)), [gram, *parts], [struct((rank, width), f32)],
                cost(12 * rank * rank * width, 8 * rank * width))[0]


def mate(value, cells, mask, other=None):
    masks = (mask, mask if other is None else other)
    return lax.ppermute(value, "cell", [(i, i ^ masks[i % 2]) for i in range(cells)])


def legs(value, cells):
    return [mate(value, cells, 6), mate(value, cells, 2, 4), mate(value, cells, 4, 2)]


def total_over_cells(value, cells):
    value = (value + mate(value, cells, GROUP | 1)) + (mate(value, cells, GROUP) + mate(value, cells, 1))
    across, one, two = legs(value, cells)
    return (value + across) + (one + two)


def cuts(width, *percents):
    edges = [0]
    for percent in percents:
        edges.append(edges[-1] + -(-percent * width // 12800) * 128)
    edges = [edge for edge in edges if edge < width] + [width]
    return list(zip(edges, edges[1:]))


def square_program(cells, expression, start_basis):
    width, rank = start_basis.shape
    masks = ((0, 0), (1, 1), (6, 6), (7, 7), (2, 4), (3, 5), (4, 2), (5, 3))
    packs = pack(expression, masks, width)
    slots = [mate(x, cells, *pair) if k else x for k, (x, pair) in enumerate(zip(packs, masks))]

    def image_from(work, bases, before, normalised, *rest):
        (odd,) = scores(slots, work, bases, before[1:], *rest, odds=(1,))
        (even,) = scores(slots, work, bases, before[:1], *rest, odds=(0,))
        even = even + mate(odd, cells, 1)
        image = image_of(even, legs(even, cells), rank, normalised)
        return whiten(image, mate(image, cells, 1))

    basis = start_basis.T
    bases = {0: [basis], 1: [mate(basis, cells, GROUP)]}
    early = scores(slots, [(0, (0, 1))], bases)
    *images, factor = image_from([(0, ()), (1, (0, 1))], bases, early, False)
    everything = [(0, (0, 1)), (1, (0, 1))]
    for _ in range(1, ITERS):
        total, before = [], ()
        arrived = []
        for start, stop in cuts(width, 45, 33):
            sent = terms(slots, (start, width + start), stop - start, images, bf16, None if start else factor)
            arrived.append((start, stop, sent, mate(sent, cells, GROUP)))
        for start, stop, sent, received in arrived:
            if not start:
                change = change_of(factor, received)
            if before:
                received, *before = lax.optimization_barrier((received, *before))
            own, other, gram = both(sent, received, stop - start, change, total)
            total, rows = [gram], {0: [own], 1: [other]}
            if stop < width:
                before = scores(slots, everything, rows, before, offset=start)
        *images, factor = image_from(everything, rows, before, True, gram, start)
    parts, total = [], []
    for start, stop in cuts(width, 60):
        sent = terms(slots, (width + start,), stop - start, images, bf16, None if start else factor)
        received = mate(sent, cells, GROUP)
        if not start:
            change = change_of(factor, received)
        rows, gram = loading_and_gram(received, terms(slots, (start,), stop - start, images, f32), change, total)
        parts.append(rows)
        total = [gram]
    return output_call(total_over_cells(gram, cells), parts).T


def plain_program(expression, start_basis):
    basis = start_basis
    for _ in range(ITERS):
        whole = lax.all_gather(basis, "cell", axis=0, tiled=True)
        partial = jnp.dot(expression, whole, preferred_element_type=f32)
        image = lax.psum(partial, "gene").astype(bf16)
        partial = lax.dot_general(expression, image, (((0,), (0,)), ((), ())), preferred_element_type=f32)
        loading = lax.psum_scatter(partial, "cell", scatter_dimension=0, tiled=True)
        gram = lax.dot_general(loading, loading, (((0,), (0,)), ((), ())), precision=HIGHEST, preferred_element_type=f32)
        lower = jnp.linalg.cholesky(lax.psum(gram, ("cell", "gene")))
        ortho = jax.scipy.linalg.solve_triangular(lower, loading.T, lower=True).T
        basis = ortho.astype(bf16)
    return ortho * math.sqrt(GENES)


def solution(mesh):
    cells, genes = mesh.shape["cell"], mesh.shape["gene"]

    def on_device(expression, start_basis):
        width, rank = start_basis.shape
        fits = genes == 1 and cells == 2 * GROUP and width % 128 == 0 and rank == 64
        if fits and expression.shape[0] % 16 == 0:
            return square_program(cells, expression, start_basis)
        return plain_program(expression, start_basis)

    return jax.shard_map(
        on_device,
        mesh=mesh,
        in_specs=(P(("groups", "cell"), "gene"), P(("groups", "gene", "cell"), None)),
        out_specs=P(("groups", "gene", "cell"), None),
        check_vma=False,
    )
```

```python
import functools
import math

import jax
import jax.numpy as jnp
from jax import lax
from jax.experimental import pallas as pl
from jax.experimental.pallas import tpu as pltpu
from jax.sharding import PartitionSpec as P

GENES = 30720
ITERS = 2
GROUP = 8
BIG = pltpu.CompilerParams(vmem_limit_bytes=16 * 2**20)
VMEM = pl.BlockSpec(memory_space=pltpu.VMEM)
HIGHEST = lax.Precision.HIGHEST
f32, bf16 = jnp.float32, jnp.bfloat16


def nn(a, b, precision=None):
    return lax.dot_general(a, b, (((1,), (0,)), ((), ())), precision=precision, preferred_element_type=f32)


def nt(a, b, precision=None):
    return lax.dot_general(a, b, (((1,), (1,)), ((), ())), precision=precision, preferred_element_type=f32)


def three(x):
    high = x.astype(bf16)
    rest = x - high.astype(f32)
    middle = rest.astype(bf16)
    return high, middle, (rest - middle.astype(f32)).astype(bf16)


def exact_nn(a, b):
    a1, a2, a3 = three(a)
    b1, b2, b3 = three(b)
    return nn(jnp.concatenate([a3, a2, a1, a2, a1, a1], axis=1), jnp.concatenate([b1, b2, b3, b1, b2, b1], axis=0))


def exact_nt(a, b):
    a1, a2, a3 = three(a)
    b1, b2, b3 = three(b)
    return nt(jnp.concatenate([a3, a2, a1, a2, a1, a1], axis=1), jnp.concatenate([b1, b2, b3, b1, b2, b1], axis=1))


def exact_by_bf16(a, b):
    return nn(jnp.concatenate(three(a), axis=1), jnp.concatenate([b] * 3, axis=0))


def first_half():
    return lax.axis_index("cell") & GROUP == 0


def exact_gram(a):
    size = a.shape[0]
    parts = jnp.concatenate(three(a), axis=0)
    every = nt(parts, parts)

    def part(i, j):
        return every[i * size:(i + 1) * size, j * size:(j + 1) * size]

    small = (part(0, 2) + part(2, 0)) + part(1, 1)
    return part(0, 0) + ((part(0, 1) + part(1, 0)) + small)


def struct(shape, dtype):
    return jax.ShapeDtypeStruct(shape, dtype)


def cost(flops, bytes_accessed):
    return pl.CostEstimate(flops=flops, bytes_accessed=bytes_accessed, transcendentals=0)


def pack_kernel(masks, matrix, *refs):
    outs, held, sem = refs[:-2], refs[-2], refs[-1]
    rows, width = matrix.shape[0], outs[0].shape[1] // 2
    step = 16 if rows % 16 == 0 else rows
    index = lax.axis_index("cell")
    copies = [pltpu.make_async_copy(matrix.at[pl.ds(low, step)], held.at[pl.ds(low, step)], sem.at[i])
              for i, low in enumerate(range(0, rows, step))]
    for copy in copies:
        copy.start()
    for i, copy in enumerate(copies):
        copy.wait()
        some = pl.ds(i * step, step)
        for out, pair in zip(outs, masks):
            member = index ^ jnp.where(index % 2 == 0, *pair)
            for j, block in enumerate((member, member ^ GROUP)):
                start = pl.multiple_of(block * width, 128)
                out[some, pl.ds(j * width, width)] = held[some, pl.ds(start, width)]


def pack(matrix, masks, width):
    rows, count = matrix.shape[0], len(masks)
    return pl.pallas_call(
        functools.partial(pack_kernel, masks),
        in_specs=[pl.BlockSpec(memory_space=pltpu.HBM)],
        out_specs=[VMEM] * count,
        out_shape=[struct((rows, 2 * width), matrix.dtype)] * count,
        scratch_shapes=[pltpu.VMEM(matrix.shape, matrix.dtype), pltpu.SemaphoreType.DMA((rows // 16 if rows % 16 == 0 else 1,))],
        compiler_params=pltpu.CompilerParams(vmem_limit_bytes=48 * 2**20),
        cost_estimate=cost(0, 8 * rows * count * width),
    )(matrix)


def call(kernel, args, outs, estimate):
    return pl.pallas_call(
        kernel, in_specs=[VMEM] * len(args), out_specs=[VMEM] * len(outs), out_shape=outs,
        compiler_params=BIG, cost_estimate=estimate,
    )(*args)


def scores_kernel(work, odds, counts, picked, with_gram, width, offset, *refs):
    refs = list(refs)
    bases = {block: [refs.pop(0) for _ in range(count)] for block, count in counts}
    slots = {k: refs.pop(0) for k in picked}
    gram = refs.pop(0)[...] if with_gram else None
    before, outs = refs[:-len(odds)], refs[-len(odds):]
    for i, odd in enumerate(odds):
        left, values = 0, []
        for pair, blocks in work:
            value = 0.0
            for block in blocks:
                start = block * width + offset
                for part in bases[block]:
                    stop = start + part.shape[1]
                    big = [slots[4 * pair + odd][:, start:stop], slots[4 * pair + 2 + odd][:, start:stop]]
                    value = value + nt(jnp.concatenate(big, axis=0), part[...])
                    start = stop
            lanes = slice(left, left + 2 * next(iter(slots.values())).shape[0])
            left = lanes.stop
            if blocks:
                value = value.T
            if before and lanes.stop <= before[i].shape[1]:
                value = value + before[i][:, lanes]
            values.append(value)
        if with_gram:
            rank = gram.shape[0]
            rows = rank * rank // left
            for j in range(rank // rows):
                outs[i][rank:, j * rank:(j + 1) * rank] = gram[j * rows:(j + 1) * rows]
            outs[i][:rank] = jnp.concatenate(values, axis=1)
        else:
            outs[i][...] = jnp.concatenate(values, axis=1) if len(values) > 1 else values[0]


def scores(slots, work, bases, before=(), gram=None, offset=0, odds=(0, 1)):
    rank = next(iter(bases.values()))[0].shape[0]
    picked = [4 * pair + 2 * k + odd for pair, blocks in work if blocks for k in range(2) for odd in odds]
    rows, width = slots[picked[0]].shape[0], slots[picked[0]].shape[1] // 2
    cells = 2 * rows * len(work)
    height = rank + (0 if gram is None else rank * rank // cells)
    counts = [(block, len(parts)) for block, parts in bases.items()]
    args = [x for parts in bases.values() for x in parts] + [slots[k] for k in picked]
    args += ([] if gram is None else [gram]) + list(before)
    size = 2 * len(odds) * rows * width * sum(len(blocks) for _, blocks in work)
    kernel = functools.partial(scores_kernel, work, odds, counts, picked, gram is not None, width, offset)
    return call(kernel, args, [struct((height, cells), f32)] * len(odds), cost(2 * rank * size, 2 * size))


def image_kernel(normalised, *refs):
    values, out = [ref[...] for ref in refs[:-1]], refs[-1]
    cells = out.shape[1]
    size = cells // (GROUP // 2)

    def turned(x, mask):
        return jnp.concatenate([x[:, (j ^ mask) * size:((j ^ mask) + 1) * size] for j in range(GROUP // 2)], axis=1)

    rank = out.shape[0]
    top = [x[:rank] for x in values]
    value = (top[0] + turned(top[1], 1)) + (turned(top[2], 2) + turned(top[3], 3))
    if normalised:
        below = [x[rank:] for x in values]
        below = (below[0] + below[1]) + (below[2] + below[3])
        gram = jnp.concatenate([below[:, j * rank:(j + 1) * rank] for j in range(cells // rank)], axis=0)
        value = exact_nn(factors(gram)[1], value)
    out[...] = value.astype(bf16)


def image_of(value, mates, rank, normalised):
    cells = value.shape[1]
    return call(functools.partial(image_kernel, normalised), [value, *mates], [struct((rank, cells), bf16)],
                cost(12 * value.size * rank, 16 * value.size))[0]


def whiten_kernel(even, odd, even_out, odd_out, factor):
    rank = even.shape[0]
    size = even.shape[1] // (GROUP // 2)
    chips = []
    for j in range(GROUP // 2):
        one, two = (ref[:, j * size:(j + 1) * size] for ref in (even, odd))
        chips.append(nt(one, one) + nt(two, two))
    gram = (chips[0] + chips[1]) + (chips[2] + chips[3])
    diagonal = lax.broadcasted_iota(jnp.int32, gram.shape, 0) == lax.broadcasted_iota(jnp.int32, gram.shape, 1)
    shift = jnp.sum(jnp.where(diagonal, gram, 0.0), keepdims=True) * (1e-3 / rank) + 1e-12
    upper, inverse = factors(gram + jnp.where(diagonal, shift, 0.0))
    for source, out in ((even, even_out), (odd, odd_out)):
        value = exact_by_bf16(inverse, source[...])
        high = value.astype(bf16)
        out[:rank] = high
        out[rank:] = (value - high.astype(f32)).astype(bf16)
    factor[...] = jnp.where(first_half(), inverse, upper)


def whiten(even, odd):
    rank = even.shape[0]
    return call(whiten_kernel, [even, odd], [struct((2 * rank, even.shape[1]), bf16)] * 2 + [struct((rank, rank), f32)],
                cost(12 * even.size * rank, 8 * even.size))


def change_kernel(mine, message, out):
    rank = out.shape[0]
    rows, lanes = message.shape[0], message.shape[1]
    if rows == rank:
        places = [(0, lanes - 3 * rank), (0, lanes - 2 * rank), (0, lanes - rank)]
    else:
        places = [(0, lanes - 2 * rank), (0, lanes - rank), (rank, lanes - 2 * rank)]
    high, middle, low = (message[top:top + rank, left:left + rank].astype(f32) for top, left in places)
    theirs = (high + middle) + low
    first = first_half()
    inverse = jnp.where(first, mine[...], theirs)
    upper = jnp.where(first, theirs, mine[...])
    out[...] = exact_nt(inverse, upper)


def change_of(mine, message):
    return call(change_kernel, [mine, message], [struct(mine.shape, f32)], cost(12 * mine.size, 12 * mine.size))[0]


def terms_kernel(starts, width, with_factor, *refs):
    slots, images, out = refs[:GROUP], refs[GROUP:GROUP + 2], refs[-1]
    rank = out.shape[0] // len(starts)
    step = width // 2 if width % 256 == 0 else width
    for part, start in enumerate(starts):
        for left in range(0, width, step):
            total = 0.0
            for odd in range(2):
                big = jnp.concatenate([ref[:, start + left:start + left + step] for ref in slots[odd::2]], axis=0)
                total = total + nn(images[odd][...], big)
            out[part * rank:(part + 1) * rank, left:left + step] = (total[:rank] + total[rank:]).astype(out.dtype)
    if with_factor:
        tail = list(three(refs[GROUP + 2][...]))
        if len(starts) == 2:
            tail.append(jnp.zeros_like(tail[0]))
        across = len(tail) // len(starts)
        for part in range(len(starts)):
            out[part * rank:(part + 1) * rank, width:] = jnp.concatenate(tail[part * across:(part + 1) * across], axis=1)


def terms(slots, starts, width, images, dtype, factor=None):
    rank, cells = images[0].shape[0] // 2, slots[0].shape[0] * GROUP
    size = cells * width * len(starts)
    tail = 0 if factor is None else (3 if len(starts) == 1 else 2) * rank
    args = [*slots, *images] + ([] if factor is None else [factor])
    return call(functools.partial(terms_kernel, starts, width, factor is not None), args,
                [struct((rank * len(starts), width + tail), dtype)], cost(4 * rank * size, 2 * size))[0]


def both_kernel(sent, received, change, *refs):
    before, rows, gram = refs[:-3], refs[-3:-1], refs[-1]
    rank, width = rows[0].shape
    first = first_half()
    grams = []
    for block in range(2):
        mine, theirs = slice(block * rank, (block + 1) * rank), slice((1 - block) * rank, (2 - block) * rank)
        one, two = sent[mine, :width].astype(f32), received[theirs, :width].astype(f32)
        value = jnp.where(first, one, two) + exact_by_bf16(change[...], jnp.where(first, two, one).astype(bf16))
        rows[block][...] = value.astype(bf16)
        grams.append(exact_gram(value))
    total = grams[0] + grams[1]
    for ref in before:
        total = total + ref[...]
    gram[...] = total


def both(sent, received, width, change, before):
    rank = sent.shape[0] // 2
    return call(both_kernel, [sent, received, change, *before], [struct((rank, width), bf16)] * 2 + [struct((rank, rank), f32)],
                cost(24 * rank * rank * width, 24 * rank * width))


def loading_kernel(received, own, change, *refs):
    before, loading, gram = refs[:-2], refs[-2], refs[-1]
    first = first_half()
    one, two = own[...], received[:, :own.shape[1]].astype(f32)
    value = jnp.where(first, one, two) + exact_nn(change[...], jnp.where(first, two, one))
    loading[...] = value
    total = exact_gram(value)
    for ref in before:
        total = total + ref[...]
    gram[...] = total


def loading_and_gram(received, own, change, before):
    rank, width = own.shape
    return call(loading_kernel, [received, own, change, *before], [struct((rank, width), f32), struct((rank, rank), f32)],
                cost(12 * rank * rank * width, 12 * rank * width))


def factors(gram):
    size = gram.shape[0]
    row = lax.broadcasted_iota(jnp.int32, (size, size), 0)
    column = lax.broadcasted_iota(jnp.int32, (size, size), 1)
    both = jnp.concatenate([gram, jnp.where(row == column, 1.0, 0.0).astype(f32)], axis=1)
    panels = size // 8
    shape = (8, 2 * size)
    blocks = [both[8 * b:8 * b + 8] for b in range(panels)]
    inner = lax.broadcasted_iota(jnp.int32, shape, 0)
    done = []
    for b in range(panels):
        columns = [
            {k: jnp.broadcast_to(blocks[k][:, 8 * b + t:8 * b + t + 1], shape) for k in range(b, panels)}
            for t in range(8)
        ]
        for t in range(8):
            root = lax.rsqrt(jnp.broadcast_to(columns[t][b][t:t + 1], shape))
            scaled = {k: x * root for k, x in columns[t].items()}
            for s in range(t + 1, 8):
                along = jnp.broadcast_to(scaled[b][s:s + 1], shape)
                for k in range(b, panels):
                    columns[s][k] = columns[s][k] - scaled[k] * along
            pivot = jnp.broadcast_to(blocks[b][t:t + 1], shape) * root
            done.append(pivot[:1])
            for k in range(b, panels):
                factor = jnp.where(inner > t, scaled[k], 0.0) if k == b else scaled[k]
                blocks[k] = blocks[k] - factor * pivot
    rows = jnp.concatenate(done, axis=0)
    return jnp.where(row <= column, rows[:, :size], 0.0), rows[:, size:]


def output_kernel(scale, gram, *refs):
    parts, out = refs[:-1], refs[-1]
    inverse = factors(gram[...])[1] * scale
    start = 0
    for part in parts:
        out[:, start:start + part.shape[1]] = exact_nn(inverse, part[...])
        start += part.shape[1]


def output_call(gram, parts):
    rank, width = gram.shape[0], sum(x.shape[1] for x in parts)
    return call(functools.partial(output_kernel, math.sqrt(GENES)), [gram, *parts], [struct((rank, width), f32)],
                cost(12 * rank * rank * width, 8 * rank * width))[0]


def mate(value, cells, mask, other=None):
    masks = (mask, mask if other is None else other)
    return lax.ppermute(value, "cell", [(i, i ^ masks[i % 2]) for i in range(cells)])


def legs(value, cells):
    return [mate(value, cells, 6), mate(value, cells, 2, 4), mate(value, cells, 4, 2)]


def total_over_cells(value, cells):
    value = (value + mate(value, cells, GROUP | 1)) + (mate(value, cells, GROUP) + mate(value, cells, 1))
    across, one, two = legs(value, cells)
    return (value + across) + (one + two)


def cuts(width, *percents):
    edges = [0]
    for percent in percents:
        edges.append(edges[-1] + -(-percent * width // 12800) * 128)
    edges = [edge for edge in edges if edge < width] + [width]
    return list(zip(edges, edges[1:]))


def square_program(cells, expression, start_basis):
    width, rank = start_basis.shape
    masks = ((0, 0), (1, 1), (6, 6), (7, 7), (2, 4), (3, 5), (4, 2), (5, 3))
    packs = pack(expression, masks, width)
    slots = [mate(x, cells, *pair) if k else x for k, (x, pair) in enumerate(zip(packs, masks))]

    def image_from(work, bases, before, normalised, *rest):
        (odd,) = scores(slots, work, bases, before[1:], *rest, odds=(1,))
        (even,) = scores(slots, work, bases, before[:1], *rest, odds=(0,))
        even = even + mate(odd, cells, 1)
        image = image_of(even, legs(even, cells), rank, normalised)
        return whiten(image, mate(image, cells, 1))

    basis = start_basis.T
    bases = {0: [basis], 1: [mate(basis, cells, GROUP)]}
    early = scores(slots, [(0, (0, 1))], bases)
    *images, factor = image_from([(0, ()), (1, (0, 1))], bases, early, False)
    everything = [(0, (0, 1)), (1, (0, 1))]
    for _ in range(1, ITERS):
        total, before = [], ()
        arrived = []
        for start, stop in cuts(width, 45, 33):
            sent = terms(slots, (start, width + start), stop - start, images, bf16, None if start else factor)
            arrived.append((start, stop, sent, mate(sent, cells, GROUP)))
        for start, stop, sent, received in arrived:
            if not start:
                change = change_of(factor, received)
            if before:
                received, *before = lax.optimization_barrier((received, *before))
            own, other, gram = both(sent, received, stop - start, change, total)
            total, rows = [gram], {0: [own], 1: [other]}
            if stop < width:
                before = scores(slots, everything, rows, before, offset=start)
        *images, factor = image_from(everything, rows, before, True, gram, start)
    parts, total = [], []
    for start, stop in cuts(width, 60):
        sent = terms(slots, (width + start,), stop - start, images, bf16, None if start else factor)
        received = mate(sent, cells, GROUP)
        if not start:
            change = change_of(factor, received)
        rows, gram = loading_and_gram(received, terms(slots, (start,), stop - start, images, f32), change, total)
        parts.append(rows)
        total = [gram]
    return output_call(total_over_cells(gram, cells), parts).T


def plain_program(expression, start_basis):
    basis = start_basis
    for _ in range(ITERS):
        whole = lax.all_gather(basis, "cell", axis=0, tiled=True)
        partial = jnp.dot(expression, whole, preferred_element_type=f32)
        image = lax.psum(partial, "gene").astype(bf16)
        partial = lax.dot_general(expression, image, (((0,), (0,)), ((), ())), preferred_element_type=f32)
        loading = lax.psum_scatter(partial, "cell", scatter_dimension=0, tiled=True)
        gram = lax.dot_general(loading, loading, (((0,), (0,)), ((), ())), precision=HIGHEST, preferred_element_type=f32)
        lower = jnp.linalg.cholesky(lax.psum(gram, ("cell", "gene")))
        ortho = jax.scipy.linalg.solve_triangular(lower, loading.T, lower=True).T
        basis = ortho.astype(bf16)
    return ortho * math.sqrt(GENES)


def solution(mesh):
    cells, genes = mesh.shape["cell"], mesh.shape["gene"]

    def on_device(expression, start_basis):
        width, rank = start_basis.shape
        fits = genes == 1 and cells == 2 * GROUP and width % 128 == 0 and rank == 64
        if fits and expression.shape[0] % 16 == 0:
            return square_program(cells, expression, start_basis)
        return plain_program(expression, start_basis)

    return jax.shard_map(
        on_device,
        mesh=mesh,
        in_specs=(P(("groups", "cell"), "gene"), P(("groups", "gene", "cell"), None)),
        out_specs=P(("groups", "gene", "cell"), None),
        check_vma=False,
    )
```
